32 devices in a mesh: seq: 32 (over z, y, x, core), tensor: 1.
Axes of the slice: x: 2, y: 2, z: 4, core: 2. Of those that a mesh axis runs over, the one named last changes fastest.
Arguments:
- query_rows: bfloat16 [4096, 4096], P('seq', 'tensor'), may hold values from -6 to 6
- key_rows: bfloat16 [4096, 4096], P('seq', 'tensor'), may hold values from -6 to 6
- value_rows: bfloat16 [4096, 4096], P('seq', 'tensor'), may hold values from -18 to 18
- cluster_id: int32 [32, 4096], P('tensor', 'seq'), may hold values from 0 to 255, as said below
- slot_index: int32 [32, 4096], P('tensor', 'seq'), may hold values from 0 to 31, as said below
- out_weight: bfloat16 [4096, 2048], P('tensor', 'seq'), may hold values from -0.09375 to 0.09375
- grad_out: bfloat16 [4096, 2048], P(('seq', 'tensor')), may hold values from -6 to 6
Outputs:
- mixed: bfloat16 [4096, 2048], P(('seq', 'tensor'))
- grad_query: bfloat16 [4096, 4096], P('seq', 'tensor')
- grad_key: bfloat16 [4096, 4096], P('seq', 'tensor')
- grad_value: bfloat16 [4096, 4096], P('seq', 'tensor')
The draws below stay inside these ranges and needn't reach their ends.
Inputs may be any that keep to these rules, and one draw needn't show every extreme that they name: `cluster_id`: cluster c of a head belongs to the index c // 8 of seq. Each cluster of a head holds at most 32 tokens and in every head some cluster holds exactly 32. The tokens of one index of seq go, for one head, to at most 8 slots among the clusters of one owner, and every index of seq reaches 8 for some owner in every head. `slot_index`: within one head and cluster the slots of its tokens are distinct.
All inputs are finite; a program needn't handle non-finite values.
Results may differ from the reference program's by a relative error of at most 0.025.
Values may be sent and summed in bfloat16 or wider, within the bound.
No kernel may reach another device: no remote copies, remote signals or barrier semaphores. Data moves between devices by JAX's collectives and lax.ppermute only.
A program may use at most 128 MiB of HBM per device.

```python
import math
import jax
import jax.numpy as jnp
from jax import lax

H = 32
DH = 128
D_OUT = 2048
CLU_DEV = 8
TOK_DEV = 128
CAP = 32
CLUSTERS = 256
TOKENS = 4096
N_SEQ = 32


def route_table(key):
    owners = N_SEQ
    pair_total = 2 * (TOK_DEV // N_SEQ)
    room = CLU_DEV * CAP

    def one_sender(sender_key):
        first_key, second_key, third_key = jax.random.split(sender_key, 3)
        order = jax.random.permutation(first_key, owners)
        shares = jax.random.randint(second_key, (owners // 2,), 0, pair_total + 1)
        shares = shares.at[0].set(pair_total)
        counts = jnp.zeros((owners,), jnp.int32).at[order[0::2]].set(shares).at[order[1::2]].set(pair_total - shares)
        bounds = jnp.cumsum(counts)
        sorted_owner = jnp.searchsorted(bounds, jnp.arange(TOK_DEV, dtype=jnp.int32), side='right').astype(jnp.int32)
        shuffle = jax.random.permutation(third_key, TOK_DEV)
        owner = jnp.zeros((TOK_DEV,), jnp.int32).at[shuffle].set(sorted_owner)
        return (owner, counts)

    def one_head(head_key):
        sender_keys = jax.random.split(jax.random.fold_in(head_key, 0), owners)
        owner, counts = jax.vmap(one_sender)(sender_keys)
        onehot = (owner[:, :, None] == jnp.arange(owners, dtype=jnp.int32)[None, None, :]).astype(jnp.int32)
        rank = jnp.sum((jnp.cumsum(onehot, axis=1) - onehot) * onehot, axis=2)
        offsets = jnp.cumsum(counts, axis=0) - counts
        arrival = rank + jnp.take_along_axis(offsets, owner, axis=1)
        favored = jax.random.randint(jax.random.fold_in(head_key, 1), (owners,), 0, CLU_DEV)
        ranks = jax.vmap(lambda owner_key: jax.random.permutation(owner_key, room))(jax.random.split(jax.random.fold_in(head_key, 2), owners))
        cell_of = jnp.arange(room, dtype=jnp.int32) // CAP
        ranks = ranks + jnp.where(cell_of[None, :] == favored[:, None], 0, room)
        layout = jnp.argsort(ranks, axis=1, stable=True).astype(jnp.int32)
        position = layout[owner, arrival]
        cluster = owner * CLU_DEV + position // CAP
        return (cluster.reshape(-1).astype(jnp.int32), (position % CAP).reshape(-1).astype(jnp.int32))
    return lax.map(one_head, jax.random.split(key, H))


def draw_cluster_id(key, part):
    return route_table(jax.random.fold_in(key, 7))[0]


def draw_slot_index(key, part):
    return route_table(jax.random.fold_in(key, 7))[1]


def attention_rows(key, for_keys):
    base = jnp.clip(jax.random.normal(jax.random.fold_in(key, 11 + for_keys), (TOKENS, H * DH), jnp.float32), -6.0, 6.0)
    return base


def draw_query_rows(key, part):
    return attention_rows(key, 0).astype(jnp.bfloat16)


def draw_key_rows(key, part):
    return attention_rows(key, 1).astype(jnp.bfloat16)


def shard_levels(key, dims, cuts, least, high):
    loudness, own = 1.0, jax.random.fold_in(key, 6)
    for dim, shards_of in cuts:
        steps = jnp.exp(jax.random.uniform(jax.random.fold_in(own, dim), (shards_of,), jnp.float32, least / len(cuts), high / len(cuts)))
        loudness = loudness * jnp.repeat(steps, dims[dim] // shards_of).reshape([-1 if axis == dim else 1 for axis in range(len(dims))])
    return loudness


def normal_values(key, shape, spread, most, cuts=(), kind=jnp.bfloat16):
    values = jax.random.normal(key, shape, jnp.float32) * spread
    if len(cuts) > 0:
        values = shard_levels(key, shape, cuts, -0.22, 0.18) * values
    return jnp.clip(values, min=-most, max=most).astype(kind)


def setup_inputs(seed: int = 0) -> dict:
    arg_keys = jax.random.split(jax.random.key(seed), 8)
    query_rows = draw_query_rows(jax.random.fold_in(arg_keys[7], 71), 0)
    key_rows = draw_key_rows(jax.random.fold_in(arg_keys[7], 71), 0)
    value_rows = normal_values(arg_keys[2], (TOKENS, H * DH), 3.0, 18.0, ((0, 32),))
    cluster_id = draw_cluster_id(jax.random.fold_in(arg_keys[7], 71), 0)
    slot_index = draw_slot_index(jax.random.fold_in(arg_keys[7], 71), 0)
    out_weight = normal_values(arg_keys[5], (H * DH, D_OUT), (H * DH) ** -0.5, 0.09375, ((1, 32),))
    grad_out = normal_values(arg_keys[6], (TOKENS, D_OUT), 1.0, 6.0, ((0, 32),))
    return dict(query_rows=query_rows, key_rows=key_rows, value_rows=value_rows, cluster_id=cluster_id, slot_index=slot_index, out_weight=out_weight, grad_out=grad_out)


def reference(query_rows, key_rows, value_rows, cluster_id, slot_index, out_weight, grad_out):
    score_scale = 1.0 / math.sqrt(DH)
    masked_score = -1e+30
    room = CLUSTERS * CAP
    grad_attended = jnp.dot(grad_out, out_weight.T, preferred_element_type=jnp.float32).astype(jnp.bfloat16)

    def one_head(head):
        start = head * DH
        query_head = lax.dynamic_slice_in_dim(query_rows, start, DH, 1)
        key_head = lax.dynamic_slice_in_dim(key_rows, start, DH, 1)
        value_head = lax.dynamic_slice_in_dim(value_rows, start, DH, 1)
        grad_head = lax.dynamic_slice_in_dim(grad_attended, start, DH, 1)
        position = (cluster_id[head] * CAP + slot_index[head]).astype(jnp.int32)

        def to_cells(rows):
            return jnp.zeros((room, DH), rows.dtype).at[position].set(rows).reshape(CLUSTERS, CAP, DH)
        live = jnp.zeros((room,), jnp.float32).at[position].set(1.0).reshape(CLUSTERS, CAP)
        query_cells = to_cells(query_head).astype(jnp.float32)
        key_cells = to_cells(key_head).astype(jnp.float32)
        value_cells = to_cells(value_head).astype(jnp.float32)
        grad_cells = to_cells(grad_head).astype(jnp.float32)
        scores = jnp.einsum('cqd,ckd->cqk', query_cells, key_cells) * score_scale
        scores = jnp.where(live[:, None, :] > 0.5, scores, masked_score)
        top = lax.optimization_barrier(jnp.max(scores, axis=-1, keepdims=True))
        weights = jnp.exp(scores - top)
        probs = weights / lax.optimization_barrier(jnp.sum(weights, axis=-1, keepdims=True))
        probs_low = probs.astype(jnp.bfloat16).astype(jnp.float32)
        attended = jnp.einsum('cqk,ckd->cqd', probs_low, value_cells).astype(jnp.bfloat16)
        delta = jnp.einsum('cqd,cqd->cq', grad_cells, attended.astype(jnp.float32))
        grad_value = jnp.einsum('cqk,cqd->ckd', probs_low, grad_cells).astype(jnp.bfloat16)
        grad_probs = jnp.einsum('cqd,ckd->cqk', grad_cells, value_cells)
        grad_scores = (probs * (grad_probs - delta[..., None])).astype(jnp.bfloat16).astype(jnp.float32)
        grad_query = (jnp.einsum('cqk,ckd->cqd', grad_scores, key_cells) * score_scale).astype(jnp.bfloat16)
        grad_key = (jnp.einsum('cqk,cqd->ckd', grad_scores, query_cells) * score_scale).astype(jnp.bfloat16)

        def back(cells):
            return cells.reshape(room, DH)[position]
        return (back(attended), back(grad_query), back(grad_key), back(grad_value))
    stacks = lax.map(one_head, jnp.arange(H, dtype=jnp.int32))

    def merge_heads(stack):
        return jnp.transpose(stack, (1, 0, 2)).reshape(TOKENS, H * DH)
    attended_all = merge_heads(stacks[0])
    mixed = jnp.dot(attended_all, out_weight, preferred_element_type=jnp.float32).astype(jnp.bfloat16)
    return (mixed, merge_heads(stacks[1]), merge_heads(stacks[2]), merge_heads(stacks[3]))
```

```python
import functools
import math

import jax
import jax.numpy as jnp
from jax import lax
from jax.experimental import pallas as pl
from jax.experimental.pallas import tpu as pltpu
from jax.sharding import PartitionSpec as P

CLU_DEV = 8
CAP = 32
TILE = 64
WIN = TILE + 2 * CAP
VMEM_LIMIT = 48 * 1024 * 1024


def place_kernel(clusters, ids_ref, pos_ref, seg_rows_ref, seg_cols_ref):
    blocks, lanes = pos_ref.shape
    bf, f32 = jnp.bfloat16, jnp.float32
    cluster_ids = lax.broadcasted_iota(jnp.int32, (clusters, lanes), 0).astype(f32)
    slot_ids = lax.broadcasted_iota(jnp.int32, (CAP, lanes), 0).astype(f32)

    def tables(b):
        held = ids_ref[b].astype(f32)
        cluster = held[0:1] * lanes + held[1:2]
        return (
            jnp.where(cluster_ids == cluster, 1.0, 0.0),
            jnp.where(slot_ids == held[2:3], 1.0, 0.0),
        )

    def count(b, occupied):
        by_cluster, by_slot = tables(b)
        return occupied + lax.dot_general(
            by_cluster.astype(bf), by_slot.astype(bf), (((1,), (1,)), ((), ())),
            preferred_element_type=f32,
        )

    occupied = lax.fori_loop(0, blocks, count, jnp.zeros((clusters, CAP), f32))
    occupied_low = occupied.astype(bf)
    slot_from = lax.broadcasted_iota(jnp.int32, (CAP, CAP), 0)
    slot_to = lax.broadcasted_iota(jnp.int32, (CAP, CAP), 1)
    within = jnp.dot(
        occupied_low, jnp.where(slot_from < slot_to, 1.0, 0.0).astype(bf),
        preferred_element_type=f32,
    )
    size_col = jnp.sum(occupied, axis=1, keepdims=True)
    sizes = jnp.broadcast_to(size_col, (clusters, 128)).astype(bf)
    row_ids = lax.broadcasted_iota(jnp.int32, (clusters, clusters), 0)
    col_ids = lax.broadcasted_iota(jnp.int32, (clusters, clusters), 1)
    before = jnp.where(col_ids < row_ids, 1.0, 0.0).astype(bf)
    start = jnp.dot(before, sizes, preferred_element_type=f32)
    ends_col = start[:, 0:1] + size_col
    upto = jnp.where(row_ids <= col_ids, 1.0, 0.0).astype(bf)
    ends_row = lax.dot_general(
        sizes, upto, (((0,), (0,)), ((), ())), preferred_element_type=f32
    )[0:1]
    high = jnp.floor(start * (1.0 / 64.0))
    low = start - high * 64.0
    high_low, low_low, within_low = high.astype(bf), low.astype(bf), within.astype(bf)
    dims = (((0,), (0,)), ((), ()))

    def place(b, carry):
        by_cluster, by_slot = tables(b)
        by_cluster = by_cluster.astype(bf)
        high_of = lax.dot_general(high_low, by_cluster, dims, preferred_element_type=f32)[0:1]
        low_of = lax.dot_general(low_low, by_cluster, dims, preferred_element_type=f32)[0:1]
        within_of = lax.dot_general(within_low, by_cluster, dims, preferred_element_type=f32)
        inner = jnp.sum(within_of * by_slot, axis=0, keepdims=True)
        pos_ref[pl.ds(b, 1), :] = (high_of * 64.0 + low_of + inner).astype(jnp.int32)
        return carry

    lax.fori_loop(0, blocks, place, 0)
    rows = blocks * lanes

    def label_rows(t, carry):
        at = (t * TILE + lax.broadcasted_iota(jnp.int32, (TILE, clusters), 0)).astype(f32)
        label = jnp.sum(jnp.where(ends_row <= at, 1.0, 0.0), axis=1, keepdims=True)
        seg_rows_ref[pl.ds(pl.multiple_of(t * TILE, TILE), TILE), :] = label
        wide = t * TILE - CAP + lax.broadcasted_iota(jnp.int32, (clusters, WIN), 1)
        label = jnp.sum(jnp.where(ends_col <= wide.astype(f32), 1.0, 0.0), axis=0, keepdims=True)
        spot = wide[0:1]
        seg_cols_ref[t] = jnp.where((spot >= 0) & (spot < rows), label, -1.0)
        return carry

    lax.fori_loop(0, rows // TILE, label_rows, 0)


def place(ids, clusters):
    blocks, _, lanes = ids.shape
    rows = blocks * lanes
    vmem = pl.BlockSpec(memory_space=pltpu.VMEM)
    return pl.pallas_call(
        functools.partial(place_kernel, clusters),
        out_shape=(
            jax.ShapeDtypeStruct((blocks, lanes), jnp.int32),
            jax.ShapeDtypeStruct((rows, 1), jnp.float32),
            jax.ShapeDtypeStruct((rows // TILE, 1, WIN), jnp.float32),
        ),
        in_specs=[vmem],
        out_specs=(vmem, vmem, vmem),
        compiler_params=pltpu.CompilerParams(vmem_limit_bytes=VMEM_LIMIT),
        name="place",
    )(ids)


ROWS_AT_ONCE = 16


def move_in(pos_ref, block_of, load, wide, sorted_ref):
    blocks, lanes = pos_ref.shape

    def one(b, carry):
        wide[...] = load(block_of(b)).astype(jnp.float32)
        for first in range(0, lanes, ROWS_AT_ONCE):
            held = [wide[pl.ds(first + r, 1), :] for r in range(ROWS_AT_ONCE)]
            for r in range(ROWS_AT_ONCE):
                sorted_ref[pl.ds(pos_ref[b, first + r] + CAP, 1), :] = held[r]
        return carry

    lax.fori_loop(0, blocks, one, 0)


def move_out(pos_ref, block_of, sorted_ref, offset, wide, store):
    blocks, lanes = pos_ref.shape

    def one(b, carry):
        for first in range(0, lanes, ROWS_AT_ONCE):
            held = [
                sorted_ref[pl.ds(pos_ref[b, first + r] + offset, 1), :]
                for r in range(ROWS_AT_ONCE)
            ]
            for r in range(ROWS_AT_ONCE):
                wide[pl.ds(first + r, 1), :] = held[r]
        store(block_of(b), wide[...])
        return carry

    lax.fori_loop(0, blocks, one, 0)


def attend_kernel(
    high, scale, unroll,
    pos_ref, qkv_ref, grad_ref, seg_rows_ref, seg_cols_ref,
    attended_ref, grads_ref,
    wide, query, key, value, grad, att, grad_query, grad_key, grad_value,
):
    bf, f32 = jnp.bfloat16, jnp.float32
    blocks, lanes = pos_ref.shape
    rows = blocks * lanes
    low = blocks // high

    def straight(b):
        return b

    def swapped(b):
        return lax.rem(b, low) * high + b // low

    edge = jnp.zeros((CAP, wide.shape[1]), f32)
    for ref in (query, key, value, grad):
        ref[pl.ds(0, CAP), :] = edge
        ref[pl.ds(rows + CAP, CAP), :] = edge
    for part, ref in enumerate((query, key, value)):
        move_in(
            pos_ref, straight,
            lambda b, part=part: qkv_ref[b, pl.ds(part * lanes, lanes), :], wide, ref,
        )
    move_in(pos_ref, swapped, lambda b: grad_ref[b], wide, grad)
    grad_key[...] = jnp.zeros_like(grad_key)
    grad_value[...] = jnp.zeros_like(grad_value)
    nt = (((1,), (1,)), ((), ()))
    tn = (((0,), (0,)), ((), ()))

    def one_tile(t):
        base = pl.multiple_of(t * TILE, TILE)
        mine = pl.ds(pl.multiple_of(base + CAP, CAP), TILE)
        window = pl.ds(base, WIN)
        q = query[mine, :].astype(bf)
        g = grad[mine, :].astype(bf)
        k = key[window, :].astype(bf)
        v = value[window, :].astype(bf)
        same = seg_rows_ref[pl.ds(base, TILE), :] == seg_cols_ref[t]
        scores = lax.dot_general(q, k, nt, preferred_element_type=f32) * scale
        scores = jnp.where(same, scores, -1e30)
        top = jnp.max(scores, axis=1, keepdims=True)
        weights = jnp.exp(scores - top)
        probs = weights / jnp.sum(weights, axis=1, keepdims=True)
        probs_low = probs.astype(bf)
        attended = jnp.dot(probs_low, v, preferred_element_type=f32).astype(bf).astype(f32)
        att[pl.ds(base, TILE), :] = attended
        delta = jnp.sum(g.astype(f32) * attended, axis=1, keepdims=True)
        grad_probs = lax.dot_general(g, v, nt, preferred_element_type=f32)
        grad_scores = (probs * (grad_probs - delta)).astype(bf)
        grad_query[pl.ds(base, TILE), :] = jnp.dot(grad_scores, k, preferred_element_type=f32)
        more_key = lax.dot_general(grad_scores, q, tn, preferred_element_type=f32)
        more_value = lax.dot_general(probs_low, g, tn, preferred_element_type=f32)
        return window, more_key, more_value

    def tiles(step, carry):
        for window, more_key, more_value in [one_tile(step * unroll + u) for u in range(unroll)]:
            grad_key[window, :] += more_key
            grad_value[window, :] += more_value
        return carry

    lax.fori_loop(0, rows // TILE // unroll, tiles, 0)

    def put(part, factor):
        def store(b, block):
            grads_ref[b, pl.ds(part * lanes, lanes), :] = (block * factor).astype(bf)
        return store

    def put_attended(b, block):
        attended_ref[b] = block.astype(bf)

    move_out(pos_ref, swapped, att, 0, wide, put_attended)
    move_out(pos_ref, straight, grad_query, 0, wide, put(0, scale))
    move_out(pos_ref, straight, grad_key, CAP, wide, put(1, scale))
    move_out(pos_ref, straight, grad_value, CAP, wide, put(2, 1.0))


def attend(pos, qkv, grad, seg_rows, seg_cols, high):
    blocks, lanes = pos.shape
    rows = blocks * lanes
    size = qkv.shape[-1]
    f32 = jnp.float32
    vmem = pl.BlockSpec(memory_space=pltpu.VMEM)
    smem = pl.BlockSpec(memory_space=pltpu.SMEM)
    padded = pltpu.VMEM((rows + 2 * CAP, size), f32)
    plain = pltpu.VMEM((rows, size), f32)
    return pl.pallas_call(
        functools.partial(attend_kernel, high, 1.0 / math.sqrt(size), 4),
        out_shape=(
            jax.ShapeDtypeStruct((blocks, lanes, size), jnp.bfloat16),
            jax.ShapeDtypeStruct((blocks, 3 * lanes, size), jnp.bfloat16),
        ),
        in_specs=[smem, vmem, vmem, vmem, vmem],
        out_specs=(vmem, vmem),
        scratch_shapes=[
            pltpu.VMEM((lanes, size), f32),
            padded, padded, padded, padded, plain, plain, padded, padded,
        ],
        compiler_params=pltpu.CompilerParams(vmem_limit_bytes=VMEM_LIMIT),
        name="attend",
    )(pos, qkv, grad, seg_rows, seg_cols)


def by_clusters(query_rows, key_rows, value_rows, cluster_id, slot_index, out_weight, grad_out):
    rows_dev = query_rows.shape[0]
    heads_dev = cluster_id.shape[0]
    head_size = query_rows.shape[1] // heads_dev
    owners = lax.axis_size("seq")
    send_most = 2 * rows_dev // owners
    buffer_rows = owners * send_most
    room = CLU_DEV * CAP
    score_scale = 1.0 / math.sqrt(head_size)
    masked_score = -1e30
    owner = cluster_id // CLU_DEV
    owner_onehot = (owner[:, :, None] == jnp.arange(owners, dtype=jnp.int32)[None, None, :]).astype(
        jnp.bfloat16
    )
    row_ids = jnp.arange(rows_dev, dtype=jnp.int32)
    lower = (row_ids[:, None] > row_ids[None, :]).astype(jnp.bfloat16)
    earlier = jnp.einsum("ij,hjo->hio", lower, owner_onehot, preferred_element_type=jnp.float32)
    rank = jnp.sum(earlier * owner_onehot.astype(jnp.float32), axis=2).astype(jnp.int32)
    place = owner * send_most + rank
    target = cluster_id % CLU_DEV * CAP + slot_index
    buffer_ids = jnp.arange(buffer_rows, dtype=jnp.int32)
    send_table = (place[:, None, :] == buffer_ids[None, :, None]).astype(jnp.bfloat16)

    def to_buffer(rows):
        split = rows.reshape(rows_dev, heads_dev, head_size)
        filled = jnp.einsum(
            "hbi,ihd->bhd", send_table, split, preferred_element_type=jnp.float32
        ).astype(rows.dtype)
        return filled.reshape(buffer_rows, heads_dev * head_size)

    def from_buffer(buffer):
        split = buffer.reshape(buffer_rows, heads_dev, head_size)
        picked = jnp.einsum(
            "hbi,bhd->ihd", send_table, split, preferred_element_type=jnp.float32
        ).astype(buffer.dtype)
        return picked.reshape(rows_dev, heads_dev * head_size)

    target_rows = (
        jnp.einsum(
            "hbi,hi->bh", send_table.astype(jnp.float32), (target - room).astype(jnp.float32)
        ).astype(jnp.int32)
        + room
    )
    arrived = lax.all_to_all(target_rows, "seq", split_axis=0, concat_axis=0, tiled=True)
    routed_query, routed_key, routed_value = (
        lax.all_to_all(to_buffer(query_rows), "seq", split_axis=0, concat_axis=0, tiled=True),
        lax.all_to_all(to_buffer(key_rows), "seq", split_axis=0, concat_axis=0, tiled=True),
        lax.all_to_all(to_buffer(value_rows), "seq", split_axis=0, concat_axis=0, tiled=True),
    )
    room_ids = jnp.arange(room, dtype=jnp.int32)
    cell_table = (arrived.T[:, None, :] == room_ids[None, :, None]).astype(jnp.bfloat16)

    def to_cells(buffer):
        split = buffer.reshape(buffer_rows, heads_dev, head_size)
        cells = jnp.einsum(
            "hrb,bhd->hrd", cell_table, split, preferred_element_type=jnp.float32
        ).astype(buffer.dtype)
        return cells.reshape(heads_dev, CLU_DEV, CAP, head_size)

    def to_returns(cells):
        flat = cells.reshape(heads_dev, room, head_size)
        picked = jnp.einsum(
            "hrb,hrd->bhd", cell_table, flat, preferred_element_type=jnp.float32
        ).astype(cells.dtype)
        return picked.reshape(buffer_rows, heads_dev * head_size)

    live = jnp.sum(cell_table.astype(jnp.float32), axis=2).reshape(heads_dev, CLU_DEV, CAP)
    query_cells = to_cells(routed_query)
    key_cells = to_cells(routed_key)
    value_cells = to_cells(routed_value)
    scores = (
        jnp.einsum("hcqd,hckd->hcqk", query_cells, key_cells, preferred_element_type=jnp.float32)
        * score_scale
    )
    scores = jnp.where(live[:, :, None, :] > 0.5, scores, masked_score)
    top = jnp.max(scores, axis=-1, keepdims=True)
    weights = jnp.exp(scores - top)
    probs = weights / jnp.sum(weights, axis=-1, keepdims=True)
    probs_low = probs.astype(jnp.bfloat16)
    attended_cells = jnp.einsum(
        "hcqk,hckd->hcqd", probs_low, value_cells, preferred_element_type=jnp.float32
    ).astype(jnp.bfloat16)
    returned = lax.all_to_all(
        to_returns(attended_cells), "seq", split_axis=0, concat_axis=0, tiled=True
    )
    attended = from_buffer(returned)
    full_weight = lax.all_gather(out_weight, "seq", axis=1, tiled=True)
    rows = attended
    mixed = lax.psum_scatter(
        jnp.dot(rows, full_weight, preferred_element_type=jnp.float32).astype(jnp.bfloat16),
        "tensor",
        scatter_dimension=0,
        tiled=True,
    )
    grad_attended = lax.dot_general(
        lax.all_gather(grad_out, "tensor", axis=0, tiled=True),
        full_weight,
        (((1,), (1,)), ((), ())),
        preferred_element_type=jnp.float32,
    )
    grad_low = grad_attended.astype(jnp.bfloat16)
    routed_grad = lax.all_to_all(
        to_buffer(grad_low), "seq", split_axis=0, concat_axis=0, tiled=True
    )
    grad_cells = to_cells(routed_grad)
    backward_low = probs.astype(jnp.bfloat16)
    delta = jnp.einsum(
        "hcqd,hcqd->hcq", grad_cells, attended_cells, preferred_element_type=jnp.float32
    )
    grad_value = jnp.einsum(
        "hcqk,hcqd->hckd", backward_low, grad_cells, preferred_element_type=jnp.float32
    ).astype(jnp.bfloat16)
    grad_probs = jnp.einsum(
        "hcqd,hckd->hcqk", grad_cells, value_cells, preferred_element_type=jnp.float32
    )
    grad_scores = (probs * (grad_probs - delta[..., None])).astype(jnp.bfloat16)
    grad_query = (
        jnp.einsum("hcqk,hckd->hcqd", grad_scores, key_cells, preferred_element_type=jnp.float32)
        * score_scale
    ).astype(jnp.bfloat16)
    grad_key = (
        jnp.einsum("hcqk,hcqd->hckd", grad_scores, query_cells, preferred_element_type=jnp.float32)
        * score_scale
    ).astype(jnp.bfloat16)
    back_query, back_key, back_value = (
        lax.all_to_all(to_returns(grad_query), "seq", split_axis=0, concat_axis=0, tiled=True),
        lax.all_to_all(to_returns(grad_key), "seq", split_axis=0, concat_axis=0, tiled=True),
        lax.all_to_all(to_returns(grad_value), "seq", split_axis=0, concat_axis=0, tiled=True),
    )
    return (mixed, from_buffer(back_query), from_buffer(back_key), from_buffer(back_value))


def by_heads(query_rows, key_rows, value_rows, cluster_id, slot_index, out_weight, grad_out):
    rows_dev, width = query_rows.shape
    heads_dev = cluster_id.shape[0]
    head_size = width // heads_dev
    owners = lax.axis_size("seq")
    columns_dev = out_weight.shape[1]
    columns = owners * columns_dev
    high, low = split(owners)
    planes = [[h * low + p for p in range(low)] for h in range(high)]
    stacks = [[h * low + p for h in range(high)] for p in range(low)]
    bf, f32 = jnp.bfloat16, jnp.float32

    def exchange(rows, groups=None):
        return lax.all_to_all(
            rows, "seq", split_axis=0, concat_axis=0, tiled=True, axis_index_groups=groups
        )

    def of_heads(rows):
        return rows.reshape(rows_dev, heads_dev, head_size).transpose(1, 0, 2)

    def of_rows(heads):
        return heads.transpose(1, 0, 2).reshape(rows_dev, width)

    weight_rows = out_weight.T.reshape(columns_dev, heads_dev, head_size).transpose(1, 0, 2)
    ids = jnp.stack([cluster_id // rows_dev, cluster_id % rows_dev, slot_index], axis=1)
    ids = jnp.pad(ids, ((0, 0), (0, 13), (0, 0))).astype(bf)
    first = exchange(jnp.concatenate([weight_rows, ids], axis=1))
    grad_out_stack = lax.all_gather(grad_out, "seq", axis=0, tiled=True, axis_index_groups=stacks)
    head_weight = first[:, :columns_dev].reshape(columns, head_size)
    plane_weight = lax.all_gather(head_weight, "seq", axis=0, axis_index_groups=planes)
    pos, seg_rows, seg_cols = place(first[:, columns_dev:], CLU_DEV * owners)
    qkv = exchange(
        jnp.concatenate([of_heads(query_rows), of_heads(key_rows), of_heads(value_rows)], axis=1)
    )
    grad_plane = lax.dot_general(
        plane_weight, grad_out_stack, (((1,), (1,)), ((), ())), preferred_element_type=f32
    ).astype(bf)
    grad_head = exchange(grad_plane.transpose(0, 2, 1), planes)
    grad_head = grad_head.reshape(owners, rows_dev, head_size)
    attended, grads = attend(pos, qkv, grad_head, seg_rows, seg_cols, high)
    attended_plane = exchange(attended.reshape(low, high * rows_dev, head_size), planes)
    back = exchange(grads)
    partial = lax.dot_general(
        attended_plane, plane_weight, (((0, 2), (0, 2)), ((), ())), preferred_element_type=f32
    ).astype(bf)
    mixed = lax.psum_scatter(
        partial, "seq", scatter_dimension=0, tiled=True, axis_index_groups=stacks
    )
    grad_query, grad_key, grad_value = (
        of_rows(back[:, part * rows_dev : (part + 1) * rows_dev]) for part in range(3)
    )
    return mixed, grad_query, grad_key, grad_value


def split(owners):
    high = 1
    while 4 * high * high <= owners:
        high *= 2
    return high, owners // high


def solution(mesh):
    def shards(*args):
        heads_dev = args[3].shape[0]
        owners = lax.axis_size("seq")
        if heads_dev == owners and lax.axis_size("tensor") == 1:
            return by_heads(*args)
        return by_clusters(*args)

    return jax.shard_map(
        shards,
        mesh=mesh,
        in_specs=(
            P("seq", "tensor"),
            P("seq", "tensor"),
            P("seq", "tensor"),
            P("tensor", "seq"),
            P("tensor", "seq"),
            P("tensor", "seq"),
            P(("seq", "tensor"), None),
        ),
        out_specs=(
            P(("seq", "tensor"), None),
            P("seq", "tensor"),
            P("seq", "tensor"),
            P("seq", "tensor"),
        ),
        check_vma=False,
    )
```

```python
import functools
import math

import jax
import jax.numpy as jnp
from jax import lax
from jax.experimental import pallas as pl
from jax.experimental.pallas import tpu as pltpu
from jax.sharding import PartitionSpec as P

CLU_DEV = 8
CAP = 32
TILE = 64
WIN = TILE + 2 * CAP
MASKED = -1e30
UNROLL = 8
VMEM = pl.BlockSpec(memory_space=pltpu.VMEM)
SMEM = pl.BlockSpec(memory_space=pltpu.SMEM)
PARAMS = pltpu.CompilerParams(vmem_limit_bytes=48 * 1024 * 1024)
NT = (((1,), (1,)), ((), ()))
TN = (((0,), (0,)), ((), ()))


def place_kernel(clusters, ids_ref, pos_ref, bias_ref):
    blocks, lanes = pos_ref.shape
    bf, f32 = jnp.bfloat16, jnp.float32
    cluster_ids = lax.broadcasted_iota(jnp.int32, (clusters, lanes), 0).astype(f32)
    slot_ids = lax.broadcasted_iota(jnp.int32, (CAP, lanes), 0).astype(f32)

    def tables(b):
        held = ids_ref[b].astype(f32)
        cluster = held[0:1] * lanes + held[1:2]
        return (
            jnp.where(cluster_ids == cluster, 1.0, 0.0),
            jnp.where(slot_ids == held[2:3], 1.0, 0.0),
        )

    def count(b, occupied):
        by_cluster, by_slot = tables(b)
        return occupied + lax.dot_general(
            by_cluster.astype(bf), by_slot.astype(bf), (((1,), (1,)), ((), ())),
            preferred_element_type=f32,
        )

    occupied = lax.fori_loop(0, blocks, count, jnp.zeros((clusters, CAP), f32))
    occupied_low = occupied.astype(bf)
    slot_from = lax.broadcasted_iota(jnp.int32, (CAP, CAP), 0)
    slot_to = lax.broadcasted_iota(jnp.int32, (CAP, CAP), 1)
    within = jnp.dot(
        occupied_low, jnp.where(slot_from < slot_to, 1.0, 0.0).astype(bf),
        preferred_element_type=f32,
    )
    size_col = jnp.sum(occupied, axis=1, keepdims=True)
    sizes = jnp.broadcast_to(size_col, (clusters, 128)).astype(bf)
    row_ids = lax.broadcasted_iota(jnp.int32, (clusters, clusters), 0)
    col_ids = lax.broadcasted_iota(jnp.int32, (clusters, clusters), 1)
    before = jnp.where(col_ids < row_ids, 1.0, 0.0).astype(bf)
    start = jnp.dot(before, sizes, preferred_element_type=f32)
    ends_col = start[:, 0:1] + size_col
    upto = jnp.where(row_ids <= col_ids, 1.0, 0.0).astype(bf)
    ends_row = lax.dot_general(
        sizes, upto, (((0,), (0,)), ((), ())), preferred_element_type=f32
    )[0:1]
    high = jnp.floor(start * (1.0 / 64.0))
    low = start - high * 64.0
    high_low, low_low, within_low = high.astype(bf), low.astype(bf), within.astype(bf)
    dims = (((0,), (0,)), ((), ()))

    def place(b, carry):
        by_cluster, by_slot = tables(b)
        by_cluster = by_cluster.astype(bf)
        high_of = lax.dot_general(high_low, by_cluster, dims, preferred_element_type=f32)[0:1]
        low_of = lax.dot_general(low_low, by_cluster, dims, preferred_element_type=f32)[0:1]
        within_of = lax.dot_general(within_low, by_cluster, dims, preferred_element_type=f32)
        inner = jnp.sum(within_of * by_slot, axis=0, keepdims=True)
        pos_ref[pl.ds(b, 1), :] = (high_of * 64.0 + low_of + inner).astype(jnp.int32)
        return carry

    lax.fori_loop(0, blocks, place, 0)
    rows = blocks * lanes

    def labels(t, carry):
        at = (t * TILE + lax.broadcasted_iota(jnp.int32, (TILE, clusters), 0)).astype(f32)
        mine = jnp.sum(jnp.where(ends_row <= at, 1.0, 0.0), axis=1, keepdims=True)
        wide = t * TILE - CAP + lax.broadcasted_iota(jnp.int32, (clusters, WIN), 1)
        other = jnp.sum(jnp.where(ends_col <= wide.astype(f32), 1.0, 0.0), axis=0, keepdims=True)
        spot = wide[0:1]
        other = jnp.where((spot >= 0) & (spot < rows), other, -1.0)
        at = pl.ds(pl.multiple_of(t * TILE, TILE), TILE)
        bias_ref[at, :] = jnp.where(mine == other, 0.0, MASKED).astype(bf)
        return carry

    lax.fori_loop(0, rows // TILE, labels, 0)


def place(ids, clusters):
    blocks, _, lanes = ids.shape
    rows = blocks * lanes
    return pl.pallas_call(
        functools.partial(place_kernel, clusters),
        out_shape=(
            jax.ShapeDtypeStruct((blocks, lanes), jnp.int32),
            jax.ShapeDtypeStruct((rows, WIN), jnp.bfloat16),
        ),
        in_specs=[VMEM],
        out_specs=(VMEM, VMEM),
        compiler_params=PARAMS,
        name="place",
    )(ids)


ROWS_AT_ONCE = 16


def move_in(pos_ref, block_of, load, wide, sorted_ref, offset):
    blocks, lanes = pos_ref.shape

    def one(b, carry):
        wide[...] = load(block_of(b)).astype(jnp.float32)
        for first in range(0, lanes, ROWS_AT_ONCE):
            held = [wide[pl.ds(first + r, 1), :] for r in range(ROWS_AT_ONCE)]
            for r in range(ROWS_AT_ONCE):
                sorted_ref[pl.ds(pos_ref[b, first + r] + offset, 1), :] = held[r]
        return carry

    lax.fori_loop(0, blocks, one, 0)


def move_out(pos_ref, sorted_ref, offset, wide, store):
    blocks, lanes = pos_ref.shape

    def one(b, carry):
        for first in range(0, lanes, ROWS_AT_ONCE):
            held = [
                sorted_ref[pl.ds(pos_ref[b, first + r] + offset, 1), :]
                for r in range(ROWS_AT_ONCE)
            ]
            for r in range(ROWS_AT_ONCE):
                wide[pl.ds(first + r, 1), :] = held[r]
        store(b, wide[...])
        return carry

    lax.fori_loop(0, blocks, one, 0)


def tiles_of(step):
    bases = [pl.multiple_of((step * UNROLL + u) * TILE, TILE) for u in range(UNROLL)]
    tiles = [pl.ds(base, TILE) for base in bases]
    windows = [pl.ds(base, WIN) for base in bases]
    inner = [pl.ds(pl.multiple_of(base + CAP, CAP), TILE) for base in bases]
    return tiles, windows, inner


def forward_kernel(
    low, scale,
    pos_ref, qkv_ref, bias_ref,
    attended_ref, sorted_ref, query_ref, key_ref, value_ref, probs_ref,
    wide, query, key, value, att,
):
    bf, f32 = jnp.bfloat16, jnp.float32
    blocks, lanes = pos_ref.shape
    rows = blocks * lanes
    high = blocks // low
    edge = jnp.zeros((CAP, wide.shape[1]), f32)
    for part, (ref, out) in enumerate(
        ((query, query_ref), (key, key_ref), (value, value_ref))
    ):
        ref[pl.ds(0, CAP), :] = edge
        ref[pl.ds(rows + CAP, CAP), :] = edge
        move_in(
            pos_ref, lambda b: b,
            lambda b, part=part: qkv_ref[b, pl.ds(part * lanes, lanes), :], wide, ref, CAP,
        )
        out[...] = ref[...].astype(bf)

    def some(step, carry):
        tiles, windows, inner = tiles_of(step)
        qs = [query_ref[at, :] for at in inner]
        ks = [key_ref[at, :] for at in windows]
        vs = [value_ref[at, :] for at in windows]
        biases = [bias_ref[at, :].astype(f32) for at in tiles]
        scores = [lax.dot_general(q, k, NT, preferred_element_type=f32) for q, k in zip(qs, ks)]
        scores = [s * scale + bias for s, bias in zip(scores, biases)]
        tops = [jnp.max(s, axis=1, keepdims=True) for s in scores]
        weights = [jnp.exp(s - top) for s, top in zip(scores, tops)]
        sums = [jnp.sum(w, axis=1, keepdims=True) for w in weights]
        probs = [w / total for w, total in zip(weights, sums)]
        attended = [
            jnp.dot(p.astype(bf), v, preferred_element_type=f32) for p, v in zip(probs, vs)
        ]
        for at, p, one in zip(tiles, probs, attended):
            probs_ref[at, :] = p
            att[at, :] = one
            sorted_ref[at, :] = one.astype(bf)
        return carry

    lax.fori_loop(0, rows // TILE // UNROLL, some, 0)

    def put(b, block):
        attended_ref[lax.rem(b, low) * high + b // low] = block.astype(bf)

    move_out(pos_ref, att, 0, wide, put)


def forward(pos, qkv, bias, low):
    blocks, lanes = pos.shape
    rows = blocks * lanes
    size = qkv.shape[-1]
    bf = jnp.bfloat16
    padded = jax.ShapeDtypeStruct((rows + 2 * CAP, size), bf)
    sorted_rows = pltpu.VMEM((rows + 2 * CAP, size), jnp.float32)
    return pl.pallas_call(
        functools.partial(forward_kernel, low, 1.0 / math.sqrt(size)),
        out_shape=(
            jax.ShapeDtypeStruct((blocks, lanes, size), bf),
            jax.ShapeDtypeStruct((rows, size), bf),
            padded, padded, padded,
            jax.ShapeDtypeStruct((rows, WIN), jnp.float32),
        ),
        in_specs=[SMEM, VMEM, VMEM],
        out_specs=(VMEM,) * 6,
        scratch_shapes=[
            pltpu.VMEM((lanes, size), jnp.float32),
            sorted_rows, sorted_rows, sorted_rows,
            pltpu.VMEM((rows, size), jnp.float32),
        ],
        compiler_params=PARAMS,
        name="forward",
    )(pos, qkv, bias)


def backward_kernel(
    low, scale,
    pos_ref, grad_ref, sorted_ref, query_ref, key_ref, value_ref, probs_ref,
    grads_ref,
    wide, grad, grad_query, grad_key, grad_value,
):
    bf, f32 = jnp.bfloat16, jnp.float32
    blocks, lanes = pos_ref.shape
    rows = blocks * lanes
    high = blocks // low
    move_in(
        pos_ref, lambda b: lax.rem(b, low) * high + b // low,
        lambda b: grad_ref[b], wide, grad, 0,
    )
    grad_key[...] = jnp.zeros_like(grad_key)
    grad_value[...] = jnp.zeros_like(grad_value)

    def some(step, carry):
        tiles, windows, inner = tiles_of(step)
        gs = [grad[at, :].astype(bf) for at in tiles]
        qs = [query_ref[at, :] for at in inner]
        ks = [key_ref[at, :] for at in windows]
        vs = [value_ref[at, :] for at in windows]
        probs = [probs_ref[at, :] for at in tiles]
        attended = [sorted_ref[at, :].astype(f32) for at in tiles]
        grad_probs = [lax.dot_general(g, v, NT, preferred_element_type=f32) for g, v in zip(gs, vs)]
        lows = [p.astype(bf) for p in probs]
        more_values = [
            lax.dot_general(p, g, TN, preferred_element_type=f32) for p, g in zip(lows, gs)
        ]
        deltas = [
            jnp.sum(g.astype(f32) * one, axis=1, keepdims=True) for g, one in zip(gs, attended)
        ]
        grad_scores = [
            (p * (gp - delta)).astype(bf) for p, gp, delta in zip(probs, grad_probs, deltas)
        ]
        grad_queries = [jnp.dot(d, k, preferred_element_type=f32) for d, k in zip(grad_scores, ks)]
        more_keys = [
            lax.dot_general(d, q, TN, preferred_element_type=f32) for d, q in zip(grad_scores, qs)
        ]
        for at, one in zip(tiles, grad_queries):
            grad_query[at, :] = one
        for at, more_key, more_value in zip(windows, more_keys, more_values):
            grad_key[at, :] += more_key
            grad_value[at, :] += more_value
        return carry

    lax.fori_loop(0, rows // TILE // UNROLL, some, 0)

    def put(part, factor):
        def store(b, block):
            grads_ref[b, pl.ds(part * lanes, lanes), :] = (block * factor).astype(bf)
        return store

    move_out(pos_ref, grad_query, 0, wide, put(0, scale))
    move_out(pos_ref, grad_key, CAP, wide, put(1, scale))
    move_out(pos_ref, grad_value, CAP, wide, put(2, 1.0))


def backward(pos, grad, kept, low):
    blocks, lanes = pos.shape
    rows = blocks * lanes
    size = grad.shape[-1]
    f32 = jnp.float32
    plain = pltpu.VMEM((rows, size), f32)
    padded = pltpu.VMEM((rows + 2 * CAP, size), f32)
    return pl.pallas_call(
        functools.partial(backward_kernel, low, 1.0 / math.sqrt(size)),
        out_shape=jax.ShapeDtypeStruct((blocks, 3 * lanes, size), jnp.bfloat16),
        in_specs=[SMEM] + [VMEM] * 6,
        out_specs=VMEM,
        scratch_shapes=[pltpu.VMEM((lanes, size), f32), plain, plain, padded, padded],
        compiler_params=PARAMS,
        name="backward",
    )(pos, grad, *kept)


def pack_kernel(*refs):
    out_ref = refs[-1]
    heads, rows, size = out_ref.shape
    rows = rows // (len(refs) - 1)
    for part, ref in enumerate(refs[:-1]):
        for h in range(heads):
            out_ref[h, pl.ds(part * rows, rows), :] = ref[:, pl.ds(h * size, size)]


def pack(arrays, heads):
    rows, width = arrays[0].shape
    size = width // heads
    step = math.gcd(heads, 8)
    return pl.pallas_call(
        pack_kernel,
        grid=(heads // step,),
        out_shape=jax.ShapeDtypeStruct((heads, len(arrays) * rows, size), arrays[0].dtype),
        in_specs=[pl.BlockSpec((rows, step * size), lambda i: (0, i))] * len(arrays),
        out_specs=pl.BlockSpec((step, len(arrays) * rows, size), lambda i: (i, 0, 0)),
        compiler_params=PARAMS,
        name="pack",
    )(*arrays)


def unpack_kernel(in_ref, *refs):
    heads, rows, size = in_ref.shape
    rows = rows // len(refs)
    for part, ref in enumerate(refs):
        for h in range(heads):
            ref[:, pl.ds(h * size, size)] = in_ref[h, pl.ds(part * rows, rows), :]


def unpack(packed, parts):
    heads, rows, size = packed.shape
    rows = rows // parts
    step = math.gcd(heads, 8)
    return pl.pallas_call(
        unpack_kernel,
        grid=(heads // step,),
        out_shape=(jax.ShapeDtypeStruct((rows, heads * size), packed.dtype),) * parts,
        in_specs=[pl.BlockSpec((step, parts * rows, size), lambda i: (i, 0, 0))],
        out_specs=(pl.BlockSpec((rows, step * size), lambda i: (0, i)),) * parts,
        compiler_params=PARAMS,
        name="unpack",
    )(packed)


def by_clusters(query_rows, key_rows, value_rows, cluster_id, slot_index, out_weight, grad_out):
    rows_dev = query_rows.shape[0]
    heads_dev = cluster_id.shape[0]
    head_size = query_rows.shape[1] // heads_dev
    owners = lax.axis_size("seq")
    send_most = 2 * rows_dev // owners
    buffer_rows = owners * send_most
    room = CLU_DEV * CAP
    score_scale = 1.0 / math.sqrt(head_size)
    masked_score = -1e30
    owner = cluster_id // CLU_DEV
    owner_onehot = (owner[:, :, None] == jnp.arange(owners, dtype=jnp.int32)[None, None, :]).astype(
        jnp.bfloat16
    )
    row_ids = jnp.arange(rows_dev, dtype=jnp.int32)
    lower = (row_ids[:, None] > row_ids[None, :]).astype(jnp.bfloat16)
    earlier = jnp.einsum("ij,hjo->hio", lower, owner_onehot, preferred_element_type=jnp.float32)
    rank = jnp.sum(earlier * owner_onehot.astype(jnp.float32), axis=2).astype(jnp.int32)
    place = owner * send_most + rank
    target = cluster_id % CLU_DEV * CAP + slot_index
    buffer_ids = jnp.arange(buffer_rows, dtype=jnp.int32)
    send_table = (place[:, None, :] == buffer_ids[None, :, None]).astype(jnp.bfloat16)

    def to_buffer(rows):
        split = rows.reshape(rows_dev, heads_dev, head_size)
        filled = jnp.einsum(
            "hbi,ihd->bhd", send_table, split, preferred_element_type=jnp.float32
        ).astype(rows.dtype)
        return filled.reshape(buffer_rows, heads_dev * head_size)

    def from_buffer(buffer):
        split = buffer.reshape(buffer_rows, heads_dev, head_size)
        picked = jnp.einsum(
            "hbi,bhd->ihd", send_table, split, preferred_element_type=jnp.float32
        ).astype(buffer.dtype)
        return picked.reshape(rows_dev, heads_dev * head_size)

    target_rows = (
        jnp.einsum(
            "hbi,hi->bh", send_table.astype(jnp.float32), (target - room).astype(jnp.float32)
        ).astype(jnp.int32)
        + room
    )
    arrived = lax.all_to_all(target_rows, "seq", split_axis=0, concat_axis=0, tiled=True)
    routed_query, routed_key, routed_value = (
        lax.all_to_all(to_buffer(query_rows), "seq", split_axis=0, concat_axis=0, tiled=True),
        lax.all_to_all(to_buffer(key_rows), "seq", split_axis=0, concat_axis=0, tiled=True),
        lax.all_to_all(to_buffer(value_rows), "seq", split_axis=0, concat_axis=0, tiled=True),
    )
    room_ids = jnp.arange(room, dtype=jnp.int32)
    cell_table = (arrived.T[:, None, :] == room_ids[None, :, None]).astype(jnp.bfloat16)

    def to_cells(buffer):
        split = buffer.reshape(buffer_rows, heads_dev, head_size)
        cells = jnp.einsum(
            "hrb,bhd->hrd", cell_table, split, preferred_element_type=jnp.float32
        ).astype(buffer.dtype)
        return cells.reshape(heads_dev, CLU_DEV, CAP, head_size)

    def to_returns(cells):
        flat = cells.reshape(heads_dev, room, head_size)
        picked = jnp.einsum(
            "hrb,hrd->bhd", cell_table, flat, preferred_element_type=jnp.float32
        ).astype(cells.dtype)
        return picked.reshape(buffer_rows, heads_dev * head_size)

    live = jnp.sum(cell_table.astype(jnp.float32), axis=2).reshape(heads_dev, CLU_DEV, CAP)
    query_cells = to_cells(routed_query)
    key_cells = to_cells(routed_key)
    value_cells = to_cells(routed_value)
    scores = (
        jnp.einsum("hcqd,hckd->hcqk", query_cells, key_cells, preferred_element_type=jnp.float32)
        * score_scale
    )
    scores = jnp.where(live[:, :, None, :] > 0.5, scores, masked_score)
    top = jnp.max(scores, axis=-1, keepdims=True)
    weights = jnp.exp(scores - top)
    probs = weights / jnp.sum(weights, axis=-1, keepdims=True)
    probs_low = probs.astype(jnp.bfloat16)
    attended_cells = jnp.einsum(
        "hcqk,hckd->hcqd", probs_low, value_cells, preferred_element_type=jnp.float32
    ).astype(jnp.bfloat16)
    returned = lax.all_to_all(
        to_returns(attended_cells), "seq", split_axis=0, concat_axis=0, tiled=True
    )
    attended = from_buffer(returned)
    full_weight = lax.all_gather(out_weight, "seq", axis=1, tiled=True)
    rows = attended
    mixed = lax.psum_scatter(
        jnp.dot(rows, full_weight, preferred_element_type=jnp.float32).astype(jnp.bfloat16),
        "tensor",
        scatter_dimension=0,
        tiled=True,
    )
    grad_attended = lax.dot_general(
        lax.all_gather(grad_out, "tensor", axis=0, tiled=True),
        full_weight,
        (((1,), (1,)), ((), ())),
        preferred_element_type=jnp.float32,
    )
    grad_low = grad_attended.astype(jnp.bfloat16)
    routed_grad = lax.all_to_all(
        to_buffer(grad_low), "seq", split_axis=0, concat_axis=0, tiled=True
    )
    grad_cells = to_cells(routed_grad)
    backward_low = probs.astype(jnp.bfloat16)
    delta = jnp.einsum(
        "hcqd,hcqd->hcq", grad_cells, attended_cells, preferred_element_type=jnp.float32
    )
    grad_value = jnp.einsum(
        "hcqk,hcqd->hckd", backward_low, grad_cells, preferred_element_type=jnp.float32
    ).astype(jnp.bfloat16)
    grad_probs = jnp.einsum(
        "hcqd,hckd->hcqk", grad_cells, value_cells, preferred_element_type=jnp.float32
    )
    grad_scores = (probs * (grad_probs - delta[..., None])).astype(jnp.bfloat16)
    grad_query = (
        jnp.einsum("hcqk,hckd->hcqd", grad_scores, key_cells, preferred_element_type=jnp.float32)
        * score_scale
    ).astype(jnp.bfloat16)
    grad_key = (
        jnp.einsum("hcqk,hcqd->hckd", grad_scores, query_cells, preferred_element_type=jnp.float32)
        * score_scale
    ).astype(jnp.bfloat16)
    back_query, back_key, back_value = (
        lax.all_to_all(to_returns(grad_query), "seq", split_axis=0, concat_axis=0, tiled=True),
        lax.all_to_all(to_returns(grad_key), "seq", split_axis=0, concat_axis=0, tiled=True),
        lax.all_to_all(to_returns(grad_value), "seq", split_axis=0, concat_axis=0, tiled=True),
    )
    return (mixed, from_buffer(back_query), from_buffer(back_key), from_buffer(back_value))


def by_heads(query_rows, key_rows, value_rows, cluster_id, slot_index, out_weight, grad_out):
    rows_dev, width = query_rows.shape
    heads_dev = cluster_id.shape[0]
    head_size = width // heads_dev
    owners = lax.axis_size("seq")
    columns_dev = out_weight.shape[1]
    columns = owners * columns_dev
    high, low = split(owners)
    planes = [[h * low + p for p in range(low)] for h in range(high)]
    stacks = [[h * low + p for h in range(high)] for p in range(low)]
    bf, f32 = jnp.bfloat16, jnp.float32

    def exchange(rows, groups=None):
        return lax.all_to_all(
            rows, "seq", split_axis=0, concat_axis=0, tiled=True, axis_index_groups=groups
        )

    weight_rows = out_weight.T.reshape(columns_dev, heads_dev, head_size).transpose(1, 0, 2)
    ids = jnp.stack([cluster_id // rows_dev, cluster_id % rows_dev, slot_index], axis=1)
    ids = jnp.pad(ids, ((0, 0), (0, 13), (0, 0))).astype(bf)
    first = exchange(jnp.concatenate([weight_rows, ids], axis=1))
    grad_out_stack = lax.all_gather(grad_out, "seq", axis=0, tiled=True, axis_index_groups=stacks)
    packed = pack((query_rows, key_rows, value_rows), heads_dev)
    packed, first = lax.optimization_barrier((packed, first))
    qkv = exchange(packed)
    head_weight = first[:, :columns_dev].reshape(columns, head_size)
    plane_weight = lax.all_gather(head_weight, "seq", axis=0, axis_index_groups=planes)
    pos, bias = place(first[:, columns_dev:], CLU_DEV * owners)
    grad_plane = lax.dot_general(
        plane_weight, grad_out_stack, (((1,), (1,)), ((), ())), preferred_element_type=f32
    ).astype(bf)
    grad_plane = grad_plane.transpose(0, 2, 1)
    grad_plane, qkv = lax.optimization_barrier((grad_plane, qkv))
    grad_head = exchange(grad_plane, planes).reshape(owners, rows_dev, head_size)
    attended, *kept = forward(pos, qkv, bias, low)
    attended_plane = exchange(attended.reshape(low, high * rows_dev, head_size), planes)
    grads = backward(pos, grad_head, kept, low)
    back = exchange(grads)
    partial = lax.dot_general(
        attended_plane, plane_weight, (((0, 2), (0, 2)), ((), ())), preferred_element_type=f32
    ).astype(bf)
    mixed = lax.psum_scatter(
        partial, "seq", scatter_dimension=0, tiled=True, axis_index_groups=stacks
    )
    return (mixed, *unpack(back, 3))


def split(owners):
    high = 1
    while 4 * high * high <= owners:
        high *= 2
    return high, owners // high


def solution(mesh):
    def shards(*args):
        heads_dev = args[3].shape[0]
        owners = lax.axis_size("seq")
        if heads_dev == owners and lax.axis_size("tensor") == 1:
            return by_heads(*args)
        return by_clusters(*args)

    return jax.shard_map(
        shards,
        mesh=mesh,
        in_specs=(
            P("seq", "tensor"),
            P("seq", "tensor"),
            P("seq", "tensor"),
            P("tensor", "seq"),
            P("tensor", "seq"),
            P("tensor", "seq"),
            P(("seq", "tensor"), None),
        ),
        out_specs=(
            P(("seq", "tensor"), None),
            P("seq", "tensor"),
            P("seq", "tensor"),
            P("seq", "tensor"),
        ),
        check_vma=False,
    )
```

```python
import functools
import math

import jax
import jax.numpy as jnp
from jax import lax
from jax.experimental import pallas as pl
from jax.experimental.pallas import tpu as pltpu
from jax.sharding import PartitionSpec as P

CLU_DEV = 8
CAP = 32
TILE = 64
WIN = TILE + 2 * CAP
MASKED = -1e30
UNROLL = 8
VMEM = pl.BlockSpec(memory_space=pltpu.VMEM)
SMEM = pl.BlockSpec(memory_space=pltpu.SMEM)
PARAMS = pltpu.CompilerParams(vmem_limit_bytes=48 * 1024 * 1024)


def lasts(micros):
    return pl.CostEstimate(flops=0, bytes_accessed=int(micros * 3.5e6), transcendentals=0)


NT = (((1,), (1,)), ((), ()))
TN = (((0,), (0,)), ((), ()))


def place_kernel(clusters, ids_ref, pos_ref, bias_ref):
    blocks, lanes = pos_ref.shape
    bf, f32 = jnp.bfloat16, jnp.float32
    cluster_ids = lax.broadcasted_iota(jnp.int32, (clusters, lanes), 0).astype(f32)
    slot_ids = lax.broadcasted_iota(jnp.int32, (CAP, lanes), 0).astype(f32)

    def tables(b):
        held = ids_ref[b].astype(f32)
        cluster = held[0:1] * lanes + held[1:2]
        return (
            jnp.where(cluster_ids == cluster, 1.0, 0.0),
            jnp.where(slot_ids == held[2:3], 1.0, 0.0),
        )

    def count(step, occupied):
        some = [tables(step * 4 + u) for u in range(4)]
        by_cluster = jnp.concatenate([t[0] for t in some], axis=1).astype(bf)
        by_slot = jnp.concatenate([t[1] for t in some], axis=1).astype(bf)
        return occupied + lax.dot_general(
            by_cluster, by_slot, NT, preferred_element_type=f32
        )

    occupied = lax.fori_loop(0, blocks // 4, count, jnp.zeros((clusters, CAP), f32))
    occupied_low = occupied.astype(bf)
    slot_from = lax.broadcasted_iota(jnp.int32, (CAP, CAP), 0)
    slot_to = lax.broadcasted_iota(jnp.int32, (CAP, CAP), 1)
    within = jnp.dot(
        occupied_low, jnp.where(slot_from < slot_to, 1.0, 0.0).astype(bf),
        preferred_element_type=f32,
    )
    size_col = jnp.sum(occupied, axis=1, keepdims=True)
    sizes = jnp.broadcast_to(size_col, (clusters, 128)).astype(bf)
    row_ids = lax.broadcasted_iota(jnp.int32, (clusters, clusters), 0)
    col_ids = lax.broadcasted_iota(jnp.int32, (clusters, clusters), 1)
    before = jnp.where(col_ids < row_ids, 1.0, 0.0).astype(bf)
    start = jnp.dot(before, sizes, preferred_element_type=f32)
    ends_col = start[:, 0:1] + size_col
    upto = jnp.where(row_ids <= col_ids, 1.0, 0.0).astype(bf)
    ends_row = lax.dot_general(
        sizes, upto, (((0,), (0,)), ((), ())), preferred_element_type=f32
    )[0:1]
    high = jnp.floor(start * (1.0 / 64.0))
    low = start - high * 64.0
    lookup = jnp.concatenate([within, high[:, :CAP], low[:, :CAP]], axis=1).astype(bf)

    def find(step, carry):
        some = [tables(step * 4 + u) for u in range(4)]
        found = [
            lax.dot_general(lookup, by_cluster.astype(bf), TN, preferred_element_type=f32)
            for by_cluster, _ in some
        ]
        for u in range(4):
            inner = jnp.sum(found[u][:CAP] * some[u][1], axis=0, keepdims=True)
            outer = found[u][CAP : CAP + 1] * 64.0 + found[u][2 * CAP : 2 * CAP + 1]
            pos_ref[pl.ds(step * 4 + u, 1), :] = (outer + inner).astype(jnp.int32)
        return carry

    lax.fori_loop(0, blocks // 4, find, 0)
    rows = blocks * lanes

    ones = jnp.ones((clusters, WIN), bf)
    few = jnp.ones((8, clusters), bf)

    def labels(step, carry):
        mines, others = [], []
        for u in range(UNROLL):
            t = step * UNROLL + u
            at = (t * TILE + lax.broadcasted_iota(jnp.int32, (TILE, clusters), 0)).astype(f32)
            ended = jnp.where(ends_row <= at, 1.0, 0.0).astype(bf)
            mines.append(jnp.dot(ended, ones, preferred_element_type=f32))
            wide = t * TILE - CAP + lax.broadcasted_iota(jnp.int32, (clusters, WIN), 1)
            ended = jnp.where(ends_col <= wide.astype(f32), 1.0, 0.0).astype(bf)
            other = jnp.dot(few, ended, preferred_element_type=f32)[0:1]
            spot = wide[0:1]
            others.append(jnp.where((spot >= 0) & (spot < rows), other, -1.0))
        for u in range(UNROLL):
            at = pl.ds(pl.multiple_of((step * UNROLL + u) * TILE, TILE), TILE)
            bias_ref[at, :] = jnp.where(mines[u] == others[u], 0.0, MASKED).astype(bf)
        return carry

    lax.fori_loop(0, rows // TILE // UNROLL, labels, 0)


def place(ids, clusters):
    blocks, _, lanes = ids.shape
    rows = blocks * lanes
    return pl.pallas_call(
        functools.partial(place_kernel, clusters),
        out_shape=(
            jax.ShapeDtypeStruct((blocks, lanes), jnp.int32),
            jax.ShapeDtypeStruct((rows, WIN), jnp.bfloat16),
        ),
        in_specs=[VMEM],
        out_specs=(VMEM, VMEM),
        compiler_params=PARAMS,
        cost_estimate=lasts(10),
        name="place",
    )(ids)


ROWS_AT_ONCE = 16


def move_in(pos_ref, block_of, load, wide, sorted_ref, offset, count):
    lanes = pos_ref.shape[1]

    def one(r, carry):
        b = block_of(r)
        wide[...] = load(r).astype(jnp.float32)
        for first in range(0, lanes, ROWS_AT_ONCE):
            held = [wide[pl.ds(first + row, 1), :] for row in range(ROWS_AT_ONCE)]
            for row in range(ROWS_AT_ONCE):
                sorted_ref[pl.ds(pos_ref[b, first + row] + offset, 1), :] = held[row]
        return carry

    lax.fori_loop(0, count, one, 0)


def move_out(pos_ref, block_of, sorted_ref, offset, wide, store, count):
    lanes = pos_ref.shape[1]

    def one(r, carry):
        b = block_of(r)
        for first in range(0, lanes, ROWS_AT_ONCE):
            held = [
                sorted_ref[pl.ds(pos_ref[b, first + row] + offset, 1), :]
                for row in range(ROWS_AT_ONCE)
            ]
            for row in range(ROWS_AT_ONCE):
                wide[pl.ds(first + row, 1), :] = held[row]
        store(r, wide[...])
        return carry

    lax.fori_loop(0, count, one, 0)


def tiles_of(step):
    bases = [pl.multiple_of((step * UNROLL + u) * TILE, TILE) for u in range(UNROLL)]
    tiles = [pl.ds(base, TILE) for base in bases]
    windows = [pl.ds(base, WIN) for base in bases]
    inner = [pl.ds(pl.multiple_of(base + CAP, CAP), TILE) for base in bases]
    return tiles, windows, inner


def scores_kernel(
    scale, pos_ref, rows_ref, bias_ref, query_ref, key_ref, probs_ref, wide, query, key
):
    bf, f32 = jnp.bfloat16, jnp.float32
    blocks, lanes = pos_ref.shape
    rows = blocks * lanes
    edge = jnp.zeros((CAP, wide.shape[1]), f32)
    for part, (ref, out) in enumerate(((query, query_ref), (key, key_ref))):
        ref[pl.ds(0, CAP), :] = edge
        ref[pl.ds(rows + CAP, CAP), :] = edge
        move_in(
            pos_ref, lambda b: b,
            lambda b, part=part: rows_ref[b, pl.ds(part * lanes, lanes), :], wide, ref, CAP, blocks,
        )
        out[...] = ref[...].astype(bf)

    def some(step, carry):
        tiles, windows, inner = tiles_of(step)
        qs = [query_ref[at, :] for at in inner]
        ks = [key_ref[at, :] for at in windows]
        biases = [bias_ref[at, :].astype(f32) for at in tiles]
        scores = [lax.dot_general(q, k, NT, preferred_element_type=f32) for q, k in zip(qs, ks)]
        scores = [s * scale + bias for s, bias in zip(scores, biases)]
        tops = [jnp.max(s, axis=1, keepdims=True) for s in scores]
        weights = [jnp.exp(s - top) for s, top in zip(scores, tops)]
        sums = [jnp.sum(w, axis=1, keepdims=True) for w in weights]
        for at, w, total in zip(tiles, weights, sums):
            probs_ref[at, :] = w / total
        return carry

    lax.fori_loop(0, rows // TILE // UNROLL, some, 0)


def attend_kernel(
    low, me_ref, pos_ref, rows_ref, probs_ref, *refs
):
    parts, (sorted_ref, value_ref, wide, value, att) = refs[:low], refs[low:]
    bf, f32 = jnp.bfloat16, jnp.float32
    blocks, lanes = pos_ref.shape
    rows = blocks * lanes
    high = blocks // low
    edge = jnp.zeros((CAP, wide.shape[1]), f32)
    value[pl.ds(0, CAP), :] = edge
    value[pl.ds(rows + CAP, CAP), :] = edge
    move_in(pos_ref, lambda b: b, lambda b: rows_ref[b], wide, value, CAP, blocks)
    value_ref[...] = value[...].astype(bf)

    def some(step, carry):
        tiles, windows, _ = tiles_of(step)
        vs = [value_ref[at, :] for at in windows]
        probs = [probs_ref[at, :].astype(bf) for at in tiles]
        attended = [jnp.dot(p, v, preferred_element_type=f32) for p, v in zip(probs, vs)]
        for at, one in zip(tiles, attended):
            att[at, :] = one
            sorted_ref[at, :] = one.astype(bf)
        return carry

    lax.fori_loop(0, rows // TILE // UNROLL, some, 0)

    for k in range(low):
        def put(r, block, k=k):
            parts[k][pl.ds(pl.multiple_of(r * lanes, lanes), lanes), :] = block.astype(bf)

        move_out(pos_ref, lambda r, k=k: r * low + (me_ref[0] ^ k), att, 0, wide, put, high)


def value_kernel(
    low, me_ref, pos_ref, probs_ref, *refs
):
    parts, (out_ref, sorted_ref, wide, grad, grad_value) = refs[:low], refs[low:]
    bf, f32 = jnp.bfloat16, jnp.float32
    blocks, lanes = pos_ref.shape
    rows = blocks * lanes
    high = blocks // low
    for k in range(low):
        def block_of(r, k=k):
            return r * low + (me_ref[0] ^ k)

        def load(r, k=k):
            return parts[k][pl.ds(pl.multiple_of(r * lanes, lanes), lanes), :]

        move_in(pos_ref, block_of, load, wide, grad, 0, high)
    sorted_ref[...] = grad[...].astype(bf)
    grad_value[...] = jnp.zeros_like(grad_value)

    def some(step, carry):
        tiles, windows, _ = tiles_of(step)
        gs = [sorted_ref[at, :] for at in tiles]
        probs = [probs_ref[at, :].astype(bf) for at in tiles]
        more = [lax.dot_general(p, g, TN, preferred_element_type=f32) for p, g in zip(probs, gs)]
        for at, one in zip(windows, more):
            grad_value[at, :] += one
        return carry

    lax.fori_loop(0, rows // TILE // UNROLL, some, 0)

    def put(b, block):
        out_ref[b] = block.astype(bf)

    move_out(pos_ref, lambda b: b, grad_value, CAP, wide, put, blocks)


def rest_kernel(
    scale, pos_ref, grad_ref, sorted_ref, query_ref, key_ref, value_ref, probs_ref,
    out_ref, wide, grad_query, grad_key,
):
    bf, f32 = jnp.bfloat16, jnp.float32
    blocks, lanes = pos_ref.shape
    rows = blocks * lanes
    grad_key[...] = jnp.zeros_like(grad_key)

    def some(step, carry):
        tiles, windows, inner = tiles_of(step)
        gs = [grad_ref[at, :] for at in tiles]
        qs = [query_ref[at, :] for at in inner]
        ks = [key_ref[at, :] for at in windows]
        vs = [value_ref[at, :] for at in windows]
        probs = [probs_ref[at, :] for at in tiles]
        attended = [sorted_ref[at, :].astype(f32) for at in tiles]
        grad_probs = [lax.dot_general(g, v, NT, preferred_element_type=f32) for g, v in zip(gs, vs)]
        deltas = [
            jnp.sum(g.astype(f32) * one, axis=1, keepdims=True) for g, one in zip(gs, attended)
        ]
        grad_scores = [
            (p * (gp - delta)).astype(bf) for p, gp, delta in zip(probs, grad_probs, deltas)
        ]
        grad_queries = [jnp.dot(d, k, preferred_element_type=f32) for d, k in zip(grad_scores, ks)]
        more_keys = [
            lax.dot_general(d, q, TN, preferred_element_type=f32) for d, q in zip(grad_scores, qs)
        ]
        for at, one in zip(tiles, grad_queries):
            grad_query[at, :] = one
        for at, one in zip(windows, more_keys):
            grad_key[at, :] += one
        return carry

    lax.fori_loop(0, rows // TILE // UNROLL, some, 0)

    def put(part):
        def store(b, block):
            out_ref[b, pl.ds(part * lanes, lanes), :] = (block * scale).astype(bf)
        return store

    move_out(pos_ref, lambda b: b, grad_query, 0, wide, put(0), blocks)
    move_out(pos_ref, lambda b: b, grad_key, CAP, wide, put(1), blocks)


def project_back_kernel(low, rows_ref, *refs):
    bf, f32 = jnp.bfloat16, jnp.float32
    weights, outs = refs[:low], refs[low:]
    for k in range(0, low, 2):
        weight = jnp.concatenate([weights[k][...], weights[k + 1][...]], axis=1)
        both = jnp.dot(rows_ref[...], weight, preferred_element_type=f32).astype(bf)
        size = both.shape[1] // 2
        outs[k][...] = both[:, :size]
        outs[k + 1][...] = both[:, size:]


def project_kernel(low, chunk, *refs):
    bf, f32 = jnp.bfloat16, jnp.float32
    weights, parts, out_ref = refs[:low], refs[low:-1], refs[-1]
    rows = jnp.concatenate([ref[...] for ref in parts], axis=1)

    def one(c, carry):
        at = pl.ds(pl.multiple_of(c * chunk, chunk), chunk)
        weight = jnp.concatenate([ref[at, :] for ref in weights], axis=1)
        out_ref[:, at] = lax.dot_general(rows, weight, NT, preferred_element_type=f32).astype(bf)
        return carry

    lax.fori_loop(0, out_ref.shape[1] // chunk, one, 0)


def place_in_plane(low):
    index = lax.axis_index("seq")
    return jnp.stack([index % low, index // low]).astype(jnp.int32)


def project_back(weights, rows):
    low = len(weights)
    size = weights[0].shape[1]
    return pl.pallas_call(
        functools.partial(project_back_kernel, low),
        out_shape=(jax.ShapeDtypeStruct((rows.shape[0], size), jnp.bfloat16),) * low,
        in_specs=[VMEM] * (1 + low),
        out_specs=(VMEM,) * low,
        compiler_params=PARAMS,
        cost_estimate=lasts(8),
        name="project_back",
    )(rows, *weights)


def project(weights, parts):
    low = len(weights)
    columns = weights[0].shape[0]
    return pl.pallas_call(
        functools.partial(project_kernel, low, math.gcd(columns, 512)),
        out_shape=jax.ShapeDtypeStruct((parts[0].shape[0], columns), jnp.bfloat16),
        in_specs=[VMEM] * (2 * low),
        out_specs=VMEM,
        compiler_params=PARAMS,
        cost_estimate=lasts(6),
        name="project",
    )(*weights, *parts)


def head_kernels(pos, size, low):
    blocks, lanes = pos.shape
    rows = blocks * lanes
    bf, f32 = jnp.bfloat16, jnp.float32
    scale = 1.0 / math.sqrt(size)
    plain, padded = (rows, size), (rows + 2 * CAP, size)
    me = place_in_plane(low)

    def call(kernel, operands, outs, scratch, micros, name):
        return pl.pallas_call(
            kernel,
            out_shape=tuple(jax.ShapeDtypeStruct(shape, kind) for shape, kind in outs),
            in_specs=[SMEM if x.dtype == jnp.int32 else VMEM for x in operands],
            out_specs=(VMEM,) * len(outs),
            scratch_shapes=[pltpu.VMEM(shape, f32) for shape in ((lanes, size), *scratch)],
            compiler_params=PARAMS,
            cost_estimate=lasts(micros),
            name=name,
        )(*operands)

    def scores(query_key, bias):
        return call(
            functools.partial(scores_kernel, scale), (pos, query_key, bias),
            ((padded, bf), (padded, bf), ((rows, WIN), f32)), (padded, padded), 12, "scores",
        )

    def attend(value, probs):
        return call(
            functools.partial(attend_kernel, low), (me, pos, value, probs),
            (((blocks // low * lanes, size), bf),) * low + ((plain, bf), (padded, bf)),
            (padded, plain), 12, "attend",
        )

    def grad_value(grads, probs):
        return call(
            functools.partial(value_kernel, low), (me, pos, probs, *grads),
            (((blocks, lanes, size), bf), (plain, bf)), (plain, padded), 12, "grad_value",
        )

    def rest(grad, attended, query, key, value, probs):
        return call(
            functools.partial(rest_kernel, scale),
            (pos, grad, attended, query, key, value, probs),
            (((blocks, 2 * lanes, size), bf),), (plain, padded), 16, "rest",
        )[0]

    return scores, attend, grad_value, rest


def pack_kernel(*refs):
    out_ref = refs[-1]
    size = out_ref.shape[2]
    first = 0
    for ref in refs[:-1]:
        rows = ref.shape[-2]
        for h in range(out_ref.shape[0]):
            if len(ref.shape) == 3:
                out_ref[h, pl.ds(first, rows), :] = ref[h]
            else:
                out_ref[h, pl.ds(first, rows), :] = ref[:, pl.ds(h * size, size)]
        first += rows


def pack(arrays, heads):
    rows = sum(array.shape[-2] for array in arrays)
    size = arrays[0].shape[1] // heads
    step = math.gcd(heads, 8)

    def block(array):
        if array.ndim == 3:
            return pl.BlockSpec((step, *array.shape[1:]), lambda i: (i, 0, 0))
        return pl.BlockSpec((array.shape[0], step * size), lambda i: (0, i))

    return pl.pallas_call(
        pack_kernel,
        grid=(heads // step,),
        out_shape=jax.ShapeDtypeStruct((heads, rows, size), arrays[0].dtype),
        in_specs=[block(array) for array in arrays],
        out_specs=pl.BlockSpec((step, rows, size), lambda i: (i, 0, 0)),
        compiler_params=PARAMS,
        cost_estimate=lasts(3),
        name="pack",
    )(*arrays)


def unpack_kernel(in_ref, *refs):
    heads, rows, size = in_ref.shape
    rows = rows // len(refs)
    for part, ref in enumerate(refs):
        for h in range(heads):
            ref[:, pl.ds(h * size, size)] = in_ref[h, pl.ds(part * rows, rows), :]


def unpack(packed, parts):
    heads, rows, size = packed.shape
    rows = rows // parts
    step = math.gcd(heads, 8)
    return pl.pallas_call(
        unpack_kernel,
        grid=(heads // step,),
        out_shape=(jax.ShapeDtypeStruct((rows, heads * size), packed.dtype),) * parts,
        in_specs=[pl.BlockSpec((step, parts * rows, size), lambda i: (i, 0, 0))],
        out_specs=(pl.BlockSpec((rows, step * size), lambda i: (0, i)),) * parts,
        compiler_params=PARAMS,
        cost_estimate=lasts(3),
        name="unpack",
    )(packed)


def by_clusters(query_rows, key_rows, value_rows, cluster_id, slot_index, out_weight, grad_out):
    rows_dev = query_rows.shape[0]
    heads_dev = cluster_id.shape[0]
    head_size = query_rows.shape[1] // heads_dev
    owners = lax.axis_size("seq")
    send_most = 2 * rows_dev // owners
    buffer_rows = owners * send_most
    room = CLU_DEV * CAP
    score_scale = 1.0 / math.sqrt(head_size)
    masked_score = -1e30
    owner = cluster_id // CLU_DEV
    owner_onehot = (owner[:, :, None] == jnp.arange(owners, dtype=jnp.int32)[None, None, :]).astype(
        jnp.bfloat16
    )
    row_ids = jnp.arange(rows_dev, dtype=jnp.int32)
    lower = (row_ids[:, None] > row_ids[None, :]).astype(jnp.bfloat16)
    earlier = jnp.einsum("ij,hjo->hio", lower, owner_onehot, preferred_element_type=jnp.float32)
    rank = jnp.sum(earlier * owner_onehot.astype(jnp.float32), axis=2).astype(jnp.int32)
    place = owner * send_most + rank
    target = cluster_id % CLU_DEV * CAP + slot_index
    buffer_ids = jnp.arange(buffer_rows, dtype=jnp.int32)
    send_table = (place[:, None, :] == buffer_ids[None, :, None]).astype(jnp.bfloat16)

    def to_buffer(rows):
        split = rows.reshape(rows_dev, heads_dev, head_size)
        filled = jnp.einsum(
            "hbi,ihd->bhd", send_table, split, preferred_element_type=jnp.float32
        ).astype(rows.dtype)
        return filled.reshape(buffer_rows, heads_dev * head_size)

    def from_buffer(buffer):
        split = buffer.reshape(buffer_rows, heads_dev, head_size)
        picked = jnp.einsum(
            "hbi,bhd->ihd", send_table, split, preferred_element_type=jnp.float32
        ).astype(buffer.dtype)
        return picked.reshape(rows_dev, heads_dev * head_size)

    target_rows = (
        jnp.einsum(
            "hbi,hi->bh", send_table.astype(jnp.float32), (target - room).astype(jnp.float32)
        ).astype(jnp.int32)
        + room
    )
    arrived = lax.all_to_all(target_rows, "seq", split_axis=0, concat_axis=0, tiled=True)
    routed_query, routed_key, routed_value = (
        lax.all_to_all(to_buffer(query_rows), "seq", split_axis=0, concat_axis=0, tiled=True),
        lax.all_to_all(to_buffer(key_rows), "seq", split_axis=0, concat_axis=0, tiled=True),
        lax.all_to_all(to_buffer(value_rows), "seq", split_axis=0, concat_axis=0, tiled=True),
    )
    room_ids = jnp.arange(room, dtype=jnp.int32)
    cell_table = (arrived.T[:, None, :] == room_ids[None, :, None]).astype(jnp.bfloat16)

    def to_cells(buffer):
        split = buffer.reshape(buffer_rows, heads_dev, head_size)
        cells = jnp.einsum(
            "hrb,bhd->hrd", cell_table, split, preferred_element_type=jnp.float32
        ).astype(buffer.dtype)
        return cells.reshape(heads_dev, CLU_DEV, CAP, head_size)

    def to_returns(cells):
        flat = cells.reshape(heads_dev, room, head_size)
        picked = jnp.einsum(
            "hrb,hrd->bhd", cell_table, flat, preferred_element_type=jnp.float32
        ).astype(cells.dtype)
        return picked.reshape(buffer_rows, heads_dev * head_size)

    live = jnp.sum(cell_table.astype(jnp.float32), axis=2).reshape(heads_dev, CLU_DEV, CAP)
    query_cells = to_cells(routed_query)
    key_cells = to_cells(routed_key)
    value_cells = to_cells(routed_value)
    scores = (
        jnp.einsum("hcqd,hckd->hcqk", query_cells, key_cells, preferred_element_type=jnp.float32)
        * score_scale
    )
    scores = jnp.where(live[:, :, None, :] > 0.5, scores, masked_score)
    top = jnp.max(scores, axis=-1, keepdims=True)
    weights = jnp.exp(scores - top)
    probs = weights / jnp.sum(weights, axis=-1, keepdims=True)
    probs_low = probs.astype(jnp.bfloat16)
    attended_cells = jnp.einsum(
        "hcqk,hckd->hcqd", probs_low, value_cells, preferred_element_type=jnp.float32
    ).astype(jnp.bfloat16)
    returned = lax.all_to_all(
        to_returns(attended_cells), "seq", split_axis=0, concat_axis=0, tiled=True
    )
    attended = from_buffer(returned)
    full_weight = lax.all_gather(out_weight, "seq", axis=1, tiled=True)
    rows = attended
    mixed = lax.psum_scatter(
        jnp.dot(rows, full_weight, preferred_element_type=jnp.float32).astype(jnp.bfloat16),
        "tensor",
        scatter_dimension=0,
        tiled=True,
    )
    grad_attended = lax.dot_general(
        lax.all_gather(grad_out, "tensor", axis=0, tiled=True),
        full_weight,
        (((1,), (1,)), ((), ())),
        preferred_element_type=jnp.float32,
    )
    grad_low = grad_attended.astype(jnp.bfloat16)
    routed_grad = lax.all_to_all(
        to_buffer(grad_low), "seq", split_axis=0, concat_axis=0, tiled=True
    )
    grad_cells = to_cells(routed_grad)
    backward_low = probs.astype(jnp.bfloat16)
    delta = jnp.einsum(
        "hcqd,hcqd->hcq", grad_cells, attended_cells, preferred_element_type=jnp.float32
    )
    grad_value = jnp.einsum(
        "hcqk,hcqd->hckd", backward_low, grad_cells, preferred_element_type=jnp.float32
    ).astype(jnp.bfloat16)
    grad_probs = jnp.einsum(
        "hcqd,hckd->hcqk", grad_cells, value_cells, preferred_element_type=jnp.float32
    )
    grad_scores = (probs * (grad_probs - delta[..., None])).astype(jnp.bfloat16)
    grad_query = (
        jnp.einsum("hcqk,hckd->hcqd", grad_scores, key_cells, preferred_element_type=jnp.float32)
        * score_scale
    ).astype(jnp.bfloat16)
    grad_key = (
        jnp.einsum("hcqk,hcqd->hckd", grad_scores, query_cells, preferred_element_type=jnp.float32)
        * score_scale
    ).astype(jnp.bfloat16)
    back_query, back_key, back_value = (
        lax.all_to_all(to_returns(grad_query), "seq", split_axis=0, concat_axis=0, tiled=True),
        lax.all_to_all(to_returns(grad_key), "seq", split_axis=0, concat_axis=0, tiled=True),
        lax.all_to_all(to_returns(grad_value), "seq", split_axis=0, concat_axis=0, tiled=True),
    )
    return (mixed, from_buffer(back_query), from_buffer(back_key), from_buffer(back_value))


def by_heads(query_rows, key_rows, value_rows, cluster_id, slot_index, out_weight, grad_out):
    rows_dev, width = query_rows.shape
    heads_dev = cluster_id.shape[0]
    head_size = width // heads_dev
    owners = lax.axis_size("seq")
    columns_dev = out_weight.shape[1]
    high, low = split(owners)
    stacks = [[h * low + p for h in range(high)] for p in range(low)]
    bf = jnp.bfloat16
    together = lax.optimization_barrier

    def exchange(rows):
        return lax.all_to_all(rows, "seq", split_axis=0, concat_axis=0, tiled=True)

    def swap(blocks, step=1):
        pairs = [[(i, i ^ (k * step)) for i in range(owners)] for k in range(len(blocks))]
        return [blocks[0]] + [
            lax.ppermute(blocks[k], "seq", pairs[k]) for k in range(1, len(blocks))
        ]

    def gather_plane(block):
        near = swap([block] * (low // 2), 2)
        other = [(i, i ^ 1) for i in range(owners)]
        return [x for one in near for x in (one, lax.ppermute(one, "seq", other))]

    weight_rows = out_weight.T.reshape(columns_dev, heads_dev, head_size).transpose(1, 0, 2)
    ids = jnp.stack([cluster_id // rows_dev, cluster_id % rows_dev, slot_index], axis=1)
    ids = jnp.pad(ids, ((0, 0), (0, 13), (0, 0))).astype(bf)
    first = exchange(jnp.concatenate([weight_rows, ids], axis=1))
    grad_out_stack = lax.all_gather(grad_out, "seq", axis=0, tiled=True, axis_index_groups=stacks)
    packed = pack((query_rows, key_rows), heads_dev)
    packed_value = pack((value_rows,), heads_dev)
    packed, packed_value, first = together((packed, packed_value, first))
    arrived = exchange(packed)
    weights = gather_plane(first[:, :columns_dev].reshape(owners * columns_dev, head_size))
    pos, bias = place(first[:, columns_dev:], CLU_DEV * owners)
    packed_value, arrived, pos, bias, weights = together(
        (packed_value, arrived, pos, bias, weights)
    )
    value = exchange(packed_value)
    grad_heads = swap(project_back(weights, grad_out_stack))
    scores, attend, grad_of_value, rest = head_kernels(pos, head_size, low)
    query, key, probs = scores(arrived, bias)
    grad_value, grad_sorted = grad_of_value(grad_heads, probs)
    value, grad_value = together((value, grad_value))
    *attended, att_sorted, value_sorted = attend(value, probs)
    back_value = exchange(grad_value)
    attended = swap(attended)
    grads = rest(grad_sorted, att_sorted, query, key, value_sorted, probs)
    grads, attended = together((grads, attended))
    grads, back_value = together((grads, back_value))
    back = exchange(grads)
    partial = project(weights, attended)
    mixed = lax.psum_scatter(
        partial, "seq", scatter_dimension=0, tiled=True, axis_index_groups=stacks
    )
    return (mixed, *unpack(back, 2), *unpack(back_value, 1))


def split(owners):
    high = 1
    while 4 * high * high <= owners:
        high *= 2
    return high, owners // high


def solution(mesh):
    def shards(*args):
        heads_dev = args[3].shape[0]
        owners = lax.axis_size("seq")
        if heads_dev == owners and owners & (owners - 1) == 0 and lax.axis_size("tensor") == 1:
            return by_heads(*args)
        return by_clusters(*args)

    return jax.shard_map(
        shards,
        mesh=mesh,
        in_specs=(
            P("seq", "tensor"),
            P("seq", "tensor"),
            P("seq", "tensor"),
            P("tensor", "seq"),
            P("tensor", "seq"),
            P("tensor", "seq"),
            P(("seq", "tensor"), None),
        ),
        out_specs=(
            P(("seq", "tensor"), None),
            P("seq", "tensor"),
            P("seq", "tensor"),
            P("seq", "tensor"),
        ),
        check_vma=False,
    )
```

```python
import functools
import math

import jax
import jax.numpy as jnp
from jax import lax
from jax.experimental import pallas as pl
from jax.experimental.pallas import tpu as pltpu
from jax.sharding import PartitionSpec as P

CLU_DEV = 8
CAP = 32
TILE = 64
WIN = TILE + 2 * CAP
MASKED = -1e30
UNROLL = 8
VMEM = pl.BlockSpec(memory_space=pltpu.VMEM)
SMEM = pl.BlockSpec(memory_space=pltpu.SMEM)
HBM = pl.BlockSpec(memory_space=pltpu.HBM)
PARAMS = pltpu.CompilerParams(vmem_limit_bytes=61 * 1024 * 1024)
SMALL = pltpu.CompilerParams(vmem_limit_bytes=16 * 1024 * 1024)


def lasts(micros):
    return pl.CostEstimate(flops=0, bytes_accessed=int(micros * 3.5e6), transcendentals=0)


NT = (((1,), (1,)), ((), ()))
TN = (((0,), (0,)), ((), ()))


def run(kernel, operands, outs, scratch, micros, name, late=0):
    where = [SMEM if x.dtype == jnp.int32 else HBM for x in operands]
    held = [pltpu.VMEM(x.shape, x.dtype) for x, spec in zip(operands, where) if spec is HBM]

    def body(*refs):
        given, rest = refs[: len(operands)], refs[len(operands) :]
        slots, sems, rest = rest[-1 - len(held) : -1], rest[-1], rest[: -1 - len(held)]
        copies, arrays = [], []
        for ref, spec in zip(given, where):
            if spec is HBM:
                slot = slots[len(copies)]
                copies.append(pltpu.make_async_copy(ref, slot, sems.at[len(copies)]))
                ref = slot
            arrays.append(ref)
        for copy in copies:
            copy.start()
        now = len(copies) - late
        for copy in copies[:now]:
            copy.wait()
        if late:
            def arrive():
                for copy in copies[now:]:
                    copy.wait()

            kernel(arrive, *arrays, *rest)
        else:
            kernel(*arrays, *rest)

    return pl.pallas_call(
        body,
        out_shape=tuple(jax.ShapeDtypeStruct(shape, kind) for shape, kind in outs),
        in_specs=where,
        out_specs=(VMEM,) * len(outs),
        scratch_shapes=[
            *(pltpu.VMEM(shape, kind) for shape, kind in scratch),
            *held,
            pltpu.SemaphoreType.DMA((len(held),)),
        ],
        compiler_params=PARAMS,
        cost_estimate=lasts(micros),
        name=name,
    )(*operands)


def place_kernel(clusters, ids_ref, pos_ref, bias_ref):
    blocks, lanes = pos_ref.shape
    bf, f32 = jnp.bfloat16, jnp.float32
    cluster_ids = lax.broadcasted_iota(jnp.int32, (clusters, lanes), 0).astype(f32)
    slot_ids = lax.broadcasted_iota(jnp.int32, (CAP, lanes), 0).astype(f32)

    def tables(b):
        held = ids_ref[b].astype(f32)
        cluster = held[0:1] * lanes + held[1:2]
        return (
            jnp.where(cluster_ids == cluster, 1.0, 0.0),
            jnp.where(slot_ids == held[2:3], 1.0, 0.0),
        )

    def count(step, occupied):
        some = [tables(step * 4 + u) for u in range(4)]
        by_cluster = jnp.concatenate([t[0] for t in some], axis=1).astype(bf)
        by_slot = jnp.concatenate([t[1] for t in some], axis=1).astype(bf)
        return occupied + lax.dot_general(
            by_cluster, by_slot, NT, preferred_element_type=f32
        )

    occupied = lax.fori_loop(0, blocks // 4, count, jnp.zeros((clusters, CAP), f32))
    occupied_low = occupied.astype(bf)
    slot_from = lax.broadcasted_iota(jnp.int32, (CAP, CAP), 0)
    slot_to = lax.broadcasted_iota(jnp.int32, (CAP, CAP), 1)
    within = jnp.dot(
        occupied_low, jnp.where(slot_from < slot_to, 1.0, 0.0).astype(bf),
        preferred_element_type=f32,
    )
    size_col = jnp.sum(occupied, axis=1, keepdims=True)
    sizes = jnp.broadcast_to(size_col, (clusters, 128)).astype(bf)
    row_ids = lax.broadcasted_iota(jnp.int32, (clusters, clusters), 0)
    col_ids = lax.broadcasted_iota(jnp.int32, (clusters, clusters), 1)
    before = jnp.where(col_ids < row_ids, 1.0, 0.0).astype(bf)
    start = jnp.dot(before, sizes, preferred_element_type=f32)
    ends_col = start[:, 0:1] + size_col
    upto = jnp.where(row_ids <= col_ids, 1.0, 0.0).astype(bf)
    ends_row = lax.dot_general(
        sizes, upto, (((0,), (0,)), ((), ())), preferred_element_type=f32
    )[0:1]
    high = jnp.floor(start * (1.0 / 64.0))
    low = start - high * 64.0
    lookup = jnp.concatenate([within, high[:, :CAP], low[:, :CAP]], axis=1).astype(bf)

    def find(step, carry):
        some = [tables(step * 4 + u) for u in range(4)]
        found = [
            lax.dot_general(lookup, by_cluster.astype(bf), TN, preferred_element_type=f32)
            for by_cluster, _ in some
        ]
        for u in range(4):
            inner = jnp.sum(found[u][:CAP] * some[u][1], axis=0, keepdims=True)
            outer = found[u][CAP : CAP + 1] * 64.0 + found[u][2 * CAP : 2 * CAP + 1]
            pos_ref[pl.ds(step * 4 + u, 1), :] = (outer + inner).astype(jnp.int32) + CAP
        return carry

    lax.fori_loop(0, blocks // 4, find, 0)
    rows = blocks * lanes

    ones = jnp.ones((clusters, WIN), bf)
    few = jnp.ones((8, clusters), bf)

    def labels(step, carry):
        mines, others = [], []
        for u in range(UNROLL):
            t = step * UNROLL + u
            at = (t * TILE + lax.broadcasted_iota(jnp.int32, (TILE, clusters), 0)).astype(f32)
            ended = jnp.where(ends_row <= at, 1.0, 0.0).astype(bf)
            mines.append(jnp.dot(ended, ones, preferred_element_type=f32))
            wide = t * TILE - CAP + lax.broadcasted_iota(jnp.int32, (clusters, WIN), 1)
            ended = jnp.where(ends_col <= wide.astype(f32), 1.0, 0.0).astype(bf)
            other = jnp.dot(few, ended, preferred_element_type=f32)[0:1]
            spot = wide[0:1]
            others.append(jnp.where((spot >= 0) & (spot < rows), other, -1.0))
        for u in range(UNROLL):
            at = pl.ds(pl.multiple_of((step * UNROLL + u) * TILE, TILE), TILE)
            bias_ref[at, :] = jnp.where(mines[u] == others[u], 0.0, MASKED).astype(bf)
        return carry

    lax.fori_loop(0, rows // TILE // UNROLL, labels, 0)


def place(ids, clusters):
    blocks, _, lanes = ids.shape
    return run(
        functools.partial(place_kernel, clusters), (ids,),
        (((blocks, lanes), jnp.int32), ((blocks * lanes, WIN), jnp.bfloat16)), (), 8, "place",
    )


ROWS_AT_ONCE = 16


def move_in(pos_ref, block_of, loads, wides, sorted_refs, count):
    lanes = pos_ref.shape[1]

    def one(r, carry):
        b = block_of(r)
        for load, wide in zip(loads, wides):
            wide[...] = load(r).astype(jnp.float32)
        for first in range(0, lanes, ROWS_AT_ONCE):
            rows = range(first, first + ROWS_AT_ONCE)
            places = [pl.ds(pos_ref[b, row], 1) for row in rows]
            held = [[wide[pl.ds(row, 1), :] for row in rows] for wide in wides]
            for i, at in enumerate(places):
                for ref, some in zip(sorted_refs, held):
                    ref[at, :] = some[i]
        return carry

    lax.fori_loop(0, count, one, 0)


def move_out(pos_ref, block_of, sorted_refs, wides, stores, count):
    lanes = pos_ref.shape[1]

    def one(r, carry):
        b = block_of(r)
        for first in range(0, lanes, ROWS_AT_ONCE):
            rows = range(first, first + ROWS_AT_ONCE)
            places = [pl.ds(pos_ref[b, row], 1) for row in rows]
            held = [[ref[at, :] for at in places] for ref in sorted_refs]
            for i, row in enumerate(rows):
                for wide, some in zip(wides, held):
                    wide[pl.ds(row, 1), :] = some[i]
        for store, wide in zip(stores, wides):
            store(r, wide[...])
        return carry

    lax.fori_loop(0, count, one, 0)


def tiles_of(step):
    bases = [pl.multiple_of((step * UNROLL + u) * TILE, TILE) for u in range(UNROLL)]
    tiles = [pl.ds(base, TILE) for base in bases]
    windows = [pl.ds(base, WIN) for base in bases]
    inner = [pl.ds(pl.multiple_of(base + CAP, CAP), TILE) for base in bases]
    return tiles, windows, inner


def scores_kernel(
    scale, arrive, pos_ref, rows_ref, bias_ref, query_ref, key_ref, probs_ref,
    wide, query, key, more,
):
    bf, f32 = jnp.bfloat16, jnp.float32
    blocks, lanes = pos_ref.shape
    rows = blocks * lanes
    edge = jnp.zeros((CAP, wide.shape[1]), f32)
    for ref in (query, key):
        ref[pl.ds(0, CAP), :] = edge
        ref[pl.ds(rows + CAP, CAP), :] = edge
    move_in(
        pos_ref, lambda b: b,
        [lambda b, part=part: rows_ref[b, pl.ds(part * lanes, lanes), :] for part in range(2)],
        [wide, more], [query, key], blocks,
    )
    query_ref[...] = query[...].astype(bf)
    key_ref[...] = key[...].astype(bf)
    arrive()

    def some(step, carry):
        tiles, windows, inner = tiles_of(step)
        qs = [query_ref[at, :] for at in inner]
        ks = [key_ref[at, :] for at in windows]
        biases = [bias_ref[at, :].astype(f32) for at in tiles]
        scores = [lax.dot_general(q, k, NT, preferred_element_type=f32) for q, k in zip(qs, ks)]
        scores = [s * scale + bias for s, bias in zip(scores, biases)]
        tops = [jnp.max(s, axis=1, keepdims=True) for s in scores]
        weights = [jnp.exp(s - top) for s, top in zip(scores, tops)]
        sums = [jnp.sum(w, axis=1, keepdims=True) for w in weights]
        for at, w, total in zip(tiles, weights, sums):
            probs_ref[at, :] = (w / total).astype(bf)
        return carry

    lax.fori_loop(0, rows // TILE // UNROLL, some, 0)


def attend_kernel(
    low, arrive, me_ref, pos_ref, rows_ref, probs_ref, *refs
):
    parts, (sorted_ref, value_ref, wide, value, att) = refs[:low], refs[low:]
    bf, f32 = jnp.bfloat16, jnp.float32
    blocks, lanes = pos_ref.shape
    rows = blocks * lanes
    high = blocks // low
    edge = jnp.zeros((CAP, wide.shape[1]), f32)
    value[pl.ds(0, CAP), :] = edge
    value[pl.ds(rows + CAP, CAP), :] = edge
    move_in(pos_ref, lambda b: b, [lambda b: rows_ref[b]], [wide], [value], blocks)
    value_ref[...] = value[...].astype(bf)
    arrive()

    def some(step, carry):
        tiles, windows, inner = tiles_of(step)
        vs = [value_ref[at, :] for at in windows]
        probs = [probs_ref[at, :] for at in tiles]
        attended = [jnp.dot(p, v, preferred_element_type=f32) for p, v in zip(probs, vs)]
        for at, to, one in zip(tiles, inner, attended):
            att[to, :] = one
            sorted_ref[at, :] = one.astype(bf)
        return carry

    lax.fori_loop(0, rows // TILE // UNROLL, some, 0)

    for k in range(low):
        def put(r, block, k=k):
            parts[k][pl.ds(pl.multiple_of(r * lanes, lanes), lanes), :] = block.astype(bf)

        move_out(
            pos_ref, lambda r, k=k: (me_ref[1] ^ r) * low + (me_ref[0] ^ k),
            [att], [wide], [put], high,
        )


def value_kernel(
    low, arrive, me_ref, pos_ref, *refs
):
    parts, (probs_ref, out_ref, sorted_ref, wide, grad, grad_value) = refs[:low], refs[low:]
    bf, f32 = jnp.bfloat16, jnp.float32
    blocks, lanes = pos_ref.shape
    rows = blocks * lanes
    high = blocks // low
    for k in range(low):
        def block_of(r, k=k):
            return (me_ref[1] ^ r) * low + (me_ref[0] ^ k)

        def load(r, k=k):
            return parts[k][pl.ds(pl.multiple_of(r * lanes, lanes), lanes), :]

        move_in(pos_ref, block_of, [load], [wide], [grad], high)
    sorted_ref[...] = grad[pl.ds(CAP, rows), :].astype(bf)
    grad_value[...] = jnp.zeros_like(grad_value)
    arrive()

    def some(step, carry):
        tiles, windows, _ = tiles_of(step)
        gs = [sorted_ref[at, :] for at in tiles]
        probs = [probs_ref[at, :] for at in tiles]
        more = [lax.dot_general(p, g, TN, preferred_element_type=f32) for p, g in zip(probs, gs)]
        for at, one in zip(windows, more):
            grad_value[at, :] += one
        return carry

    lax.fori_loop(0, rows // TILE // UNROLL, some, 0)

    def put(b, block):
        out_ref[b] = block.astype(bf)

    move_out(pos_ref, lambda b: b, [grad_value], [wide], [put], blocks)


def rest_kernel(
    scale, pos_ref, grad_ref, sorted_ref, query_ref, key_ref, value_ref, probs_ref,
    out_ref, wide, grad_query, grad_key, more,
):
    bf, f32 = jnp.bfloat16, jnp.float32
    blocks, lanes = pos_ref.shape
    rows = blocks * lanes
    grad_key[...] = jnp.zeros_like(grad_key)

    def some(step, carry):
        tiles, windows, inner = tiles_of(step)
        gs = [grad_ref[at, :] for at in tiles]
        qs = [query_ref[at, :] for at in inner]
        ks = [key_ref[at, :] for at in windows]
        vs = [value_ref[at, :] for at in windows]
        probs = [probs_ref[at, :] for at in tiles]
        attended = [sorted_ref[at, :].astype(f32) for at in tiles]
        grad_probs = [lax.dot_general(g, v, NT, preferred_element_type=f32) for g, v in zip(gs, vs)]
        deltas = [
            jnp.sum(g.astype(f32) * one, axis=1, keepdims=True) for g, one in zip(gs, attended)
        ]
        grad_scores = [
            (p.astype(f32) * (gp - delta)).astype(bf)
            for p, gp, delta in zip(probs, grad_probs, deltas)
        ]
        grad_queries = [jnp.dot(d, k, preferred_element_type=f32) for d, k in zip(grad_scores, ks)]
        more_keys = [
            lax.dot_general(d, q, TN, preferred_element_type=f32) for d, q in zip(grad_scores, qs)
        ]
        for at, one in zip(inner, grad_queries):
            grad_query[at, :] = one
        for at, one in zip(windows, more_keys):
            grad_key[at, :] += one
        return carry

    lax.fori_loop(0, rows // TILE // UNROLL, some, 0)

    def put(part):
        def store(b, block):
            out_ref[b, pl.ds(part * lanes, lanes), :] = (block * scale).astype(bf)
        return store

    move_out(
        pos_ref, lambda b: b, [grad_query, grad_key], [wide, more], [put(0), put(1)], blocks
    )


def project_back_kernel(low, *refs):
    bf, f32 = jnp.bfloat16, jnp.float32
    weights, blocks, outs, rows_ref = refs[:low], refs[low : -1 - low], refs[-1 - low : -1], refs[-1]
    rows = blocks[0].shape[0]
    for r, block in enumerate(blocks):
        rows_ref[pl.ds(r * rows, rows), :] = block[...]
    for k in range(0, low, 2):
        weight = jnp.concatenate([weights[k][...], weights[k + 1][...]], axis=1)
        both = jnp.dot(rows_ref[...], weight, preferred_element_type=f32).astype(bf)
        size = both.shape[1] // 2
        outs[k][...] = both[:, :size]
        outs[k + 1][...] = both[:, size:]


def project_kernel(low, chunk, *refs):
    bf, f32 = jnp.bfloat16, jnp.float32
    weights, parts, outs = refs[:low], refs[low : 2 * low], refs[2 * low :]
    rows = jnp.concatenate([ref[...] for ref in parts], axis=1)
    count, columns = outs[0].shape

    def one(c, carry):
        at = pl.ds(pl.multiple_of(c * chunk, chunk), chunk)
        weight = jnp.concatenate([ref[at, :] for ref in weights], axis=1)
        mixed = lax.dot_general(rows, weight, NT, preferred_element_type=f32).astype(bf)
        for r, out in enumerate(outs):
            out[:, at] = mixed[r * count : (r + 1) * count]
        return carry

    lax.fori_loop(0, columns // chunk, one, 0)


def place_in_plane(low):
    index = lax.axis_index("seq")
    return jnp.stack([index % low, index // low]).astype(jnp.int32)


def project_back(weights, blocks):
    low, bf = len(weights), jnp.bfloat16
    size = weights[0].shape[1]
    rows, depth = blocks[0].shape[0] * len(blocks), blocks[0].shape[1]
    return run(
        functools.partial(project_back_kernel, low), (*weights, *blocks),
        (((rows, size), bf),) * low, (((rows, depth), bf),), 8, "project_back",
    )


def project(weights, parts, high):
    low, columns = len(weights), weights[0].shape[0]
    return run(
        functools.partial(project_kernel, low, math.gcd(columns, 512)), (*weights, *parts),
        (((parts[0].shape[0] // high, columns), jnp.bfloat16),) * high, (), 6, "project",
    )


def head_kernels(pos, size, low):
    blocks, lanes = pos.shape
    rows = blocks * lanes
    bf, f32 = jnp.bfloat16, jnp.float32
    scale = 1.0 / math.sqrt(size)
    plain, padded, wide = (rows, size), (rows + 2 * CAP, size), (lanes, size)
    me = place_in_plane(low)

    def call(kernel, operands, outs, scratch, micros, name, late=0):
        scratch = [(shape, f32) for shape in (wide, *scratch)]
        return run(kernel, operands, outs, scratch, micros, name, late)

    def scores(query_key, bias):
        return call(
            functools.partial(scores_kernel, scale), (pos, query_key, bias),
            ((padded, bf), (padded, bf), ((rows, WIN), bf)), (padded, padded, wide), 12, "scores", 1,
        )

    def attend(value, probs):
        return call(
            functools.partial(attend_kernel, low), (me, pos, value, probs),
            (((blocks // low * lanes, size), bf),) * low + ((plain, bf), (padded, bf)),
            (padded, padded), 12, "attend", 1,
        )

    def grad_value(grads, probs):
        return call(
            functools.partial(value_kernel, low), (me, pos, *grads, probs),
            (((blocks, lanes, size), bf), (plain, bf)), (padded, padded), 12, "grad_value", 1,
        )

    def rest(grad, attended, query, key, value, probs):
        return call(
            functools.partial(rest_kernel, scale),
            (pos, grad, attended, query, key, value, probs),
            (((blocks, 2 * lanes, size), bf),), (padded, padded, wide), 16, "rest",
        )[0]

    return scores, attend, grad_value, rest


def pack_kernel(*refs):
    out_ref = refs[-1]
    size = out_ref.shape[2]
    first = 0
    for ref in refs[:-1]:
        rows = ref.shape[-2]
        for h in range(out_ref.shape[0]):
            if len(ref.shape) == 3:
                out_ref[h, pl.ds(first, rows), :] = ref[h]
            else:
                out_ref[h, pl.ds(first, rows), :] = ref[:, pl.ds(h * size, size)]
        first += rows


def pack(arrays, heads):
    rows = sum(array.shape[-2] for array in arrays)
    size = arrays[0].shape[1] // heads
    step = math.gcd(heads, 8)

    def block(array):
        if array.ndim == 3:
            return pl.BlockSpec((step, *array.shape[1:]), lambda i: (i, 0, 0))
        return pl.BlockSpec((array.shape[0], step * size), lambda i: (0, i))

    return pl.pallas_call(
        pack_kernel,
        grid=(heads // step,),
        out_shape=jax.ShapeDtypeStruct((heads, rows, size), arrays[0].dtype),
        in_specs=[block(array) for array in arrays],
        out_specs=pl.BlockSpec((step, rows, size), lambda i: (i, 0, 0)),
        compiler_params=SMALL,
        cost_estimate=lasts(0.1),
        name="pack",
    )(*arrays)


def unpack_kernel(in_ref, *refs):
    heads, rows, size = in_ref.shape
    rows = rows // len(refs)
    for part, ref in enumerate(refs):
        for h in range(heads):
            ref[:, pl.ds(h * size, size)] = in_ref[h, pl.ds(part * rows, rows), :]


def unpack(packed, parts):
    heads, rows, size = packed.shape
    rows = rows // parts
    step = math.gcd(heads, 8)
    return pl.pallas_call(
        unpack_kernel,
        grid=(heads // step,),
        out_shape=(jax.ShapeDtypeStruct((rows, heads * size), packed.dtype),) * parts,
        in_specs=[pl.BlockSpec((step, parts * rows, size), lambda i: (i, 0, 0))],
        out_specs=(pl.BlockSpec((rows, step * size), lambda i: (0, i)),) * parts,
        compiler_params=SMALL,
        cost_estimate=lasts(3),
        name="unpack",
    )(packed)


def by_clusters(query_rows, key_rows, value_rows, cluster_id, slot_index, out_weight, grad_out):
    rows_dev = query_rows.shape[0]
    heads_dev = cluster_id.shape[0]
    head_size = query_rows.shape[1] // heads_dev
    owners = lax.axis_size("seq")
    send_most = 2 * rows_dev // owners
    buffer_rows = owners * send_most
    room = CLU_DEV * CAP
    score_scale = 1.0 / math.sqrt(head_size)
    masked_score = -1e30
    owner = cluster_id // CLU_DEV
    owner_onehot = (owner[:, :, None] == jnp.arange(owners, dtype=jnp.int32)[None, None, :]).astype(
        jnp.bfloat16
    )
    row_ids = jnp.arange(rows_dev, dtype=jnp.int32)
    lower = (row_ids[:, None] > row_ids[None, :]).astype(jnp.bfloat16)
    earlier = jnp.einsum("ij,hjo->hio", lower, owner_onehot, preferred_element_type=jnp.float32)
    rank = jnp.sum(earlier * owner_onehot.astype(jnp.float32), axis=2).astype(jnp.int32)
    place = owner * send_most + rank
    target = cluster_id % CLU_DEV * CAP + slot_index
    buffer_ids = jnp.arange(buffer_rows, dtype=jnp.int32)
    send_table = (place[:, None, :] == buffer_ids[None, :, None]).astype(jnp.bfloat16)

    def to_buffer(rows):
        split = rows.reshape(rows_dev, heads_dev, head_size)
        filled = jnp.einsum(
            "hbi,ihd->bhd", send_table, split, preferred_element_type=jnp.float32
        ).astype(rows.dtype)
        return filled.reshape(buffer_rows, heads_dev * head_size)

    def from_buffer(buffer):
        split = buffer.reshape(buffer_rows, heads_dev, head_size)
        picked = jnp.einsum(
            "hbi,bhd->ihd", send_table, split, preferred_element_type=jnp.float32
        ).astype(buffer.dtype)
        return picked.reshape(rows_dev, heads_dev * head_size)

    target_rows = (
        jnp.einsum(
            "hbi,hi->bh", send_table.astype(jnp.float32), (target - room).astype(jnp.float32)
        ).astype(jnp.int32)
        + room
    )
    arrived = lax.all_to_all(target_rows, "seq", split_axis=0, concat_axis=0, tiled=True)
    routed_query, routed_key, routed_value = (
        lax.all_to_all(to_buffer(query_rows), "seq", split_axis=0, concat_axis=0, tiled=True),
        lax.all_to_all(to_buffer(key_rows), "seq", split_axis=0, concat_axis=0, tiled=True),
        lax.all_to_all(to_buffer(value_rows), "seq", split_axis=0, concat_axis=0, tiled=True),
    )
    room_ids = jnp.arange(room, dtype=jnp.int32)
    cell_table = (arrived.T[:, None, :] == room_ids[None, :, None]).astype(jnp.bfloat16)

    def to_cells(buffer):
        split = buffer.reshape(buffer_rows, heads_dev, head_size)
        cells = jnp.einsum(
            "hrb,bhd->hrd", cell_table, split, preferred_element_type=jnp.float32
        ).astype(buffer.dtype)
        return cells.reshape(heads_dev, CLU_DEV, CAP, head_size)

    def to_returns(cells):
        flat = cells.reshape(heads_dev, room, head_size)
        picked = jnp.einsum(
            "hrb,hrd->bhd", cell_table, flat, preferred_element_type=jnp.float32
        ).astype(cells.dtype)
        return picked.reshape(buffer_rows, heads_dev * head_size)

    live = jnp.sum(cell_table.astype(jnp.float32), axis=2).reshape(heads_dev, CLU_DEV, CAP)
    query_cells = to_cells(routed_query)
    key_cells = to_cells(routed_key)
    value_cells = to_cells(routed_value)
    scores = (
        jnp.einsum("hcqd,hckd->hcqk", query_cells, key_cells, preferred_element_type=jnp.float32)
        * score_scale
    )
    scores = jnp.where(live[:, :, None, :] > 0.5, scores, masked_score)
    top = jnp.max(scores, axis=-1, keepdims=True)
    weights = jnp.exp(scores - top)
    probs = weights / jnp.sum(weights, axis=-1, keepdims=True)
    probs_low = probs.astype(jnp.bfloat16)
    attended_cells = jnp.einsum(
        "hcqk,hckd->hcqd", probs_low, value_cells, preferred_element_type=jnp.float32
    ).astype(jnp.bfloat16)
    returned = lax.all_to_all(
        to_returns(attended_cells), "seq", split_axis=0, concat_axis=0, tiled=True
    )
    attended = from_buffer(returned)
    full_weight = lax.all_gather(out_weight, "seq", axis=1, tiled=True)
    rows = attended
    mixed = lax.psum_scatter(
        jnp.dot(rows, full_weight, preferred_element_type=jnp.float32).astype(jnp.bfloat16),
        "tensor",
        scatter_dimension=0,
        tiled=True,
    )
    grad_attended = lax.dot_general(
        lax.all_gather(grad_out, "tensor", axis=0, tiled=True),
        full_weight,
        (((1,), (1,)), ((), ())),
        preferred_element_type=jnp.float32,
    )
    grad_low = grad_attended.astype(jnp.bfloat16)
    routed_grad = lax.all_to_all(
        to_buffer(grad_low), "seq", split_axis=0, concat_axis=0, tiled=True
    )
    grad_cells = to_cells(routed_grad)
    backward_low = probs.astype(jnp.bfloat16)
    delta = jnp.einsum(
        "hcqd,hcqd->hcq", grad_cells, attended_cells, preferred_element_type=jnp.float32
    )
    grad_value = jnp.einsum(
        "hcqk,hcqd->hckd", backward_low, grad_cells, preferred_element_type=jnp.float32
    ).astype(jnp.bfloat16)
    grad_probs = jnp.einsum(
        "hcqd,hckd->hcqk", grad_cells, value_cells, preferred_element_type=jnp.float32
    )
    grad_scores = (probs * (grad_probs - delta[..., None])).astype(jnp.bfloat16)
    grad_query = (
        jnp.einsum("hcqk,hckd->hcqd", grad_scores, key_cells, preferred_element_type=jnp.float32)
        * score_scale
    ).astype(jnp.bfloat16)
    grad_key = (
        jnp.einsum("hcqk,hcqd->hckd", grad_scores, query_cells, preferred_element_type=jnp.float32)
        * score_scale
    ).astype(jnp.bfloat16)
    back_query, back_key, back_value = (
        lax.all_to_all(to_returns(grad_query), "seq", split_axis=0, concat_axis=0, tiled=True),
        lax.all_to_all(to_returns(grad_key), "seq", split_axis=0, concat_axis=0, tiled=True),
        lax.all_to_all(to_returns(grad_value), "seq", split_axis=0, concat_axis=0, tiled=True),
    )
    return (mixed, from_buffer(back_query), from_buffer(back_key), from_buffer(back_value))


def by_heads(query_rows, key_rows, value_rows, cluster_id, slot_index, out_weight, grad_out):
    rows_dev, width = query_rows.shape
    heads_dev = cluster_id.shape[0]
    head_size = width // heads_dev
    owners = lax.axis_size("seq")
    columns_dev = out_weight.shape[1]
    high, low = split(owners)
    bf, f32 = jnp.bfloat16, jnp.float32
    together = lax.optimization_barrier

    def exchange(rows):
        return lax.all_to_all(rows, "seq", split_axis=0, concat_axis=0, tiled=True)

    def send(block, bits):
        return lax.ppermute(block, "seq", [(i, i ^ bits) for i in range(owners)])

    def swap(blocks):
        return [blocks[0]] + [send(blocks[k], k) for k in range(1, low)]

    def gather_plane(block, after):
        near = [block] + [send(block, k) for k in range(2, low, 2)]
        near, after = together((near, after))
        return [x for one in near for x in (one, send(one, 1))], after

    def gather_stack(block, after):
        blocks, bit = {0: block}, high // 2
        while bit:
            blocks |= {r | bit: send(one, bit * low) for r, one in blocks.items()}
            bit //= 2
            if bit == high // 4:
                blocks, after = together((blocks, after))
        return [blocks[r] for r in range(high)], after

    def sum_stack(blocks):
        blocks, bit = dict(enumerate(blocks)), 1
        while bit < high:
            blocks = {
                r: (one.astype(f32) + send(blocks[r | bit], bit * low).astype(f32)).astype(bf)
                for r, one in blocks.items()
                if not r & bit
            }
            bit *= 2
        return blocks[0]

    weight_rows = out_weight.T.reshape(columns_dev, heads_dev, head_size).transpose(1, 0, 2)
    ids = jnp.stack([cluster_id // rows_dev, cluster_id % rows_dev, slot_index], axis=1)
    ids = jnp.pad(ids, ((0, 0), (0, 13), (0, 0))).astype(bf)
    first = exchange(jnp.concatenate([weight_rows, ids], axis=1))
    grad_out_stack, first = gather_stack(grad_out, first)
    packed = pack((query_rows, key_rows), heads_dev)
    packed_value = pack((value_rows,), heads_dev)
    packed, packed_value, first = together((packed, packed_value, first))
    arrived = exchange(packed)
    placed = place(first[:, columns_dev:], CLU_DEV * owners)
    head_weight = first[:, :columns_dev].reshape(owners * columns_dev, head_size)
    weights, (pos, bias) = gather_plane(head_weight, placed)
    grad_heads = project_back(weights, grad_out_stack)
    packed_value, arrived, grad_heads = together((packed_value, arrived, grad_heads))
    value = exchange(packed_value)
    grad_heads = swap(grad_heads)
    scores, attend, grad_of_value, rest = head_kernels(pos, head_size, low)
    query, key, probs = scores(arrived, bias)
    grad_value, grad_sorted = grad_of_value(grad_heads, probs)
    value, grad_value = together((value, grad_value))
    *attended, att_sorted, value_sorted = attend(value, probs)
    back_value = exchange(grad_value)
    attended = swap(attended)
    grads = rest(grad_sorted, att_sorted, query, key, value_sorted, probs)
    grads, attended = together((grads, attended))
    grads, back_value = together((grads, back_value))
    back = exchange(grads)
    mixed = sum_stack(project(weights, attended, high))
    return (mixed, *unpack(back, 2), *unpack(back_value, 1))


def split(owners):
    high = 1
    while 4 * high * high <= owners:
        high *= 2
    return high, owners // high


def solution(mesh):
    def shards(*args):
        heads_dev = args[3].shape[0]
        owners = lax.axis_size("seq")
        if heads_dev == owners and owners & (owners - 1) == 0 and lax.axis_size("tensor") == 1:
            return by_heads(*args)
        return by_clusters(*args)

    return jax.shard_map(
        shards,
        mesh=mesh,
        in_specs=(
            P("seq", "tensor"),
            P("seq", "tensor"),
            P("seq", "tensor"),
            P("tensor", "seq"),
            P("tensor", "seq"),
            P("tensor", "seq"),
            P(("seq", "tensor"), None),
        ),
        out_specs=(
            P(("seq", "tensor"), None),
            P("seq", "tensor"),
            P("seq", "tensor"),
            P("seq", "tensor"),
        ),
        check_vma=False,
    )
```

```python
import functools
import math

import jax
import jax.numpy as jnp
from jax import lax
from jax.experimental import pallas as pl
from jax.experimental.pallas import tpu as pltpu
from jax.sharding import PartitionSpec as P

CLU_DEV = 8
CAP = 32
TILE = 64
WIN = TILE + 2 * CAP
MASKED = -1e30
UNROLL = 8
VMEM = pl.BlockSpec(memory_space=pltpu.VMEM)
SMEM = pl.BlockSpec(memory_space=pltpu.SMEM)
HBM = pl.BlockSpec(memory_space=pltpu.HBM)
PARAMS = pltpu.CompilerParams(vmem_limit_bytes=61 * 1024 * 1024)
SMALL = pltpu.CompilerParams(vmem_limit_bytes=16 * 1024 * 1024)


def lasts(micros):
    return pl.CostEstimate(flops=0, bytes_accessed=int(micros * 3.5e6), transcendentals=0)


NT = (((1,), (1,)), ((), ()))
TN = (((0,), (0,)), ((), ()))


def run(kernel, operands, outs, scratch, micros, name, late=0):
    where = [SMEM if x.dtype == jnp.int32 else HBM for x in operands]
    held = [pltpu.VMEM(x.shape, x.dtype) for x, spec in zip(operands, where) if spec is HBM]

    def body(*refs):
        given, rest = refs[: len(operands)], refs[len(operands) :]
        slots, sems, rest = rest[-1 - len(held) : -1], rest[-1], rest[: -1 - len(held)]
        copies, arrays = [], []
        for ref, spec in zip(given, where):
            if spec is HBM:
                slot = slots[len(copies)]
                copies.append(pltpu.make_async_copy(ref, slot, sems.at[len(copies)]))
                ref = slot
            arrays.append(ref)
        for copy in copies:
            copy.start()
        now = len(copies) - late
        for copy in copies[:now]:
            copy.wait()
        if late:
            def arrive():
                for copy in copies[now:]:
                    copy.wait()

            kernel(arrive, *arrays, *rest)
        else:
            kernel(*arrays, *rest)

    return pl.pallas_call(
        body,
        out_shape=tuple(jax.ShapeDtypeStruct(shape, kind) for shape, kind in outs),
        in_specs=where,
        out_specs=(VMEM,) * len(outs),
        scratch_shapes=[
            *(pltpu.VMEM(shape, kind) for shape, kind in scratch),
            *held,
            pltpu.SemaphoreType.DMA((len(held),)),
        ],
        compiler_params=PARAMS,
        cost_estimate=lasts(micros),
        name=name,
    )(*operands)


def place_kernel(clusters, low, high, me_ref, *refs):
    parts, (pos_ref, bias_ref, stage, *ids) = refs[:low], refs[low:]
    blocks, lanes = pos_ref.shape
    bf, f32 = jnp.bfloat16, jnp.float32
    cluster_ids = lax.broadcasted_iota(jnp.int32, (clusters, lanes), 0).astype(f32)
    slot_ids = lax.broadcasted_iota(jnp.int32, (CAP, lanes), 0).astype(f32)
    count_rows = stage.shape[0]
    for k in range(low):
        for s in range(high):
            b = (me_ref[1] ^ s) * low + (me_ref[0] ^ k)
            stage[...] = parts[k][s, parts[k].shape[1] - count_rows :, :].astype(f32)
            for kind, ref in enumerate(ids):
                ref[pl.ds(b, 1), :] = stage[pl.ds(kind * low + me_ref[0], 1), :]

    def tables(b):
        cluster = ids[0][pl.ds(b, 1), :] * lanes + ids[1][pl.ds(b, 1), :]
        return (
            jnp.where(cluster_ids == cluster, 1.0, 0.0),
            jnp.where(slot_ids == ids[2][pl.ds(b, 1), :], 1.0, 0.0),
        )

    def count(step, occupied):
        some = [tables(step * 4 + u) for u in range(4)]
        by_cluster = jnp.concatenate([t[0] for t in some], axis=1).astype(bf)
        by_slot = jnp.concatenate([t[1] for t in some], axis=1).astype(bf)
        return occupied + lax.dot_general(
            by_cluster, by_slot, NT, preferred_element_type=f32
        )

    occupied = lax.fori_loop(0, blocks // 4, count, jnp.zeros((clusters, CAP), f32))
    occupied_low = occupied.astype(bf)
    slot_from = lax.broadcasted_iota(jnp.int32, (CAP, CAP), 0)
    slot_to = lax.broadcasted_iota(jnp.int32, (CAP, CAP), 1)
    within = jnp.dot(
        occupied_low, jnp.where(slot_from < slot_to, 1.0, 0.0).astype(bf),
        preferred_element_type=f32,
    )
    size_col = jnp.sum(occupied, axis=1, keepdims=True)
    sizes = jnp.broadcast_to(size_col, (clusters, 128)).astype(bf)
    row_ids = lax.broadcasted_iota(jnp.int32, (clusters, clusters), 0)
    col_ids = lax.broadcasted_iota(jnp.int32, (clusters, clusters), 1)
    before = jnp.where(col_ids < row_ids, 1.0, 0.0).astype(bf)
    start = jnp.dot(before, sizes, preferred_element_type=f32)
    ends_col = start[:, 0:1] + size_col
    upto = jnp.where(row_ids <= col_ids, 1.0, 0.0).astype(bf)
    ends_row = lax.dot_general(
        sizes, upto, (((0,), (0,)), ((), ())), preferred_element_type=f32
    )[0:1]
    high = jnp.floor(start * (1.0 / 64.0))
    low = start - high * 64.0
    lookup = jnp.concatenate([within, high[:, :CAP], low[:, :CAP]], axis=1).astype(bf)

    def find(step, carry):
        some = [tables(step * 4 + u) for u in range(4)]
        found = [
            lax.dot_general(lookup, by_cluster.astype(bf), TN, preferred_element_type=f32)
            for by_cluster, _ in some
        ]
        for u in range(4):
            inner = jnp.sum(found[u][:CAP] * some[u][1], axis=0, keepdims=True)
            outer = found[u][CAP : CAP + 1] * 64.0 + found[u][2 * CAP : 2 * CAP + 1]
            pos_ref[pl.ds(step * 4 + u, 1), :] = (outer + inner).astype(jnp.int32) + CAP
        return carry

    lax.fori_loop(0, blocks // 4, find, 0)
    rows = blocks * lanes

    ones = jnp.ones((clusters, WIN), bf)
    few = jnp.ones((8, clusters), bf)

    def labels(step, carry):
        mines, others = [], []
        for u in range(UNROLL):
            t = step * UNROLL + u
            at = (t * TILE + lax.broadcasted_iota(jnp.int32, (TILE, clusters), 0)).astype(f32)
            ended = jnp.where(ends_row <= at, 1.0, 0.0).astype(bf)
            mines.append(jnp.dot(ended, ones, preferred_element_type=f32))
            wide = t * TILE - CAP + lax.broadcasted_iota(jnp.int32, (clusters, WIN), 1)
            ended = jnp.where(ends_col <= wide.astype(f32), 1.0, 0.0).astype(bf)
            other = jnp.dot(few, ended, preferred_element_type=f32)[0:1]
            spot = wide[0:1]
            others.append(jnp.where((spot >= 0) & (spot < rows), other, -1.0))
        for u in range(UNROLL):
            at = pl.ds(pl.multiple_of((step * UNROLL + u) * TILE, TILE), TILE)
            bias_ref[at, :] = jnp.where(mines[u] == others[u], 0.0, MASKED).astype(bf)
        return carry

    lax.fori_loop(0, rows // TILE // UNROLL, labels, 0)


def id_rows(low):
    return -(-3 * low // 16) * 16


def place(gathered, clusters):
    low, (high, _, lanes) = len(gathered), gathered[0].shape
    f32, blocks = jnp.float32, len(gathered) * high
    return run(
        functools.partial(place_kernel, clusters, low, high), (place_in_plane(low), *gathered),
        (((blocks, lanes), jnp.int32), ((blocks * lanes, WIN), jnp.bfloat16)),
        (((id_rows(low), lanes), f32),) + (((blocks, lanes), f32),) * 3, 8, "place",
    )


ROWS_AT_ONCE = 16


def move_in(pos_ref, block_of, loads, wides, sorted_refs, count):
    lanes = pos_ref.shape[1]

    def one(r, carry):
        b = block_of(r)
        for load, wide in zip(loads, wides):
            wide[...] = load(r).astype(jnp.float32)
        for first in range(0, lanes, ROWS_AT_ONCE):
            rows = range(first, first + ROWS_AT_ONCE)
            places = [pl.ds(pos_ref[b, row], 1) for row in rows]
            held = [[wide[pl.ds(row, 1), :] for row in rows] for wide in wides]
            for i, at in enumerate(places):
                for ref, some in zip(sorted_refs, held):
                    ref[at, :] = some[i]
        return carry

    lax.fori_loop(0, count, one, 0)


def move_out(pos_ref, block_of, sorted_refs, wides, stores, count):
    lanes = pos_ref.shape[1]

    def one(r, carry):
        b = block_of(r)
        for first in range(0, lanes, ROWS_AT_ONCE):
            rows = range(first, first + ROWS_AT_ONCE)
            places = [pl.ds(pos_ref[b, row], 1) for row in rows]
            held = [[ref[at, :] for at in places] for ref in sorted_refs]
            for i, row in enumerate(rows):
                for wide, some in zip(wides, held):
                    wide[pl.ds(row, 1), :] = some[i]
        for store, wide in zip(stores, wides):
            store(r, wide[...])
        return carry

    lax.fori_loop(0, count, one, 0)


def tiles_of(step):
    bases = [pl.multiple_of((step * UNROLL + u) * TILE, TILE) for u in range(UNROLL)]
    tiles = [pl.ds(base, TILE) for base in bases]
    windows = [pl.ds(base, WIN) for base in bases]
    inner = [pl.ds(pl.multiple_of(base + CAP, CAP), TILE) for base in bases]
    return tiles, windows, inner


def scores_kernel(
    scale, arrive, pos_ref, rows_ref, bias_ref, query_ref, key_ref, probs_ref,
    wide, query, key, more,
):
    bf, f32 = jnp.bfloat16, jnp.float32
    blocks, lanes = pos_ref.shape
    rows = blocks * lanes
    edge = jnp.zeros((CAP, wide.shape[1]), f32)
    for ref in (query, key):
        ref[pl.ds(0, CAP), :] = edge
        ref[pl.ds(rows + CAP, CAP), :] = edge
    move_in(
        pos_ref, lambda b: b,
        [lambda b, part=part: rows_ref[b, pl.ds(part * lanes, lanes), :] for part in range(2)],
        [wide, more], [query, key], blocks,
    )
    query_ref[...] = query[...].astype(bf)
    key_ref[...] = key[...].astype(bf)
    arrive()

    def some(step, carry):
        tiles, windows, inner = tiles_of(step)
        qs = [query_ref[at, :] for at in inner]
        ks = [key_ref[at, :] for at in windows]
        biases = [bias_ref[at, :].astype(f32) for at in tiles]
        scores = [lax.dot_general(q, k, NT, preferred_element_type=f32) for q, k in zip(qs, ks)]
        scores = [s * scale + bias for s, bias in zip(scores, biases)]
        tops = [jnp.max(s, axis=1, keepdims=True) for s in scores]
        weights = [jnp.exp(s - top) for s, top in zip(scores, tops)]
        sums = [jnp.sum(w, axis=1, keepdims=True) for w in weights]
        for at, w, total in zip(tiles, weights, sums):
            probs_ref[at, :] = (w / total).astype(bf)
        return carry

    lax.fori_loop(0, rows // TILE // UNROLL, some, 0)


def attend_kernel(
    low, arrive, me_ref, pos_ref, rows_ref, probs_ref, *refs
):
    parts, (sorted_ref, value_ref, wide, value, att) = refs[:low], refs[low:]
    bf, f32 = jnp.bfloat16, jnp.float32
    blocks, lanes = pos_ref.shape
    rows = blocks * lanes
    high = blocks // low
    edge = jnp.zeros((CAP, wide.shape[1]), f32)
    value[pl.ds(0, CAP), :] = edge
    value[pl.ds(rows + CAP, CAP), :] = edge
    move_in(pos_ref, lambda b: b, [lambda b: rows_ref[b]], [wide], [value], blocks)
    value_ref[...] = value[...].astype(bf)
    arrive()

    def some(step, carry):
        tiles, windows, inner = tiles_of(step)
        vs = [value_ref[at, :] for at in windows]
        probs = [probs_ref[at, :] for at in tiles]
        attended = [jnp.dot(p, v, preferred_element_type=f32) for p, v in zip(probs, vs)]
        for at, to, one in zip(tiles, inner, attended):
            att[to, :] = one
            sorted_ref[at, :] = one.astype(bf)
        return carry

    lax.fori_loop(0, rows // TILE // UNROLL, some, 0)

    for k in range(low):
        def put(r, block, k=k):
            parts[k][pl.ds(pl.multiple_of(r * lanes, lanes), lanes), :] = block.astype(bf)

        move_out(
            pos_ref, lambda r, k=k: (me_ref[1] ^ r) * low + (me_ref[0] ^ k),
            [att], [wide], [put], high,
        )


def value_kernel(
    low, arrive, me_ref, pos_ref, *refs
):
    parts, (probs_ref, out_ref, sorted_ref, wide, grad, grad_value) = refs[:low], refs[low:]
    bf, f32 = jnp.bfloat16, jnp.float32
    blocks, lanes = pos_ref.shape
    rows = blocks * lanes
    high = blocks // low
    for k in range(low):
        def block_of(r, k=k):
            return (me_ref[1] ^ r) * low + (me_ref[0] ^ k)

        def load(r, k=k):
            return parts[k][pl.ds(pl.multiple_of(r * lanes, lanes), lanes), :]

        move_in(pos_ref, block_of, [load], [wide], [grad], high)
    sorted_ref[...] = grad[pl.ds(CAP, rows), :].astype(bf)
    grad_value[...] = jnp.zeros_like(grad_value)
    arrive()

    def some(step, carry):
        tiles, windows, _ = tiles_of(step)
        gs = [sorted_ref[at, :] for at in tiles]
        probs = [probs_ref[at, :] for at in tiles]
        more = [lax.dot_general(p, g, TN, preferred_element_type=f32) for p, g in zip(probs, gs)]
        for at, one in zip(windows, more):
            grad_value[at, :] += one
        return carry

    lax.fori_loop(0, rows // TILE // UNROLL, some, 0)

    def put(b, block):
        out_ref[b] = block.astype(bf)

    move_out(pos_ref, lambda b: b, [grad_value], [wide], [put], blocks)


def rest_kernel(
    scale, pos_ref, grad_ref, sorted_ref, query_ref, key_ref, value_ref, probs_ref,
    out_ref, wide, grad_query, grad_key, more,
):
    bf, f32 = jnp.bfloat16, jnp.float32
    blocks, lanes = pos_ref.shape
    rows = blocks * lanes
    grad_key[...] = jnp.zeros_like(grad_key)

    def some(step, carry):
        tiles, windows, inner = tiles_of(step)
        gs = [grad_ref[at, :] for at in tiles]
        qs = [query_ref[at, :] for at in inner]
        ks = [key_ref[at, :] for at in windows]
        vs = [value_ref[at, :] for at in windows]
        probs = [probs_ref[at, :] for at in tiles]
        attended = [sorted_ref[at, :].astype(f32) for at in tiles]
        grad_probs = [lax.dot_general(g, v, NT, preferred_element_type=f32) for g, v in zip(gs, vs)]
        deltas = [
            jnp.sum(g.astype(f32) * one, axis=1, keepdims=True) for g, one in zip(gs, attended)
        ]
        grad_scores = [
            (p.astype(f32) * (gp - delta)).astype(bf)
            for p, gp, delta in zip(probs, grad_probs, deltas)
        ]
        grad_queries = [jnp.dot(d, k, preferred_element_type=f32) for d, k in zip(grad_scores, ks)]
        more_keys = [
            lax.dot_general(d, q, TN, preferred_element_type=f32) for d, q in zip(grad_scores, qs)
        ]
        for at, one in zip(inner, grad_queries):
            grad_query[at, :] = one
        for at, one in zip(windows, more_keys):
            grad_key[at, :] += one
        return carry

    lax.fori_loop(0, rows // TILE // UNROLL, some, 0)

    def put(part):
        def store(b, block):
            out_ref[b, pl.ds(part * lanes, lanes), :] = (block * scale).astype(bf)
        return store

    move_out(
        pos_ref, lambda b: b, [grad_query, grad_key], [wide, more], [put(0), put(1)], blocks
    )


def project_back_kernel(low, high, columns, me_ref, *refs):
    bf, f32 = jnp.bfloat16, jnp.float32
    gathered, blocks = refs[:low], refs[low : low + high]
    outs, weight_ref, rows_ref = refs[low + high : -2], refs[-2], refs[-1]
    size = gathered[0].shape[2]
    rows = blocks[0].shape[0]
    for r, block in enumerate(blocks):
        rows_ref[pl.ds(r * rows, rows), :] = block[...]
    for k in range(0, low, 2):
        for source in range(low):
            for s in range(high):
                first = ((me_ref[1] ^ s) * low + (me_ref[0] ^ source)) * columns
                at = pl.ds(pl.multiple_of(first, columns), columns)
                for head in (k, k + 1):
                    start = pl.multiple_of((me_ref[0] ^ head) * columns, columns)
                    weight_ref[head, at, :] = gathered[source][s, pl.ds(start, columns), :]
        weight = jnp.concatenate([weight_ref[k], weight_ref[k + 1]], axis=1)
        both = jnp.dot(rows_ref[...], weight, preferred_element_type=f32).astype(bf)
        outs[k][...] = both[:, :size]
        outs[k + 1][...] = both[:, size:]


def project_kernel(low, chunk, weight_ref, *refs):
    bf, f32 = jnp.bfloat16, jnp.float32
    parts, outs = refs[:low], refs[low:]
    rows = jnp.concatenate([ref[...] for ref in parts], axis=1)
    count, columns = outs[0].shape

    def one(c, carry):
        at = pl.ds(pl.multiple_of(c * chunk, chunk), chunk)
        weight = jnp.concatenate([weight_ref[k, at, :] for k in range(low)], axis=1)
        mixed = lax.dot_general(rows, weight, NT, preferred_element_type=f32).astype(bf)
        for r, out in enumerate(outs):
            out[:, at] = mixed[r * count : (r + 1) * count]
        return carry

    lax.fori_loop(0, columns // chunk, one, 0)


def pack_weight_kernel(low, me_ref, weight_ref, ids_ref, *outs):
    size, columns = outs[0].shape[1], weight_ref.shape[0]
    for s, out in enumerate(outs):
        plane = me_ref[1] ^ s
        for h in range(low):
            at = pl.ds(pl.multiple_of((plane * low + h) * size, size), size)
            out[pl.ds(h * columns, columns), :] = weight_ref[:, at]
        out[low * columns :, :] = ids_ref[plane]


def pack_weight(weight, ids, low):
    high, rows, size = ids.shape
    return run(
        functools.partial(pack_weight_kernel, low), (place_in_plane(low), weight, ids),
        (((low * weight.shape[0] + rows, size), weight.dtype),) * high, (), 2, "pack_weight",
    )


def place_in_plane(low):
    index = lax.axis_index("seq")
    return jnp.stack([index % low, index // low]).astype(jnp.int32)


def project_back(gathered, blocks):
    low, high, bf = len(gathered), len(blocks), jnp.bfloat16
    size = gathered[0].shape[-1]
    rows, depth = blocks[0].shape[0] * high, blocks[0].shape[1]
    *heads, weight = run(
        functools.partial(project_back_kernel, low, high, depth // (low * high)),
        (place_in_plane(low), *gathered, *blocks),
        (((rows, size), bf),) * low + (((low, depth, size), bf),),
        (((rows, depth), bf),), 8, "project_back",
    )
    return heads, weight


def project(weight, parts, high):
    low, columns = weight.shape[:2]
    return run(
        functools.partial(project_kernel, low, math.gcd(columns, 512)), (weight, *parts),
        (((parts[0].shape[0] // high, columns), jnp.bfloat16),) * high, (), 6, "project",
    )


def head_kernels(pos, size, low):
    blocks, lanes = pos.shape
    rows = blocks * lanes
    bf, f32 = jnp.bfloat16, jnp.float32
    scale = 1.0 / math.sqrt(size)
    plain, padded, wide = (rows, size), (rows + 2 * CAP, size), (lanes, size)
    me = place_in_plane(low)

    def call(kernel, operands, outs, scratch, micros, name, late=0):
        scratch = [(shape, f32) for shape in (wide, *scratch)]
        return run(kernel, operands, outs, scratch, micros, name, late)

    def scores(query_key, bias):
        return call(
            functools.partial(scores_kernel, scale), (pos, query_key, bias),
            ((padded, bf), (padded, bf), ((rows, WIN), bf)), (padded, padded, wide), 12, "scores", 1,
        )

    def attend(value, probs):
        return call(
            functools.partial(attend_kernel, low), (me, pos, value, probs),
            (((blocks // low * lanes, size), bf),) * low + ((plain, bf), (padded, bf)),
            (padded, padded), 12, "attend", 1,
        )

    def grad_value(grads, probs):
        return call(
            functools.partial(value_kernel, low), (me, pos, *grads, probs),
            (((blocks, lanes, size), bf), (plain, bf)), (padded, padded), 12, "grad_value", 1,
        )

    def rest(grad, attended, query, key, value, probs):
        return call(
            functools.partial(rest_kernel, scale),
            (pos, grad, attended, query, key, value, probs),
            (((blocks, 2 * lanes, size), bf),), (padded, padded, wide), 16, "rest",
        )[0]

    return scores, attend, grad_value, rest


def pack_kernel(*refs):
    out_ref = refs[-1]
    size = out_ref.shape[2]
    first = 0
    for ref in refs[:-1]:
        rows = ref.shape[-2]
        for h in range(out_ref.shape[0]):
            if len(ref.shape) == 3:
                out_ref[h, pl.ds(first, rows), :] = ref[h]
            else:
                out_ref[h, pl.ds(first, rows), :] = ref[:, pl.ds(h * size, size)]
        first += rows


def pack(arrays, heads):
    rows = sum(array.shape[-2] for array in arrays)
    size = arrays[0].shape[1] // heads
    step = math.gcd(heads, 8)

    def block(array):
        if array.ndim == 3:
            return pl.BlockSpec((step, *array.shape[1:]), lambda i: (i, 0, 0))
        return pl.BlockSpec((array.shape[0], step * size), lambda i: (0, i))

    return pl.pallas_call(
        pack_kernel,
        grid=(heads // step,),
        out_shape=jax.ShapeDtypeStruct((heads, rows, size), arrays[0].dtype),
        in_specs=[block(array) for array in arrays],
        out_specs=pl.BlockSpec((step, rows, size), lambda i: (i, 0, 0)),
        compiler_params=SMALL,
        cost_estimate=lasts(0.1),
        name="pack",
    )(*arrays)


def unpack_kernel(in_ref, *refs):
    heads, rows, size = in_ref.shape
    rows = rows // len(refs)
    for part, ref in enumerate(refs):
        for h in range(heads):
            ref[:, pl.ds(h * size, size)] = in_ref[h, pl.ds(part * rows, rows), :]


def unpack(packed, parts):
    heads, rows, size = packed.shape
    rows = rows // parts
    step = math.gcd(heads, 8)
    return pl.pallas_call(
        unpack_kernel,
        grid=(heads // step,),
        out_shape=(jax.ShapeDtypeStruct((rows, heads * size), packed.dtype),) * parts,
        in_specs=[pl.BlockSpec((step, parts * rows, size), lambda i: (i, 0, 0))],
        out_specs=(pl.BlockSpec((rows, step * size), lambda i: (0, i)),) * parts,
        compiler_params=SMALL,
        cost_estimate=lasts(3),
        name="unpack",
    )(packed)


def by_clusters(query_rows, key_rows, value_rows, cluster_id, slot_index, out_weight, grad_out):
    rows_dev = query_rows.shape[0]
    heads_dev = cluster_id.shape[0]
    head_size = query_rows.shape[1] // heads_dev
    owners = lax.axis_size("seq")
    send_most = 2 * rows_dev // owners
    buffer_rows = owners * send_most
    room = CLU_DEV * CAP
    score_scale = 1.0 / math.sqrt(head_size)
    masked_score = -1e30
    owner = cluster_id // CLU_DEV
    owner_onehot = (owner[:, :, None] == jnp.arange(owners, dtype=jnp.int32)[None, None, :]).astype(
        jnp.bfloat16
    )
    row_ids = jnp.arange(rows_dev, dtype=jnp.int32)
    lower = (row_ids[:, None] > row_ids[None, :]).astype(jnp.bfloat16)
    earlier = jnp.einsum("ij,hjo->hio", lower, owner_onehot, preferred_element_type=jnp.float32)
    rank = jnp.sum(earlier * owner_onehot.astype(jnp.float32), axis=2).astype(jnp.int32)
    place = owner * send_most + rank
    target = cluster_id % CLU_DEV * CAP + slot_index
    buffer_ids = jnp.arange(buffer_rows, dtype=jnp.int32)
    send_table = (place[:, None, :] == buffer_ids[None, :, None]).astype(jnp.bfloat16)

    def to_buffer(rows):
        split = rows.reshape(rows_dev, heads_dev, head_size)
        filled = jnp.einsum(
            "hbi,ihd->bhd", send_table, split, preferred_element_type=jnp.float32
        ).astype(rows.dtype)
        return filled.reshape(buffer_rows, heads_dev * head_size)

    def from_buffer(buffer):
        split = buffer.reshape(buffer_rows, heads_dev, head_size)
        picked = jnp.einsum(
            "hbi,bhd->ihd", send_table, split, preferred_element_type=jnp.float32
        ).astype(buffer.dtype)
        return picked.reshape(rows_dev, heads_dev * head_size)

    target_rows = (
        jnp.einsum(
            "hbi,hi->bh", send_table.astype(jnp.float32), (target - room).astype(jnp.float32)
        ).astype(jnp.int32)
        + room
    )
    arrived = lax.all_to_all(target_rows, "seq", split_axis=0, concat_axis=0, tiled=True)
    routed_query, routed_key, routed_value = (
        lax.all_to_all(to_buffer(query_rows), "seq", split_axis=0, concat_axis=0, tiled=True),
        lax.all_to_all(to_buffer(key_rows), "seq", split_axis=0, concat_axis=0, tiled=True),
        lax.all_to_all(to_buffer(value_rows), "seq", split_axis=0, concat_axis=0, tiled=True),
    )
    room_ids = jnp.arange(room, dtype=jnp.int32)
    cell_table = (arrived.T[:, None, :] == room_ids[None, :, None]).astype(jnp.bfloat16)

    def to_cells(buffer):
        split = buffer.reshape(buffer_rows, heads_dev, head_size)
        cells = jnp.einsum(
            "hrb,bhd->hrd", cell_table, split, preferred_element_type=jnp.float32
        ).astype(buffer.dtype)
        return cells.reshape(heads_dev, CLU_DEV, CAP, head_size)

    def to_returns(cells):
        flat = cells.reshape(heads_dev, room, head_size)
        picked = jnp.einsum(
            "hrb,hrd->bhd", cell_table, flat, preferred_element_type=jnp.float32
        ).astype(cells.dtype)
        return picked.reshape(buffer_rows, heads_dev * head_size)

    live = jnp.sum(cell_table.astype(jnp.float32), axis=2).reshape(heads_dev, CLU_DEV, CAP)
    query_cells = to_cells(routed_query)
    key_cells = to_cells(routed_key)
    value_cells = to_cells(routed_value)
    scores = (
        jnp.einsum("hcqd,hckd->hcqk", query_cells, key_cells, preferred_element_type=jnp.float32)
        * score_scale
    )
    scores = jnp.where(live[:, :, None, :] > 0.5, scores, masked_score)
    top = jnp.max(scores, axis=-1, keepdims=True)
    weights = jnp.exp(scores - top)
    probs = weights / jnp.sum(weights, axis=-1, keepdims=True)
    probs_low = probs.astype(jnp.bfloat16)
    attended_cells = jnp.einsum(
        "hcqk,hckd->hcqd", probs_low, value_cells, preferred_element_type=jnp.float32
    ).astype(jnp.bfloat16)
    returned = lax.all_to_all(
        to_returns(attended_cells), "seq", split_axis=0, concat_axis=0, tiled=True
    )
    attended = from_buffer(returned)
    full_weight = lax.all_gather(out_weight, "seq", axis=1, tiled=True)
    rows = attended
    mixed = lax.psum_scatter(
        jnp.dot(rows, full_weight, preferred_element_type=jnp.float32).astype(jnp.bfloat16),
        "tensor",
        scatter_dimension=0,
        tiled=True,
    )
    grad_attended = lax.dot_general(
        lax.all_gather(grad_out, "tensor", axis=0, tiled=True),
        full_weight,
        (((1,), (1,)), ((), ())),
        preferred_element_type=jnp.float32,
    )
    grad_low = grad_attended.astype(jnp.bfloat16)
    routed_grad = lax.all_to_all(
        to_buffer(grad_low), "seq", split_axis=0, concat_axis=0, tiled=True
    )
    grad_cells = to_cells(routed_grad)
    backward_low = probs.astype(jnp.bfloat16)
    delta = jnp.einsum(
        "hcqd,hcqd->hcq", grad_cells, attended_cells, preferred_element_type=jnp.float32
    )
    grad_value = jnp.einsum(
        "hcqk,hcqd->hckd", backward_low, grad_cells, preferred_element_type=jnp.float32
    ).astype(jnp.bfloat16)
    grad_probs = jnp.einsum(
        "hcqd,hckd->hcqk", grad_cells, value_cells, preferred_element_type=jnp.float32
    )
    grad_scores = (probs * (grad_probs - delta[..., None])).astype(jnp.bfloat16)
    grad_query = (
        jnp.einsum("hcqk,hckd->hcqd", grad_scores, key_cells, preferred_element_type=jnp.float32)
        * score_scale
    ).astype(jnp.bfloat16)
    grad_key = (
        jnp.einsum("hcqk,hcqd->hckd", grad_scores, query_cells, preferred_element_type=jnp.float32)
        * score_scale
    ).astype(jnp.bfloat16)
    back_query, back_key, back_value = (
        lax.all_to_all(to_returns(grad_query), "seq", split_axis=0, concat_axis=0, tiled=True),
        lax.all_to_all(to_returns(grad_key), "seq", split_axis=0, concat_axis=0, tiled=True),
        lax.all_to_all(to_returns(grad_value), "seq", split_axis=0, concat_axis=0, tiled=True),
    )
    return (mixed, from_buffer(back_query), from_buffer(back_key), from_buffer(back_value))


def by_heads(query_rows, key_rows, value_rows, cluster_id, slot_index, out_weight, grad_out):
    rows_dev, width = query_rows.shape
    heads_dev = cluster_id.shape[0]
    head_size = width // heads_dev
    owners = lax.axis_size("seq")
    high, low = split(owners)
    bf, f32 = jnp.bfloat16, jnp.float32
    together = lax.optimization_barrier

    def exchange(rows):
        return lax.all_to_all(rows, "seq", split_axis=0, concat_axis=0, tiled=True)

    def send(block, bits):
        return lax.ppermute(block, "seq", [(i, i ^ bits) for i in range(owners)])

    def swap(blocks):
        return [blocks[0]] + [send(blocks[k], k) for k in range(1, low)]

    ranks = [
        [r for r in range(1, high) if bin(r).count("1") == count]
        for count in range(1, high.bit_length())
    ]

    def over(block, r):
        return send(block, (r & -r) * low)

    def gather_stack(block):
        blocks = {0: block}
        for rank in ranks:
            blocks |= {r: over(blocks[r & (r - 1)], r) for r in rank}
        return [blocks[r] for r in range(high)]

    def sum_stack(blocks, after):
        blocks = {r: block.astype(f32) for r, block in enumerate(blocks)}
        for rank in ranks[::-1]:
            there = {r: over(blocks.pop(r).astype(bf), r) for r in rank}
            if rank is ranks[0]:
                there, after = together((there, after))
            else:
                there, blocks = together((there, blocks))
            for r, block in there.items():
                blocks[r & (r - 1)] += block.astype(f32)
        return blocks[0].astype(bf), after

    ids = jnp.stack([cluster_id // rows_dev, cluster_id % rows_dev, slot_index])
    ids = ids.reshape(3, high, low, rows_dev).transpose(1, 0, 2, 3).reshape(high, 3 * low, rows_dev)
    ids = jnp.pad(ids, ((0, 0), (0, id_rows(low) - 3 * low), (0, 0))).astype(bf)
    weight = pack_weight(out_weight.T, ids, low)
    weight = [weight[0]] + [send(weight[s], s * low) for s in range(1, high)]
    weight, grad_out = together((weight, grad_out))
    weight = jnp.stack(weight)
    weight = [weight] + [send(weight, k) for k in range(2, low, 2)]
    blocks = gather_stack(grad_out)
    packed = pack((query_rows, key_rows), heads_dev)
    packed_value = pack((value_rows,), heads_dev)
    packed, packed_value, weight, blocks = together((packed, packed_value, weight, blocks))
    arrived = exchange(packed)
    weight = [x for one in weight for x in (one, send(one, 1))]
    grad_heads, rows_of_heads = project_back(weight, blocks)
    grad_heads = swap(grad_heads)
    pos, bias = place(weight, CLU_DEV * owners)
    packed_value, arrived, grad_heads, pos, bias = together(
        (packed_value, arrived, grad_heads, pos, bias)
    )
    value = exchange(packed_value)
    scores, attend, grad_of_value, rest = head_kernels(pos, head_size, low)
    query, key, probs = scores(arrived, bias)
    grad_value, grad_sorted = grad_of_value(grad_heads, probs)
    value, grad_value = together((value, grad_value))
    *attended, att_sorted, value_sorted = attend(value, probs)
    back_value = exchange(grad_value)
    attended = swap(attended)
    grads = rest(grad_sorted, att_sorted, query, key, value_sorted, probs)
    grads, attended = together((grads, attended))
    grads, back_value = together((grads, back_value))
    back = exchange(grads)
    outs = (*unpack(back, 2), *unpack(back_value, 1))
    mixed, outs = sum_stack(project(rows_of_heads, attended, high), outs)
    return (mixed, *outs)


def split(owners):
    high = 1
    while 4 * high * high <= owners:
        high *= 2
    return high, owners // high


def solution(mesh):
    def shards(*args):
        heads_dev = args[3].shape[0]
        owners = lax.axis_size("seq")
        if heads_dev == owners and owners & (owners - 1) == 0 and lax.axis_size("tensor") == 1:
            return by_heads(*args)
        return by_clusters(*args)

    return jax.shard_map(
        shards,
        mesh=mesh,
        in_specs=(
            P("seq", "tensor"),
            P("seq", "tensor"),
            P("seq", "tensor"),
            P("tensor", "seq"),
            P("tensor", "seq"),
            P("tensor", "seq"),
            P(("seq", "tensor"), None),
        ),
        out_specs=(
            P(("seq", "tensor"), None),
            P("seq", "tensor"),
            P("seq", "tensor"),
            P("seq", "tensor"),
        ),
        check_vma=False,
    )
```

```python
import functools
import math

import jax
import jax.numpy as jnp
from jax import lax
from jax.experimental import pallas as pl
from jax.experimental.pallas import tpu as pltpu
from jax.sharding import PartitionSpec as P

CLU_DEV = 8
CAP = 32
TILE = 64
WIN = TILE + 2 * CAP
MASKED = -1e30
UNROLL = 8
VMEM = pl.BlockSpec(memory_space=pltpu.VMEM)
SMEM = pl.BlockSpec(memory_space=pltpu.SMEM)
HBM = pl.BlockSpec(memory_space=pltpu.HBM)
PARAMS = pltpu.CompilerParams(vmem_limit_bytes=61 * 1024 * 1024)
SMALL = pltpu.CompilerParams(vmem_limit_bytes=16 * 1024 * 1024)


def lasts(micros):
    return pl.CostEstimate(flops=0, bytes_accessed=int(micros * 3.5e6), transcendentals=0)


NT = (((1,), (1,)), ((), ()))
TN = (((0,), (0,)), ((), ()))


def run(kernel, operands, outs, scratch, micros, name, late=0):
    where = [SMEM if x.dtype == jnp.int32 else HBM for x in operands]
    held = [pltpu.VMEM(x.shape, x.dtype) for x, spec in zip(operands, where) if spec is HBM]

    def body(*refs):
        given, rest = refs[: len(operands)], refs[len(operands) :]
        slots, sems, rest = rest[-1 - len(held) : -1], rest[-1], rest[: -1 - len(held)]
        copies, arrays = [], []
        for ref, spec in zip(given, where):
            if spec is HBM:
                slot = slots[len(copies)]
                copies.append(pltpu.make_async_copy(ref, slot, sems.at[len(copies)]))
                ref = slot
            arrays.append(ref)
        for copy in copies:
            copy.start()
        now = len(copies) - late
        for copy in copies[:now]:
            copy.wait()
        if late:
            def arrive():
                for copy in copies[now:]:
                    copy.wait()

            kernel(arrive, *arrays, *rest)
        else:
            kernel(*arrays, *rest)

    return pl.pallas_call(
        body,
        out_shape=tuple(jax.ShapeDtypeStruct(shape, kind) for shape, kind in outs),
        in_specs=where,
        out_specs=(VMEM,) * len(outs),
        scratch_shapes=[
            *(pltpu.VMEM(shape, kind) for shape, kind in scratch),
            *held,
            pltpu.SemaphoreType.DMA((len(held),)),
        ],
        compiler_params=PARAMS,
        cost_estimate=lasts(micros),
        name=name,
    )(*operands)


def place_kernel(clusters, low, high, me_ref, *refs):
    parts, (pos_ref, bias_ref, stage, *ids) = refs[:low], refs[low:]
    blocks, lanes = pos_ref.shape
    bf, f32 = jnp.bfloat16, jnp.float32
    cluster_ids = lax.broadcasted_iota(jnp.int32, (clusters, lanes), 0).astype(f32)
    slot_ids = lax.broadcasted_iota(jnp.int32, (CAP, lanes), 0).astype(f32)
    count_rows = stage.shape[0]
    for k in range(low):
        for s in range(high):
            b = (me_ref[1] ^ s) * low + (me_ref[0] ^ k)
            stage[...] = parts[k][s, parts[k].shape[1] - count_rows :, :].astype(f32)
            for kind, ref in enumerate(ids):
                ref[pl.ds(b, 1), :] = stage[pl.ds(kind * low + me_ref[0], 1), :]

    def tables(b):
        cluster = ids[0][pl.ds(b, 1), :] * lanes + ids[1][pl.ds(b, 1), :]
        return (
            jnp.where(cluster_ids == cluster, 1.0, 0.0),
            jnp.where(slot_ids == ids[2][pl.ds(b, 1), :], 1.0, 0.0),
        )

    def count(step, occupied):
        some = [tables(step * 4 + u) for u in range(4)]
        by_cluster = jnp.concatenate([t[0] for t in some], axis=1).astype(bf)
        by_slot = jnp.concatenate([t[1] for t in some], axis=1).astype(bf)
        return occupied + lax.dot_general(
            by_cluster, by_slot, NT, preferred_element_type=f32
        )

    occupied = lax.fori_loop(0, blocks // 4, count, jnp.zeros((clusters, CAP), f32))
    occupied_low = occupied.astype(bf)
    slot_from = lax.broadcasted_iota(jnp.int32, (CAP, CAP), 0)
    slot_to = lax.broadcasted_iota(jnp.int32, (CAP, CAP), 1)
    within = jnp.dot(
        occupied_low, jnp.where(slot_from < slot_to, 1.0, 0.0).astype(bf),
        preferred_element_type=f32,
    )
    size_col = jnp.sum(occupied, axis=1, keepdims=True)
    sizes = jnp.broadcast_to(size_col, (clusters, 128)).astype(bf)
    row_ids = lax.broadcasted_iota(jnp.int32, (clusters, clusters), 0)
    col_ids = lax.broadcasted_iota(jnp.int32, (clusters, clusters), 1)
    before = jnp.where(col_ids < row_ids, 1.0, 0.0).astype(bf)
    start = jnp.dot(before, sizes, preferred_element_type=f32)
    ends_col = start[:, 0:1] + size_col
    upto = jnp.where(row_ids <= col_ids, 1.0, 0.0).astype(bf)
    ends_row = lax.dot_general(
        sizes, upto, (((0,), (0,)), ((), ())), preferred_element_type=f32
    )[0:1]
    high = jnp.floor(start * (1.0 / 64.0))
    low = start - high * 64.0
    lookup = jnp.concatenate([within, high[:, :CAP], low[:, :CAP]], axis=1).astype(bf)

    def find(step, carry):
        some = [tables(step * 4 + u) for u in range(4)]
        found = [
            lax.dot_general(lookup, by_cluster.astype(bf), TN, preferred_element_type=f32)
            for by_cluster, _ in some
        ]
        for u in range(4):
            inner = jnp.sum(found[u][:CAP] * some[u][1], axis=0, keepdims=True)
            outer = found[u][CAP : CAP + 1] * 64.0 + found[u][2 * CAP : 2 * CAP + 1]
            pos_ref[pl.ds(step * 4 + u, 1), :] = (outer + inner).astype(jnp.int32) + CAP
        return carry

    lax.fori_loop(0, blocks // 4, find, 0)
    rows = blocks * lanes

    ones = jnp.ones((clusters, WIN), bf)
    few = jnp.ones((8, clusters), bf)

    def labels(step, carry):
        mines, others = [], []
        for u in range(UNROLL):
            t = step * UNROLL + u
            at = (t * TILE + lax.broadcasted_iota(jnp.int32, (TILE, clusters), 0)).astype(f32)
            ended = jnp.where(ends_row <= at, 1.0, 0.0).astype(bf)
            mines.append(jnp.dot(ended, ones, preferred_element_type=f32))
            wide = t * TILE - CAP + lax.broadcasted_iota(jnp.int32, (clusters, WIN), 1)
            ended = jnp.where(ends_col <= wide.astype(f32), 1.0, 0.0).astype(bf)
            other = jnp.dot(few, ended, preferred_element_type=f32)[0:1]
            spot = wide[0:1]
            others.append(jnp.where((spot >= 0) & (spot < rows), other, -1.0))
        for u in range(UNROLL):
            at = pl.ds(pl.multiple_of((step * UNROLL + u) * TILE, TILE), TILE)
            bias_ref[at, :] = jnp.where(mines[u] == others[u], 0.0, MASKED).astype(bf)
        return carry

    lax.fori_loop(0, rows // TILE // UNROLL, labels, 0)


def id_rows(low):
    return -(-3 * low // 16) * 16


def place(gathered, clusters):
    low, (high, _, lanes) = len(gathered), gathered[0].shape
    f32, blocks = jnp.float32, len(gathered) * high
    return run(
        functools.partial(place_kernel, clusters, low, high), (place_in_plane(low), *gathered),
        (((blocks, lanes), jnp.int32), ((blocks * lanes, WIN), jnp.bfloat16)),
        (((id_rows(low), lanes), f32),) + (((blocks, lanes), f32),) * 3, 8, "place",
    )


ROWS_AT_ONCE = 16


def move_in(pos_ref, block_of, loads, wides, sorted_refs, count):
    lanes = pos_ref.shape[1]

    def one(r, carry):
        b = block_of(r)
        for load, wide in zip(loads, wides):
            wide[...] = load(r).astype(jnp.float32)
        for first in range(0, lanes, ROWS_AT_ONCE):
            rows = range(first, first + ROWS_AT_ONCE)
            places = [pl.ds(pos_ref[b, row], 1) for row in rows]
            held = [[wide[pl.ds(row, 1), :] for row in rows] for wide in wides]
            for i, at in enumerate(places):
                for ref, some in zip(sorted_refs, held):
                    ref[at, :] = some[i]
        return carry

    lax.fori_loop(0, count, one, 0)


def move_out(pos_ref, block_of, sorted_refs, wides, stores, count):
    lanes = pos_ref.shape[1]

    def one(r, carry):
        b = block_of(r)
        for first in range(0, lanes, ROWS_AT_ONCE):
            rows = range(first, first + ROWS_AT_ONCE)
            places = [pl.ds(pos_ref[b, row], 1) for row in rows]
            held = [[ref[at, :] for at in places] for ref in sorted_refs]
            for i, row in enumerate(rows):
                for wide, some in zip(wides, held):
                    wide[pl.ds(row, 1), :] = some[i]
        for store, wide in zip(stores, wides):
            store(r, wide[...])
        return carry

    lax.fori_loop(0, count, one, 0)


def tiles_of(step):
    bases = [pl.multiple_of((step * UNROLL + u) * TILE, TILE) for u in range(UNROLL)]
    tiles = [pl.ds(base, TILE) for base in bases]
    windows = [pl.ds(base, WIN) for base in bases]
    inner = [pl.ds(pl.multiple_of(base + CAP, CAP), TILE) for base in bases]
    return tiles, windows, inner


def scores_kernel(
    scale, arrive, pos_ref, rows_ref, bias_ref, query_ref, key_ref, probs_ref,
    wide, query, key, more,
):
    bf, f32 = jnp.bfloat16, jnp.float32
    blocks, lanes = pos_ref.shape
    rows = blocks * lanes
    edge = jnp.zeros((CAP, wide.shape[1]), f32)
    for ref in (query, key):
        ref[pl.ds(0, CAP), :] = edge
        ref[pl.ds(rows + CAP, CAP), :] = edge
    move_in(
        pos_ref, lambda b: b,
        [lambda b, part=part: rows_ref[b, pl.ds(part * lanes, lanes), :] for part in range(2)],
        [wide, more], [query, key], blocks,
    )
    query_ref[...] = query[...].astype(bf)
    key_ref[...] = key[...].astype(bf)
    arrive()

    def some(step, carry):
        tiles, windows, inner = tiles_of(step)
        qs = [query_ref[at, :] for at in inner]
        ks = [key_ref[at, :] for at in windows]
        biases = [bias_ref[at, :].astype(f32) for at in tiles]
        scores = [lax.dot_general(q, k, NT, preferred_element_type=f32) for q, k in zip(qs, ks)]
        scores = [s * scale + bias for s, bias in zip(scores, biases)]
        tops = [jnp.max(s, axis=1, keepdims=True) for s in scores]
        weights = [jnp.exp(s - top) for s, top in zip(scores, tops)]
        sums = [jnp.sum(w, axis=1, keepdims=True) for w in weights]
        for at, w, total in zip(tiles, weights, sums):
            probs_ref[at, :] = (w / total).astype(bf)
        return carry

    lax.fori_loop(0, rows // TILE // UNROLL, some, 0)


def attend_kernel(
    low, arrive, me_ref, pos_ref, rows_ref, probs_ref, grad_ref, *refs
):
    parts, scores_ref, (wide, value, value_low, att) = refs[:low], refs[low], refs[low + 1 :]
    bf, f32 = jnp.bfloat16, jnp.float32
    blocks, lanes = pos_ref.shape
    rows = blocks * lanes
    high = blocks // low
    edge = jnp.zeros((CAP, wide.shape[1]), f32)
    value[pl.ds(0, CAP), :] = edge
    value[pl.ds(rows + CAP, CAP), :] = edge
    move_in(pos_ref, lambda b: b, [lambda b: rows_ref[b]], [wide], [value], blocks)
    value_low[...] = value[...].astype(bf)
    arrive()

    def some(step, carry):
        tiles, windows, inner = tiles_of(step)
        vs = [value_low[at, :] for at in windows]
        gs = [grad_ref[at, :] for at in tiles]
        probs = [probs_ref[at, :] for at in tiles]
        attended = [jnp.dot(p, v, preferred_element_type=f32) for p, v in zip(probs, vs)]
        grad_probs = [lax.dot_general(g, v, NT, preferred_element_type=f32) for g, v in zip(gs, vs)]
        deltas = [
            jnp.sum(g.astype(f32) * one.astype(bf).astype(f32), axis=1, keepdims=True)
            for g, one in zip(gs, attended)
        ]
        for at, to, one, p, gp, delta in zip(tiles, inner, attended, probs, grad_probs, deltas):
            att[to, :] = one
            scores_ref[at, :] = (p.astype(f32) * (gp - delta)).astype(bf)
        return carry

    lax.fori_loop(0, rows // TILE // UNROLL, some, 0)

    for k in range(low):
        def put(r, block, k=k):
            parts[k][pl.ds(pl.multiple_of(r * lanes, lanes), lanes), :] = block.astype(bf)

        move_out(
            pos_ref, lambda r, k=k: (me_ref[1] ^ r) * low + (me_ref[0] ^ k),
            [att], [wide], [put], high,
        )


def value_kernel(
    low, arrive, me_ref, pos_ref, *refs
):
    parts, (probs_ref, out_ref, sorted_ref, wide, grad, grad_value) = refs[:low], refs[low:]
    bf, f32 = jnp.bfloat16, jnp.float32
    blocks, lanes = pos_ref.shape
    rows = blocks * lanes
    high = blocks // low
    for k in range(low):
        def block_of(r, k=k):
            return (me_ref[1] ^ r) * low + (me_ref[0] ^ k)

        def load(r, k=k):
            return parts[k][pl.ds(pl.multiple_of(r * lanes, lanes), lanes), :]

        move_in(pos_ref, block_of, [load], [wide], [grad], high)
    sorted_ref[...] = grad[pl.ds(CAP, rows), :].astype(bf)
    grad_value[...] = jnp.zeros_like(grad_value)
    arrive()

    def some(step, carry):
        tiles, windows, _ = tiles_of(step)
        gs = [sorted_ref[at, :] for at in tiles]
        probs = [probs_ref[at, :] for at in tiles]
        more = [lax.dot_general(p, g, TN, preferred_element_type=f32) for p, g in zip(probs, gs)]
        for at, one in zip(windows, more):
            grad_value[at, :] += one
        return carry

    lax.fori_loop(0, rows // TILE // UNROLL, some, 0)

    def put(b, block):
        out_ref[b] = block.astype(bf)

    move_out(pos_ref, lambda b: b, [grad_value], [wide], [put], blocks)


def rest_kernel(
    scale, pos_ref, scores_ref, query_ref, key_ref, out_ref, wide, more, grad_query, grad_key
):
    bf, f32 = jnp.bfloat16, jnp.float32
    blocks, lanes = pos_ref.shape
    rows = blocks * lanes
    grad_key[...] = jnp.zeros_like(grad_key)

    def some(step, carry):
        tiles, windows, inner = tiles_of(step)
        ds = [scores_ref[at, :] for at in tiles]
        qs = [query_ref[at, :] for at in inner]
        ks = [key_ref[at, :] for at in windows]
        grad_queries = [jnp.dot(d, k, preferred_element_type=f32) for d, k in zip(ds, ks)]
        more_keys = [
            lax.dot_general(d, q, TN, preferred_element_type=f32) for d, q in zip(ds, qs)
        ]
        for at, one in zip(inner, grad_queries):
            grad_query[at, :] = one
        for at, one in zip(windows, more_keys):
            grad_key[at, :] += one
        return carry

    lax.fori_loop(0, rows // TILE // UNROLL, some, 0)

    def put(part):
        def store(b, block):
            out_ref[b, pl.ds(part * lanes, lanes), :] = (block * scale).astype(bf)
        return store

    move_out(
        pos_ref, lambda b: b, [grad_query, grad_key], [wide, more], [put(0), put(1)], blocks
    )


def project_back_kernel(low, high, columns, me_ref, *refs):
    bf, f32 = jnp.bfloat16, jnp.float32
    gathered, blocks = refs[:low], refs[low : low + high]
    outs, weight_ref, rows_ref = refs[low + high : -2], refs[-2], refs[-1]
    size = gathered[0].shape[2]
    rows = blocks[0].shape[0]
    for r, block in enumerate(blocks):
        rows_ref[pl.ds(r * rows, rows), :] = block[...]
    for k in range(0, low, 2):
        for source in range(low):
            for s in range(high):
                first = ((me_ref[1] ^ s) * low + (me_ref[0] ^ source)) * columns
                at = pl.ds(pl.multiple_of(first, columns), columns)
                for head in (k, k + 1):
                    start = pl.multiple_of((me_ref[0] ^ head) * columns, columns)
                    weight_ref[head, at, :] = gathered[source][s, pl.ds(start, columns), :]
        weight = jnp.concatenate([weight_ref[k], weight_ref[k + 1]], axis=1)
        both = jnp.dot(rows_ref[...], weight, preferred_element_type=f32).astype(bf)
        outs[k][...] = both[:, :size]
        outs[k + 1][...] = both[:, size:]


def project_kernel(low, chunk, weight_ref, *refs):
    bf, f32 = jnp.bfloat16, jnp.float32
    parts, outs = refs[:low], refs[low:]
    rows = jnp.concatenate([ref[...] for ref in parts], axis=1)
    count, columns = outs[0].shape

    def one(c, carry):
        at = pl.ds(pl.multiple_of(c * chunk, chunk), chunk)
        weight = jnp.concatenate([weight_ref[k, at, :] for k in range(low)], axis=1)
        mixed = lax.dot_general(rows, weight, NT, preferred_element_type=f32).astype(bf)
        for r, out in enumerate(outs):
            out[:, at] = mixed[r * count : (r + 1) * count]
        return carry

    lax.fori_loop(0, columns // chunk, one, 0)


def pack_weight_kernel(low, me_ref, weight_ref, ids_ref, *outs):
    size, columns = outs[0].shape[1], weight_ref.shape[0]
    for s, out in enumerate(outs):
        plane = me_ref[1] ^ s
        for h in range(low):
            at = pl.ds(pl.multiple_of((plane * low + h) * size, size), size)
            out[pl.ds(h * columns, columns), :] = weight_ref[:, at]
        out[low * columns :, :] = ids_ref[plane]


def pack_weight(weight, ids, low):
    high, rows, size = ids.shape
    return run(
        functools.partial(pack_weight_kernel, low), (place_in_plane(low), weight, ids),
        (((low * weight.shape[0] + rows, size), weight.dtype),) * high, (), 2, "pack_weight",
    )


def place_in_plane(low):
    index = lax.axis_index("seq")
    return jnp.stack([index % low, index // low]).astype(jnp.int32)


def project_back(gathered, blocks):
    low, high, bf = len(gathered), len(blocks), jnp.bfloat16
    size = gathered[0].shape[-1]
    rows, depth = blocks[0].shape[0] * high, blocks[0].shape[1]
    *heads, weight = run(
        functools.partial(project_back_kernel, low, high, depth // (low * high)),
        (place_in_plane(low), *gathered, *blocks),
        (((rows, size), bf),) * low + (((low, depth, size), bf),),
        (((rows, depth), bf),), 8, "project_back",
    )
    return heads, weight


def project(weight, parts, high):
    low, columns = weight.shape[:2]
    return run(
        functools.partial(project_kernel, low, math.gcd(columns, 512)), (weight, *parts),
        (((parts[0].shape[0] // high, columns), jnp.bfloat16),) * high, (), 6, "project",
    )


def head_kernels(pos, size, low):
    blocks, lanes = pos.shape
    rows = blocks * lanes
    bf, f32 = jnp.bfloat16, jnp.float32
    scale = 1.0 / math.sqrt(size)
    plain, padded, wide = (rows, size), (rows + 2 * CAP, size), (lanes, size)
    me = place_in_plane(low)

    def call(kernel, operands, outs, scratch, micros, name, late=0):
        scratch = [(shape, f32) for shape in (wide, *scratch)]
        return run(kernel, operands, outs, scratch, micros, name, late)

    def scores(query_key, bias):
        return call(
            functools.partial(scores_kernel, scale), (pos, query_key, bias),
            ((padded, bf), (padded, bf), ((rows, WIN), bf)), (padded, padded, wide), 12, "scores", 1,
        )

    def attend(value, probs, grad):
        *attended, scores = run(
            functools.partial(attend_kernel, low), (me, pos, value, probs, grad),
            (((blocks // low * lanes, size), bf),) * low + (((rows, WIN), bf),),
            ((wide, f32), (padded, f32), (padded, bf), (padded, f32)), 12, "attend", 2,
        )
        return attended, scores

    def grad_value(grads, probs):
        return call(
            functools.partial(value_kernel, low), (me, pos, *grads, probs),
            (((blocks, lanes, size), bf), (plain, bf)), (padded, padded), 12, "grad_value", 1,
        )

    def rest(scores, query, key):
        return call(
            functools.partial(rest_kernel, scale), (pos, scores, query, key),
            (((blocks, 2 * lanes, size), bf),), (wide, padded, padded), 12, "rest",
        )[0]

    return scores, attend, grad_value, rest


def pack_kernel(*refs):
    out_ref = refs[-1]
    size = out_ref.shape[2]
    first = 0
    for ref in refs[:-1]:
        rows = ref.shape[-2]
        for h in range(out_ref.shape[0]):
            if len(ref.shape) == 3:
                out_ref[h, pl.ds(first, rows), :] = ref[h]
            else:
                out_ref[h, pl.ds(first, rows), :] = ref[:, pl.ds(h * size, size)]
        first += rows


def pack(arrays, heads):
    rows = sum(array.shape[-2] for array in arrays)
    size = arrays[0].shape[1] // heads
    step = math.gcd(heads, 8)

    def block(array):
        if array.ndim == 3:
            return pl.BlockSpec((step, *array.shape[1:]), lambda i: (i, 0, 0))
        return pl.BlockSpec((array.shape[0], step * size), lambda i: (0, i))

    return pl.pallas_call(
        pack_kernel,
        grid=(heads // step,),
        out_shape=jax.ShapeDtypeStruct((heads, rows, size), arrays[0].dtype),
        in_specs=[block(array) for array in arrays],
        out_specs=pl.BlockSpec((step, rows, size), lambda i: (i, 0, 0)),
        compiler_params=SMALL,
        cost_estimate=lasts(0.1),
        name="pack",
    )(*arrays)


def unpack_kernel(in_ref, *refs):
    heads, rows, size = in_ref.shape
    rows = rows // len(refs)
    for part, ref in enumerate(refs):
        for h in range(heads):
            ref[:, pl.ds(h * size, size)] = in_ref[h, pl.ds(part * rows, rows), :]


def unpack(packed, parts):
    heads, rows, size = packed.shape
    rows = rows // parts
    step = math.gcd(heads, 8)
    return pl.pallas_call(
        unpack_kernel,
        grid=(heads // step,),
        out_shape=(jax.ShapeDtypeStruct((rows, heads * size), packed.dtype),) * parts,
        in_specs=[pl.BlockSpec((step, parts * rows, size), lambda i: (i, 0, 0))],
        out_specs=(pl.BlockSpec((rows, step * size), lambda i: (0, i)),) * parts,
        compiler_params=SMALL,
        cost_estimate=lasts(3),
        name="unpack",
    )(packed)


def by_clusters(query_rows, key_rows, value_rows, cluster_id, slot_index, out_weight, grad_out):
    rows_dev = query_rows.shape[0]
    heads_dev = cluster_id.shape[0]
    head_size = query_rows.shape[1] // heads_dev
    owners = lax.axis_size("seq")
    send_most = 2 * rows_dev // owners
    buffer_rows = owners * send_most
    room = CLU_DEV * CAP
    score_scale = 1.0 / math.sqrt(head_size)
    masked_score = -1e30
    owner = cluster_id // CLU_DEV
    owner_onehot = (owner[:, :, None] == jnp.arange(owners, dtype=jnp.int32)[None, None, :]).astype(
        jnp.bfloat16
    )
    row_ids = jnp.arange(rows_dev, dtype=jnp.int32)
    lower = (row_ids[:, None] > row_ids[None, :]).astype(jnp.bfloat16)
    earlier = jnp.einsum("ij,hjo->hio", lower, owner_onehot, preferred_element_type=jnp.float32)
    rank = jnp.sum(earlier * owner_onehot.astype(jnp.float32), axis=2).astype(jnp.int32)
    place = owner * send_most + rank
    target = cluster_id % CLU_DEV * CAP + slot_index
    buffer_ids = jnp.arange(buffer_rows, dtype=jnp.int32)
    send_table = (place[:, None, :] == buffer_ids[None, :, None]).astype(jnp.bfloat16)

    def to_buffer(rows):
        split = rows.reshape(rows_dev, heads_dev, head_size)
        filled = jnp.einsum(
            "hbi,ihd->bhd", send_table, split, preferred_element_type=jnp.float32
        ).astype(rows.dtype)
        return filled.reshape(buffer_rows, heads_dev * head_size)

    def from_buffer(buffer):
        split = buffer.reshape(buffer_rows, heads_dev, head_size)
        picked = jnp.einsum(
            "hbi,bhd->ihd", send_table, split, preferred_element_type=jnp.float32
        ).astype(buffer.dtype)
        return picked.reshape(rows_dev, heads_dev * head_size)

    target_rows = (
        jnp.einsum(
            "hbi,hi->bh", send_table.astype(jnp.float32), (target - room).astype(jnp.float32)
        ).astype(jnp.int32)
        + room
    )
    arrived = lax.all_to_all(target_rows, "seq", split_axis=0, concat_axis=0, tiled=True)
    routed_query, routed_key, routed_value = (
        lax.all_to_all(to_buffer(query_rows), "seq", split_axis=0, concat_axis=0, tiled=True),
        lax.all_to_all(to_buffer(key_rows), "seq", split_axis=0, concat_axis=0, tiled=True),
        lax.all_to_all(to_buffer(value_rows), "seq", split_axis=0, concat_axis=0, tiled=True),
    )
    room_ids = jnp.arange(room, dtype=jnp.int32)
    cell_table = (arrived.T[:, None, :] == room_ids[None, :, None]).astype(jnp.bfloat16)

    def to_cells(buffer):
        split = buffer.reshape(buffer_rows, heads_dev, head_size)
        cells = jnp.einsum(
            "hrb,bhd->hrd", cell_table, split, preferred_element_type=jnp.float32
        ).astype(buffer.dtype)
        return cells.reshape(heads_dev, CLU_DEV, CAP, head_size)

    def to_returns(cells):
        flat = cells.reshape(heads_dev, room, head_size)
        picked = jnp.einsum(
            "hrb,hrd->bhd", cell_table, flat, preferred_element_type=jnp.float32
        ).astype(cells.dtype)
        return picked.reshape(buffer_rows, heads_dev * head_size)

    live = jnp.sum(cell_table.astype(jnp.float32), axis=2).reshape(heads_dev, CLU_DEV, CAP)
    query_cells = to_cells(routed_query)
    key_cells = to_cells(routed_key)
    value_cells = to_cells(routed_value)
    scores = (
        jnp.einsum("hcqd,hckd->hcqk", query_cells, key_cells, preferred_element_type=jnp.float32)
        * score_scale
    )
    scores = jnp.where(live[:, :, None, :] > 0.5, scores, masked_score)
    top = jnp.max(scores, axis=-1, keepdims=True)
    weights = jnp.exp(scores - top)
    probs = weights / jnp.sum(weights, axis=-1, keepdims=True)
    probs_low = probs.astype(jnp.bfloat16)
    attended_cells = jnp.einsum(
        "hcqk,hckd->hcqd", probs_low, value_cells, preferred_element_type=jnp.float32
    ).astype(jnp.bfloat16)
    returned = lax.all_to_all(
        to_returns(attended_cells), "seq", split_axis=0, concat_axis=0, tiled=True
    )
    attended = from_buffer(returned)
    full_weight = lax.all_gather(out_weight, "seq", axis=1, tiled=True)
    rows = attended
    mixed = lax.psum_scatter(
        jnp.dot(rows, full_weight, preferred_element_type=jnp.float32).astype(jnp.bfloat16),
        "tensor",
        scatter_dimension=0,
        tiled=True,
    )
    grad_attended = lax.dot_general(
        lax.all_gather(grad_out, "tensor", axis=0, tiled=True),
        full_weight,
        (((1,), (1,)), ((), ())),
        preferred_element_type=jnp.float32,
    )
    grad_low = grad_attended.astype(jnp.bfloat16)
    routed_grad = lax.all_to_all(
        to_buffer(grad_low), "seq", split_axis=0, concat_axis=0, tiled=True
    )
    grad_cells = to_cells(routed_grad)
    backward_low = probs.astype(jnp.bfloat16)
    delta = jnp.einsum(
        "hcqd,hcqd->hcq", grad_cells, attended_cells, preferred_element_type=jnp.float32
    )
    grad_value = jnp.einsum(
        "hcqk,hcqd->hckd", backward_low, grad_cells, preferred_element_type=jnp.float32
    ).astype(jnp.bfloat16)
    grad_probs = jnp.einsum(
        "hcqd,hckd->hcqk", grad_cells, value_cells, preferred_element_type=jnp.float32
    )
    grad_scores = (probs * (grad_probs - delta[..., None])).astype(jnp.bfloat16)
    grad_query = (
        jnp.einsum("hcqk,hckd->hcqd", grad_scores, key_cells, preferred_element_type=jnp.float32)
        * score_scale
    ).astype(jnp.bfloat16)
    grad_key = (
        jnp.einsum("hcqk,hcqd->hckd", grad_scores, query_cells, preferred_element_type=jnp.float32)
        * score_scale
    ).astype(jnp.bfloat16)
    back_query, back_key, back_value = (
        lax.all_to_all(to_returns(grad_query), "seq", split_axis=0, concat_axis=0, tiled=True),
        lax.all_to_all(to_returns(grad_key), "seq", split_axis=0, concat_axis=0, tiled=True),
        lax.all_to_all(to_returns(grad_value), "seq", split_axis=0, concat_axis=0, tiled=True),
    )
    return (mixed, from_buffer(back_query), from_buffer(back_key), from_buffer(back_value))


def by_heads(query_rows, key_rows, value_rows, cluster_id, slot_index, out_weight, grad_out):
    rows_dev, width = query_rows.shape
    heads_dev = cluster_id.shape[0]
    head_size = width // heads_dev
    owners = lax.axis_size("seq")
    high, low = split(owners)
    bf, f32 = jnp.bfloat16, jnp.float32
    together = lax.optimization_barrier

    def exchange(rows):
        return lax.all_to_all(rows, "seq", split_axis=0, concat_axis=0, tiled=True)

    def send(block, bits):
        return lax.ppermute(block, "seq", [(i, i ^ bits) for i in range(owners)])

    def swap(blocks):
        return [blocks[0]] + [send(blocks[k], k) for k in range(1, low)]

    ranks = [
        [r for r in range(1, high) if bin(r).count("1") == count]
        for count in range(1, high.bit_length())
    ]

    def over(block, r):
        return send(block, (r & -r) * low)

    def gather_stack(block):
        blocks = {0: block}
        for rank in ranks:
            blocks |= {r: over(blocks[r & (r - 1)], r) for r in rank}
        return [blocks[r] for r in range(high)]

    def sum_stack(blocks, after):
        blocks = {r: block.astype(f32) for r, block in enumerate(blocks)}
        for rank in ranks[::-1]:
            there = {r: over(blocks.pop(r).astype(bf), r) for r in rank}
            if rank is ranks[0]:
                there, after = together((there, after))
            for r, block in there.items():
                blocks[r & (r - 1)] += block.astype(f32)
        return blocks[0].astype(bf), after

    ids = jnp.stack([cluster_id // rows_dev, cluster_id % rows_dev, slot_index])
    ids = ids.reshape(3, high, low, rows_dev).transpose(1, 0, 2, 3).reshape(high, 3 * low, rows_dev)
    ids = jnp.pad(ids, ((0, 0), (0, id_rows(low) - 3 * low), (0, 0))).astype(bf)
    weight = pack_weight(out_weight.T, ids, low)
    weight = [weight[0]] + [send(weight[s], s * low) for s in range(1, high)]
    weight, grad_out = together((weight, grad_out))
    weight = jnp.stack(weight)
    weight = [weight] + [send(weight, k) for k in range(2, low, 2)]
    blocks = gather_stack(grad_out)
    packed = pack((query_rows, key_rows), heads_dev)
    packed_value = pack((value_rows,), heads_dev)
    packed, packed_value, weight, blocks = together((packed, packed_value, weight, blocks))
    arrived = exchange(packed)
    weight = [x for one in weight for x in (one, send(one, 1))]
    grad_heads, rows_of_heads = project_back(weight, blocks)
    grad_heads = swap(grad_heads)
    pos, bias = place(weight, CLU_DEV * owners)
    packed_value, arrived, grad_heads, pos, bias = together(
        (packed_value, arrived, grad_heads, pos, bias)
    )
    value = exchange(packed_value)
    scores, attend, grad_of_value, rest = head_kernels(pos, head_size, low)
    query, key, probs = scores(arrived, bias)
    grad_value, grad_sorted = grad_of_value(grad_heads, probs)
    value, grad_value = together((value, grad_value))
    attended, grad_scores = attend(value, probs, grad_sorted)
    back_value = exchange(grad_value)
    attended = swap(attended)
    grads = rest(grad_scores, query, key)
    grads, attended = together((grads, attended))
    grads, back_value = together((grads, back_value))
    back = exchange(grads)
    outs = (*unpack(back, 2), *unpack(back_value, 1))
    mixed, outs = sum_stack(project(rows_of_heads, attended, high), outs)
    return (mixed, *outs)


def split(owners):
    high = 1
    while 4 * high * high <= owners:
        high *= 2
    return high, owners // high


def solution(mesh):
    def shards(*args):
        heads_dev = args[3].shape[0]
        owners = lax.axis_size("seq")
        if heads_dev == owners and owners & (owners - 1) == 0 and lax.axis_size("tensor") == 1:
            return by_heads(*args)
        return by_clusters(*args)

    return jax.shard_map(
        shards,
        mesh=mesh,
        in_specs=(
            P("seq", "tensor"),
            P("seq", "tensor"),
            P("seq", "tensor"),
            P("tensor", "seq"),
            P("tensor", "seq"),
            P("tensor", "seq"),
            P(("seq", "tensor"), None),
        ),
        out_specs=(
            P(("seq", "tensor"), None),
            P("seq", "tensor"),
            P("seq", "tensor"),
            P("seq", "tensor"),
        ),
        check_vma=False,
    )
```

```python
import functools
import math

import jax
import jax.numpy as jnp
from jax import lax
from jax.experimental import pallas as pl
from jax.experimental.pallas import tpu as pltpu
from jax.sharding import PartitionSpec as P

CLU_DEV = 8
CAP = 32
TILE = 64
WIN = TILE + 2 * CAP
MASKED = -1e30
UNROLL = 8
VMEM = pl.BlockSpec(memory_space=pltpu.VMEM)
SMEM = pl.BlockSpec(memory_space=pltpu.SMEM)
HBM = pl.BlockSpec(memory_space=pltpu.HBM)
PARAMS = pltpu.CompilerParams(vmem_limit_bytes=61 * 1024 * 1024)
SMALL = pltpu.CompilerParams(vmem_limit_bytes=16 * 1024 * 1024)


def lasts(micros):
    return pl.CostEstimate(flops=0, bytes_accessed=int(micros * 3.5e6), transcendentals=0)


NT = (((1,), (1,)), ((), ()))
TN = (((0,), (0,)), ((), ()))


def run(kernel, operands, outs, scratch, micros, name, late=0):
    where = [SMEM if x.dtype == jnp.int32 else HBM for x in operands]
    held = [pltpu.VMEM(x.shape, x.dtype) for x, spec in zip(operands, where) if spec is HBM]

    def body(*refs):
        given, rest = refs[: len(operands)], refs[len(operands) :]
        slots, sems, rest = rest[-1 - len(held) : -1], rest[-1], rest[: -1 - len(held)]
        copies, arrays = [], []
        for ref, spec in zip(given, where):
            if spec is HBM:
                slot = slots[len(copies)]
                copies.append(pltpu.make_async_copy(ref, slot, sems.at[len(copies)]))
                ref = slot
            arrays.append(ref)
        for copy in copies:
            copy.start()
        now = len(copies) - late
        for copy in copies[:now]:
            copy.wait()
        if late:
            def arrive():
                for copy in copies[now:]:
                    copy.wait()

            kernel(arrive, *arrays, *rest)
        else:
            kernel(*arrays, *rest)

    return pl.pallas_call(
        body,
        out_shape=tuple(jax.ShapeDtypeStruct(shape, kind) for shape, kind in outs),
        in_specs=where,
        out_specs=(VMEM,) * len(outs),
        scratch_shapes=[
            *(pltpu.VMEM(shape, kind) for shape, kind in scratch),
            *held,
            pltpu.SemaphoreType.DMA((len(held),)),
        ],
        compiler_params=PARAMS,
        cost_estimate=lasts(micros),
        name=name,
    )(*operands)


def place_kernel(clusters, low, high, me_ref, *refs):
    parts, (pos_ref, bias_ref, stage, *ids) = refs[:low], refs[low:]
    blocks, lanes = pos_ref.shape
    bf, f32 = jnp.bfloat16, jnp.float32
    cluster_ids = lax.broadcasted_iota(jnp.int32, (clusters, lanes), 0).astype(f32)
    slot_ids = lax.broadcasted_iota(jnp.int32, (CAP, lanes), 0).astype(f32)
    count_rows = stage.shape[0]
    for k in range(low):
        for s in range(high):
            b = (me_ref[1] ^ s) * low + (me_ref[0] ^ k)
            stage[...] = parts[k][s, parts[k].shape[1] - count_rows :, :].astype(f32)
            for kind, ref in enumerate(ids):
                ref[pl.ds(b, 1), :] = stage[pl.ds(kind * low + me_ref[0], 1), :]

    def tables(b):
        cluster = ids[0][pl.ds(b, 1), :] * lanes + ids[1][pl.ds(b, 1), :]
        return (
            jnp.where(cluster_ids == cluster, 1.0, 0.0),
            jnp.where(slot_ids == ids[2][pl.ds(b, 1), :], 1.0, 0.0),
        )

    def count(step, occupied):
        some = [tables(step * 4 + u) for u in range(4)]
        by_cluster = jnp.concatenate([t[0] for t in some], axis=1).astype(bf)
        by_slot = jnp.concatenate([t[1] for t in some], axis=1).astype(bf)
        return occupied + lax.dot_general(
            by_cluster, by_slot, NT, preferred_element_type=f32
        )

    occupied = lax.fori_loop(0, blocks // 4, count, jnp.zeros((clusters, CAP), f32))
    occupied_low = occupied.astype(bf)
    slot_from = lax.broadcasted_iota(jnp.int32, (CAP, CAP), 0)
    slot_to = lax.broadcasted_iota(jnp.int32, (CAP, CAP), 1)
    within = jnp.dot(
        occupied_low, jnp.where(slot_from < slot_to, 1.0, 0.0).astype(bf),
        preferred_element_type=f32,
    )
    size_col = jnp.sum(occupied, axis=1, keepdims=True)
    sizes = jnp.broadcast_to(size_col, (clusters, 128)).astype(bf)
    row_ids = lax.broadcasted_iota(jnp.int32, (clusters, clusters), 0)
    col_ids = lax.broadcasted_iota(jnp.int32, (clusters, clusters), 1)
    before = jnp.where(col_ids < row_ids, 1.0, 0.0).astype(bf)
    start = jnp.dot(before, sizes, preferred_element_type=f32)
    ends_col = start[:, 0:1] + size_col
    upto = jnp.where(row_ids <= col_ids, 1.0, 0.0).astype(bf)
    ends_row = lax.dot_general(
        sizes, upto, (((0,), (0,)), ((), ())), preferred_element_type=f32
    )[0:1]
    high = jnp.floor(start * (1.0 / 64.0))
    low = start - high * 64.0
    lookup = jnp.concatenate([within, high[:, :CAP], low[:, :CAP]], axis=1).astype(bf)

    def find(step, carry):
        some = [tables(step * 4 + u) for u in range(4)]
        found = [
            lax.dot_general(lookup, by_cluster.astype(bf), TN, preferred_element_type=f32)
            for by_cluster, _ in some
        ]
        for u in range(4):
            inner = jnp.sum(found[u][:CAP] * some[u][1], axis=0, keepdims=True)
            outer = found[u][CAP : CAP + 1] * 64.0 + found[u][2 * CAP : 2 * CAP + 1]
            pos_ref[pl.ds(step * 4 + u, 1), :] = (outer + inner).astype(jnp.int32) + CAP
        return carry

    lax.fori_loop(0, blocks // 4, find, 0)
    rows = blocks * lanes

    ones = jnp.ones((clusters, WIN), bf)
    few = jnp.ones((8, clusters), bf)

    def labels(step, carry):
        mines, others = [], []
        for u in range(UNROLL):
            t = step * UNROLL + u
            at = (t * TILE + lax.broadcasted_iota(jnp.int32, (TILE, clusters), 0)).astype(f32)
            ended = jnp.where(ends_row <= at, 1.0, 0.0).astype(bf)
            mines.append(jnp.dot(ended, ones, preferred_element_type=f32))
            wide = t * TILE - CAP + lax.broadcasted_iota(jnp.int32, (clusters, WIN), 1)
            ended = jnp.where(ends_col <= wide.astype(f32), 1.0, 0.0).astype(bf)
            other = jnp.dot(few, ended, preferred_element_type=f32)[0:1]
            spot = wide[0:1]
            others.append(jnp.where((spot >= 0) & (spot < rows), other, -1.0))
        for u in range(UNROLL):
            at = pl.ds(pl.multiple_of((step * UNROLL + u) * TILE, TILE), TILE)
            bias_ref[at, :] = jnp.where(mines[u] == others[u], 0.0, MASKED).astype(bf)
        return carry

    lax.fori_loop(0, rows // TILE // UNROLL, labels, 0)


def id_rows(low):
    return -(-3 * low // 16) * 16


def place(gathered, clusters):
    low, (high, _, lanes) = len(gathered), gathered[0].shape
    f32, blocks = jnp.float32, len(gathered) * high
    return run(
        functools.partial(place_kernel, clusters, low, high), (place_in_plane(low), *gathered),
        (((blocks, lanes), jnp.int32), ((blocks * lanes, WIN), jnp.bfloat16)),
        (((id_rows(low), lanes), f32),) + (((blocks, lanes), f32),) * 3, 8, "place",
    )


ROWS_AT_ONCE = 16


def move_in(pos_ref, block_of, loads, wides, sorted_refs, count):
    lanes = pos_ref.shape[1]

    def two(step, carry):
        for half in range(2):
            for load, wide in zip(loads, wides):
                wide[pl.ds(half * lanes, lanes), :] = load(step * 2 + half).astype(jnp.float32)
        for half in range(2):
            b = block_of(step * 2 + half)
            for first in range(0, lanes, ROWS_AT_ONCE):
                rows = range(first, first + ROWS_AT_ONCE)
                places = [pl.ds(pos_ref[b, row], 1) for row in rows]
                held = [[wide[pl.ds(half * lanes + row, 1), :] for row in rows] for wide in wides]
                for i, at in enumerate(places):
                    for ref, some in zip(sorted_refs, held):
                        ref[at, :] = some[i]
        return carry

    lax.fori_loop(0, count // 2, two, 0)


def move_out(pos_ref, block_of, sorted_refs, wides, stores, count):
    lanes = pos_ref.shape[1]

    def two(step, carry):
        for half in range(2):
            b = block_of(step * 2 + half)
            for first in range(0, lanes, ROWS_AT_ONCE):
                rows = range(first, first + ROWS_AT_ONCE)
                places = [pl.ds(pos_ref[b, row], 1) for row in rows]
                held = [[ref[at, :] for at in places] for ref in sorted_refs]
                for i, row in enumerate(rows):
                    for wide, some in zip(wides, held):
                        wide[pl.ds(half * lanes + row, 1), :] = some[i]
        for half in range(2):
            for store, wide in zip(stores, wides):
                store(step * 2 + half, wide[pl.ds(half * lanes, lanes), :])
        return carry

    lax.fori_loop(0, count // 2, two, 0)


def tiles_of(step):
    bases = [pl.multiple_of((step * UNROLL + u) * TILE, TILE) for u in range(UNROLL)]
    tiles = [pl.ds(base, TILE) for base in bases]
    windows = [pl.ds(base, WIN) for base in bases]
    inner = [pl.ds(pl.multiple_of(base + CAP, CAP), TILE) for base in bases]
    return tiles, windows, inner


def scores_kernel(
    scale, arrive, pos_ref, rows_ref, bias_ref, query_ref, key_ref, probs_ref,
    wide, query, key, more,
):
    bf, f32 = jnp.bfloat16, jnp.float32
    blocks, lanes = pos_ref.shape
    rows = blocks * lanes
    edge = jnp.zeros((CAP, wide.shape[1]), f32)
    for ref in (query, key):
        ref[pl.ds(0, CAP), :] = edge
        ref[pl.ds(rows + CAP, CAP), :] = edge
    move_in(
        pos_ref, lambda b: b,
        [lambda b, part=part: rows_ref[b, pl.ds(part * lanes, lanes), :] for part in range(2)],
        [wide, more], [query, key], blocks,
    )
    query_ref[...] = query[...].astype(bf)
    key_ref[...] = key[...].astype(bf)
    arrive()

    def some(step, carry):
        tiles, windows, inner = tiles_of(step)
        qs = [query_ref[at, :] for at in inner]
        ks = [key_ref[at, :] for at in windows]
        biases = [bias_ref[at, :].astype(f32) for at in tiles]
        scores = [lax.dot_general(q, k, NT, preferred_element_type=f32) for q, k in zip(qs, ks)]
        scores = [s * scale + bias for s, bias in zip(scores, biases)]
        tops = [jnp.max(s, axis=1, keepdims=True) for s in scores]
        weights = [jnp.exp(s - top) for s, top in zip(scores, tops)]
        sums = [jnp.sum(w, axis=1, keepdims=True) for w in weights]
        for at, w, total in zip(tiles, weights, sums):
            probs_ref[at, :] = (w / total).astype(bf)
        return carry

    lax.fori_loop(0, rows // TILE // UNROLL, some, 0)


def attend_kernel(
    low, arrive, me_ref, pos_ref, rows_ref, probs_ref, grad_ref, *refs
):
    parts, scores_ref, (wide, value, value_low, att) = refs[:low], refs[low], refs[low + 1 :]
    bf, f32 = jnp.bfloat16, jnp.float32
    blocks, lanes = pos_ref.shape
    rows = blocks * lanes
    high = blocks // low
    edge = jnp.zeros((CAP, wide.shape[1]), f32)
    value[pl.ds(0, CAP), :] = edge
    value[pl.ds(rows + CAP, CAP), :] = edge
    move_in(pos_ref, lambda b: b, [lambda b: rows_ref[b]], [wide], [value], blocks)
    value_low[...] = value[...].astype(bf)
    arrive()

    def some(step, carry):
        tiles, windows, inner = tiles_of(step)
        vs = [value_low[at, :] for at in windows]
        gs = [grad_ref[at, :] for at in tiles]
        probs = [probs_ref[at, :] for at in tiles]
        attended = [jnp.dot(p, v, preferred_element_type=f32) for p, v in zip(probs, vs)]
        grad_probs = [lax.dot_general(g, v, NT, preferred_element_type=f32) for g, v in zip(gs, vs)]
        deltas = [
            jnp.sum(g.astype(f32) * one.astype(bf).astype(f32), axis=1, keepdims=True)
            for g, one in zip(gs, attended)
        ]
        for at, to, one, p, gp, delta in zip(tiles, inner, attended, probs, grad_probs, deltas):
            att[to, :] = one
            scores_ref[at, :] = (p.astype(f32) * (gp - delta)).astype(bf)
        return carry

    lax.fori_loop(0, rows // TILE // UNROLL, some, 0)

    for k in range(low):
        def put(r, block, k=k):
            parts[k][pl.ds(pl.multiple_of(r * lanes, lanes), lanes), :] = block.astype(bf)

        move_out(
            pos_ref, lambda r, k=k: (me_ref[1] ^ r) * low + (me_ref[0] ^ k),
            [att], [wide], [put], high,
        )


def value_kernel(
    low, arrive, me_ref, pos_ref, *refs
):
    parts, (probs_ref, out_ref, sorted_ref, wide, grad, grad_value) = refs[:low], refs[low:]
    bf, f32 = jnp.bfloat16, jnp.float32
    blocks, lanes = pos_ref.shape
    rows = blocks * lanes
    high = blocks // low
    for k in range(low):
        def block_of(r, k=k):
            return (me_ref[1] ^ r) * low + (me_ref[0] ^ k)

        def load(r, k=k):
            return parts[k][pl.ds(pl.multiple_of(r * lanes, lanes), lanes), :]

        move_in(pos_ref, block_of, [load], [wide], [grad], high)
    sorted_ref[...] = grad[pl.ds(CAP, rows), :].astype(bf)
    grad_value[...] = jnp.zeros_like(grad_value)
    arrive()

    def some(step, carry):
        tiles, windows, _ = tiles_of(step)
        gs = [sorted_ref[at, :] for at in tiles]
        probs = [probs_ref[at, :] for at in tiles]
        more = [lax.dot_general(p, g, TN, preferred_element_type=f32) for p, g in zip(probs, gs)]
        for at, one in zip(windows, more):
            grad_value[at, :] += one
        return carry

    lax.fori_loop(0, rows // TILE // UNROLL, some, 0)

    def put(b, block):
        out_ref[b] = block.astype(bf)

    move_out(pos_ref, lambda b: b, [grad_value], [wide], [put], blocks)


def rest_kernel(
    scale, pos_ref, scores_ref, query_ref, key_ref, out_ref, wide, more, grad_query, grad_key
):
    bf, f32 = jnp.bfloat16, jnp.float32
    blocks, lanes = pos_ref.shape
    rows = blocks * lanes
    grad_key[...] = jnp.zeros_like(grad_key)

    def some(step, carry):
        tiles, windows, inner = tiles_of(step)
        ds = [scores_ref[at, :] for at in tiles]
        qs = [query_ref[at, :] for at in inner]
        ks = [key_ref[at, :] for at in windows]
        grad_queries = [jnp.dot(d, k, preferred_element_type=f32) for d, k in zip(ds, ks)]
        more_keys = [
            lax.dot_general(d, q, TN, preferred_element_type=f32) for d, q in zip(ds, qs)
        ]
        for at, one in zip(inner, grad_queries):
            grad_query[at, :] = one
        for at, one in zip(windows, more_keys):
            grad_key[at, :] += one
        return carry

    lax.fori_loop(0, rows // TILE // UNROLL, some, 0)

    def put(part):
        def store(b, block):
            out_ref[b, pl.ds(part * lanes, lanes), :] = (block * scale).astype(bf)
        return store

    move_out(
        pos_ref, lambda b: b, [grad_query, grad_key], [wide, more], [put(0), put(1)], blocks
    )


def project_back_kernel(low, high, columns, me_ref, *refs):
    bf, f32 = jnp.bfloat16, jnp.float32
    gathered, blocks = refs[:low], refs[low : low + high]
    outs, weight_ref, rows_ref = refs[low + high : -2], refs[-2], refs[-1]
    size = gathered[0].shape[2]
    rows = blocks[0].shape[0]
    for r, block in enumerate(blocks):
        rows_ref[pl.ds(r * rows, rows), :] = block[...]
    for k in range(0, low, 2):
        for source in range(low):
            for s in range(high):
                first = ((me_ref[1] ^ s) * low + (me_ref[0] ^ source)) * columns
                at = pl.ds(pl.multiple_of(first, columns), columns)
                for head in (k, k + 1):
                    start = pl.multiple_of((me_ref[0] ^ head) * columns, columns)
                    weight_ref[head, at, :] = gathered[source][s, pl.ds(start, columns), :]
        weight = jnp.concatenate([weight_ref[k], weight_ref[k + 1]], axis=1)
        both = jnp.dot(rows_ref[...], weight, preferred_element_type=f32).astype(bf)
        outs[k][...] = both[:, :size]
        outs[k + 1][...] = both[:, size:]


def project_kernel(low, chunk, weight_ref, *refs):
    bf, f32 = jnp.bfloat16, jnp.float32
    parts, outs = refs[:low], refs[low:]
    rows = jnp.concatenate([ref[...] for ref in parts], axis=1)
    count, columns = outs[0].shape

    def one(c, carry):
        at = pl.ds(pl.multiple_of(c * chunk, chunk), chunk)
        weight = jnp.concatenate([weight_ref[k, at, :] for k in range(low)], axis=1)
        mixed = lax.dot_general(rows, weight, NT, preferred_element_type=f32).astype(bf)
        for r, out in enumerate(outs):
            out[:, at] = mixed[r * count : (r + 1) * count]
        return carry

    lax.fori_loop(0, columns // chunk, one, 0)


def pack_weight_kernel(low, me_ref, weight_ref, ids_ref, *outs):
    size, columns = outs[0].shape[1], weight_ref.shape[0]
    for s, out in enumerate(outs):
        plane = me_ref[1] ^ s
        for h in range(low):
            at = pl.ds(pl.multiple_of((plane * low + h) * size, size), size)
            out[pl.ds(h * columns, columns), :] = weight_ref[:, at]
        out[low * columns :, :] = ids_ref[plane]


def pack_weight(weight, ids, low):
    high, rows, size = ids.shape
    return run(
        functools.partial(pack_weight_kernel, low), (place_in_plane(low), weight, ids),
        (((low * weight.shape[0] + rows, size), weight.dtype),) * high, (), 2, "pack_weight",
    )


def place_in_plane(low):
    index = lax.axis_index("seq")
    return jnp.stack([index % low, index // low]).astype(jnp.int32)


def project_back(gathered, blocks):
    low, high, bf = len(gathered), len(blocks), jnp.bfloat16
    size = gathered[0].shape[-1]
    rows, depth = blocks[0].shape[0] * high, blocks[0].shape[1]
    *heads, weight = run(
        functools.partial(project_back_kernel, low, high, depth // (low * high)),
        (place_in_plane(low), *gathered, *blocks),
        (((rows, size), bf),) * low + (((low, depth, size), bf),),
        (((rows, depth), bf),), 8, "project_back",
    )
    return heads, weight


def project(weight, parts, high):
    low, columns = weight.shape[:2]
    return run(
        functools.partial(project_kernel, low, math.gcd(columns, 512)), (weight, *parts),
        (((parts[0].shape[0] // high, columns), jnp.bfloat16),) * high, (), 6, "project",
    )


def head_kernels(pos, size, low):
    blocks, lanes = pos.shape
    rows = blocks * lanes
    bf, f32 = jnp.bfloat16, jnp.float32
    scale = 1.0 / math.sqrt(size)
    plain, padded, wide = (rows, size), (rows + 2 * CAP, size), (2 * lanes, size)
    me = place_in_plane(low)

    def call(kernel, operands, outs, scratch, micros, name, late=0):
        scratch = [(shape, f32) for shape in (wide, *scratch)]
        return run(kernel, operands, outs, scratch, micros, name, late)

    def scores(query_key, bias):
        return call(
            functools.partial(scores_kernel, scale), (pos, query_key, bias),
            ((padded, bf), (padded, bf), ((rows, WIN), bf)), (padded, padded, wide), 12, "scores", 1,
        )

    def attend(value, probs, grad):
        *attended, scores = run(
            functools.partial(attend_kernel, low), (me, pos, value, probs, grad),
            (((blocks // low * lanes, size), bf),) * low + (((rows, WIN), bf),),
            ((wide, f32), (padded, f32), (padded, bf), (padded, f32)), 12, "attend", 2,
        )
        return attended, scores

    def grad_value(grads, probs):
        return call(
            functools.partial(value_kernel, low), (me, pos, *grads, probs),
            (((blocks, lanes, size), bf), (plain, bf)), (padded, padded), 12, "grad_value", 1,
        )

    def rest(scores, query, key):
        return call(
            functools.partial(rest_kernel, scale), (pos, scores, query, key),
            (((blocks, 2 * lanes, size), bf),), (wide, padded, padded), 12, "rest",
        )[0]

    return scores, attend, grad_value, rest


def pack_kernel(*refs):
    out_ref = refs[-1]
    size = out_ref.shape[2]
    first = 0
    for ref in refs[:-1]:
        rows = ref.shape[-2]
        for h in range(out_ref.shape[0]):
            if len(ref.shape) == 3:
                out_ref[h, pl.ds(first, rows), :] = ref[h]
            else:
                out_ref[h, pl.ds(first, rows), :] = ref[:, pl.ds(h * size, size)]
        first += rows


def pack(arrays, heads):
    rows = sum(array.shape[-2] for array in arrays)
    size = arrays[0].shape[1] // heads
    step = math.gcd(heads, 8)

    def block(array):
        if array.ndim == 3:
            return pl.BlockSpec((step, *array.shape[1:]), lambda i: (i, 0, 0))
        return pl.BlockSpec((array.shape[0], step * size), lambda i: (0, i))

    return pl.pallas_call(
        pack_kernel,
        grid=(heads // step,),
        out_shape=jax.ShapeDtypeStruct((heads, rows, size), arrays[0].dtype),
        in_specs=[block(array) for array in arrays],
        out_specs=pl.BlockSpec((step, rows, size), lambda i: (i, 0, 0)),
        compiler_params=SMALL,
        cost_estimate=lasts(0.1),
        name="pack",
    )(*arrays)


def unpack_kernel(in_ref, *refs):
    heads, rows, size = in_ref.shape
    rows = rows // len(refs)
    for part, ref in enumerate(refs):
        for h in range(heads):
            ref[:, pl.ds(h * size, size)] = in_ref[h, pl.ds(part * rows, rows), :]


def unpack(packed, parts):
    heads, rows, size = packed.shape
    rows = rows // parts
    step = math.gcd(heads, 8)
    return pl.pallas_call(
        unpack_kernel,
        grid=(heads // step,),
        out_shape=(jax.ShapeDtypeStruct((rows, heads * size), packed.dtype),) * parts,
        in_specs=[pl.BlockSpec((step, parts * rows, size), lambda i: (i, 0, 0))],
        out_specs=(pl.BlockSpec((rows, step * size), lambda i: (0, i)),) * parts,
        compiler_params=SMALL,
        cost_estimate=lasts(3),
        name="unpack",
    )(packed)


def by_clusters(query_rows, key_rows, value_rows, cluster_id, slot_index, out_weight, grad_out):
    rows_dev = query_rows.shape[0]
    heads_dev = cluster_id.shape[0]
    head_size = query_rows.shape[1] // heads_dev
    owners = lax.axis_size("seq")
    send_most = 2 * rows_dev // owners
    buffer_rows = owners * send_most
    room = CLU_DEV * CAP
    score_scale = 1.0 / math.sqrt(head_size)
    masked_score = -1e30
    owner = cluster_id // CLU_DEV
    owner_onehot = (owner[:, :, None] == jnp.arange(owners, dtype=jnp.int32)[None, None, :]).astype(
        jnp.bfloat16
    )
    row_ids = jnp.arange(rows_dev, dtype=jnp.int32)
    lower = (row_ids[:, None] > row_ids[None, :]).astype(jnp.bfloat16)
    earlier = jnp.einsum("ij,hjo->hio", lower, owner_onehot, preferred_element_type=jnp.float32)
    rank = jnp.sum(earlier * owner_onehot.astype(jnp.float32), axis=2).astype(jnp.int32)
    place = owner * send_most + rank
    target = cluster_id % CLU_DEV * CAP + slot_index
    buffer_ids = jnp.arange(buffer_rows, dtype=jnp.int32)
    send_table = (place[:, None, :] == buffer_ids[None, :, None]).astype(jnp.bfloat16)

    def to_buffer(rows):
        split = rows.reshape(rows_dev, heads_dev, head_size)
        filled = jnp.einsum(
            "hbi,ihd->bhd", send_table, split, preferred_element_type=jnp.float32
        ).astype(rows.dtype)
        return filled.reshape(buffer_rows, heads_dev * head_size)

    def from_buffer(buffer):
        split = buffer.reshape(buffer_rows, heads_dev, head_size)
        picked = jnp.einsum(
            "hbi,bhd->ihd", send_table, split, preferred_element_type=jnp.float32
        ).astype(buffer.dtype)
        return picked.reshape(rows_dev, heads_dev * head_size)

    target_rows = (
        jnp.einsum(
            "hbi,hi->bh", send_table.astype(jnp.float32), (target - room).astype(jnp.float32)
        ).astype(jnp.int32)
        + room
    )
    arrived = lax.all_to_all(target_rows, "seq", split_axis=0, concat_axis=0, tiled=True)
    routed_query, routed_key, routed_value = (
        lax.all_to_all(to_buffer(query_rows), "seq", split_axis=0, concat_axis=0, tiled=True),
        lax.all_to_all(to_buffer(key_rows), "seq", split_axis=0, concat_axis=0, tiled=True),
        lax.all_to_all(to_buffer(value_rows), "seq", split_axis=0, concat_axis=0, tiled=True),
    )
    room_ids = jnp.arange(room, dtype=jnp.int32)
    cell_table = (arrived.T[:, None, :] == room_ids[None, :, None]).astype(jnp.bfloat16)

    def to_cells(buffer):
        split = buffer.reshape(buffer_rows, heads_dev, head_size)
        cells = jnp.einsum(
            "hrb,bhd->hrd", cell_table, split, preferred_element_type=jnp.float32
        ).astype(buffer.dtype)
        return cells.reshape(heads_dev, CLU_DEV, CAP, head_size)

    def to_returns(cells):
        flat = cells.reshape(heads_dev, room, head_size)
        picked = jnp.einsum(
            "hrb,hrd->bhd", cell_table, flat, preferred_element_type=jnp.float32
        ).astype(cells.dtype)
        return picked.reshape(buffer_rows, heads_dev * head_size)

    live = jnp.sum(cell_table.astype(jnp.float32), axis=2).reshape(heads_dev, CLU_DEV, CAP)
    query_cells = to_cells(routed_query)
    key_cells = to_cells(routed_key)
    value_cells = to_cells(routed_value)
    scores = (
        jnp.einsum("hcqd,hckd->hcqk", query_cells, key_cells, preferred_element_type=jnp.float32)
        * score_scale
    )
    scores = jnp.where(live[:, :, None, :] > 0.5, scores, masked_score)
    top = jnp.max(scores, axis=-1, keepdims=True)
    weights = jnp.exp(scores - top)
    probs = weights / jnp.sum(weights, axis=-1, keepdims=True)
    probs_low = probs.astype(jnp.bfloat16)
    attended_cells = jnp.einsum(
        "hcqk,hckd->hcqd", probs_low, value_cells, preferred_element_type=jnp.float32
    ).astype(jnp.bfloat16)
    returned = lax.all_to_all(
        to_returns(attended_cells), "seq", split_axis=0, concat_axis=0, tiled=True
    )
    attended = from_buffer(returned)
    full_weight = lax.all_gather(out_weight, "seq", axis=1, tiled=True)
    rows = attended
    mixed = lax.psum_scatter(
        jnp.dot(rows, full_weight, preferred_element_type=jnp.float32).astype(jnp.bfloat16),
        "tensor",
        scatter_dimension=0,
        tiled=True,
    )
    grad_attended = lax.dot_general(
        lax.all_gather(grad_out, "tensor", axis=0, tiled=True),
        full_weight,
        (((1,), (1,)), ((), ())),
        preferred_element_type=jnp.float32,
    )
    grad_low = grad_attended.astype(jnp.bfloat16)
    routed_grad = lax.all_to_all(
        to_buffer(grad_low), "seq", split_axis=0, concat_axis=0, tiled=True
    )
    grad_cells = to_cells(routed_grad)
    backward_low = probs.astype(jnp.bfloat16)
    delta = jnp.einsum(
        "hcqd,hcqd->hcq", grad_cells, attended_cells, preferred_element_type=jnp.float32
    )
    grad_value = jnp.einsum(
        "hcqk,hcqd->hckd", backward_low, grad_cells, preferred_element_type=jnp.float32
    ).astype(jnp.bfloat16)
    grad_probs = jnp.einsum(
        "hcqd,hckd->hcqk", grad_cells, value_cells, preferred_element_type=jnp.float32
    )
    grad_scores = (probs * (grad_probs - delta[..., None])).astype(jnp.bfloat16)
    grad_query = (
        jnp.einsum("hcqk,hckd->hcqd", grad_scores, key_cells, preferred_element_type=jnp.float32)
        * score_scale
    ).astype(jnp.bfloat16)
    grad_key = (
        jnp.einsum("hcqk,hcqd->hckd", grad_scores, query_cells, preferred_element_type=jnp.float32)
        * score_scale
    ).astype(jnp.bfloat16)
    back_query, back_key, back_value = (
        lax.all_to_all(to_returns(grad_query), "seq", split_axis=0, concat_axis=0, tiled=True),
        lax.all_to_all(to_returns(grad_key), "seq", split_axis=0, concat_axis=0, tiled=True),
        lax.all_to_all(to_returns(grad_value), "seq", split_axis=0, concat_axis=0, tiled=True),
    )
    return (mixed, from_buffer(back_query), from_buffer(back_key), from_buffer(back_value))


def by_heads(query_rows, key_rows, value_rows, cluster_id, slot_index, out_weight, grad_out):
    rows_dev, width = query_rows.shape
    heads_dev = cluster_id.shape[0]
    head_size = width // heads_dev
    owners = lax.axis_size("seq")
    high, low = split(owners)
    bf, f32 = jnp.bfloat16, jnp.float32
    together = lax.optimization_barrier

    def exchange(rows):
        return lax.all_to_all(rows, "seq", split_axis=0, concat_axis=0, tiled=True)

    def send(block, bits):
        return lax.ppermute(block, "seq", [(i, i ^ bits) for i in range(owners)])

    def swap(blocks):
        return [blocks[0]] + [send(blocks[k], k) for k in range(1, low)]

    ranks = [
        [r for r in range(1, high) if bin(r).count("1") == count]
        for count in range(1, high.bit_length())
    ]

    def over(block, r):
        return send(block, (r & -r) * low)

    def gather_stack(block):
        blocks = {0: block}
        for rank in ranks:
            blocks |= {r: over(blocks[r & (r - 1)], r) for r in rank}
        return [blocks[r] for r in range(high)]

    def sum_stack(blocks, after):
        blocks = {r: block.astype(f32) for r, block in enumerate(blocks)}
        for rank in ranks[::-1]:
            there = {r: over(blocks.pop(r).astype(bf), r) for r in rank}
            if rank is ranks[0]:
                there, after = together((there, after))
            for r, block in there.items():
                blocks[r & (r - 1)] += block.astype(f32)
        return blocks[0].astype(bf), after

    ids = jnp.stack([cluster_id // rows_dev, cluster_id % rows_dev, slot_index])
    ids = ids.reshape(3, high, low, rows_dev).transpose(1, 0, 2, 3).reshape(high, 3 * low, rows_dev)
    ids = jnp.pad(ids, ((0, 0), (0, id_rows(low) - 3 * low), (0, 0))).astype(bf)
    weight = pack_weight(out_weight.T, ids, low)
    weight = [weight[0]] + [send(weight[s], s * low) for s in range(1, high)]
    weight, grad_out = together((weight, grad_out))
    weight = jnp.stack(weight)
    weight = [weight] + [send(weight, k) for k in range(2, low, 2)]
    blocks = gather_stack(grad_out)
    packed = pack((query_rows, key_rows), heads_dev)
    packed_value = pack((value_rows,), heads_dev)
    packed, packed_value, weight, blocks = together((packed, packed_value, weight, blocks))
    arrived = exchange(packed)
    weight = [x for one in weight for x in (one, send(one, 1))]
    grad_heads, rows_of_heads = project_back(weight, blocks)
    grad_heads = swap(grad_heads)
    pos, bias = place(weight, CLU_DEV * owners)
    packed_value, arrived, grad_heads, pos, bias = together(
        (packed_value, arrived, grad_heads, pos, bias)
    )
    value = exchange(packed_value)
    scores, attend, grad_of_value, rest = head_kernels(pos, head_size, low)
    query, key, probs = scores(arrived, bias)
    grad_value, grad_sorted = grad_of_value(grad_heads, probs)
    value, grad_value = together((value, grad_value))
    attended, grad_scores = attend(value, probs, grad_sorted)
    back_value = exchange(grad_value)
    attended = swap(attended)
    grads = rest(grad_scores, query, key)
    grads, attended = together((grads, attended))
    grads, back_value = together((grads, back_value))
    back = exchange(grads)
    outs = (*unpack(back, 2), *unpack(back_value, 1))
    mixed, outs = sum_stack(project(rows_of_heads, attended, high), outs)
    return (mixed, *outs)


def split(owners):
    high = 1
    while 4 * high * high <= owners:
        high *= 2
    return high, owners // high


def solution(mesh):
    def shards(*args):
        heads_dev = args[3].shape[0]
        owners = lax.axis_size("seq")
        if heads_dev == owners and owners & (owners - 1) == 0 and lax.axis_size("tensor") == 1:
            return by_heads(*args)
        return by_clusters(*args)

    return jax.shard_map(
        shards,
        mesh=mesh,
        in_specs=(
            P("seq", "tensor"),
            P("seq", "tensor"),
            P("seq", "tensor"),
            P("tensor", "seq"),
            P("tensor", "seq"),
            P("tensor", "seq"),
            P(("seq", "tensor"), None),
        ),
        out_specs=(
            P(("seq", "tensor"), None),
            P("seq", "tensor"),
            P("seq", "tensor"),
            P("seq", "tensor"),
        ),
        check_vma=False,
    )
```
